32 devices in a mesh: row: 4 (over y, x), col: 8 (over z, core).
Axes of the slice: x: 2, y: 2, z: 4, core: 2. Of those that a mesh axis runs over, the one named last changes fastest.
Arguments:
- normals: float32 [12288, 12288], P('row', 'col'), may hold values from -1 to 4, as said below
- design: float32 [128, 12288], P('row', 'col'), may hold values from -0.5 to 0.5
- filter_blocks: float32 [2, 32, 32], replicated, may hold values from -4 to 4, as said below
- regular: float32 [12288], replicated, may hold values from 0.1 to 1
Outputs:
- factored: float32 [12288, 12288], P('row', 'col')
The draws below stay inside these ranges and needn't reach their ends.
Inputs may be any that keep to these rules, and one draw needn't show every extreme that they name: normals is symmetric; each diagonal entry is at least 1 and each off-diagonal entry has magnitude at most 1 / 256. filter_blocks[0][i, j] = f[i - j] for i >= j and 0 above the diagonal; filter_blocks[1][i, j] = f[32 + i - j] for j >= i and 0 below; f holds the 33 taps of one causal filter with f[0] at least 1.
All inputs are finite; a program needn't handle non-finite values.
Results may differ from the reference program's by a relative error of at most 0.00007.
Values sent between devices are 32-bit elements; how exact they have to be, the bound alone decides.
No kernel may reach another device: no remote copies, remote signals or barrier semaphores. Data moves between devices by JAX's collectives and lax.ppermute only.
A program may use at most 128 MiB of HBM per device.

```python
import math
import jax
import jax.numpy as jnp
from jax import lax

M = 12288
B = 256
P_SIZE = 32
OBS = 128


def draw_normals(key, part):
    key_noise = jax.random.fold_in(key, 11)
    key_diag = jax.random.fold_in(key, 12)
    noise = jax.random.uniform(key_noise, (M, M), jnp.float32, -1.0, 1.0)
    symmetric = (noise + noise.T) * (0.5 / B)
    diagonal = jax.random.uniform(key_diag, (M,), jnp.float32, 1.0, 2.0)
    positions = jnp.arange(M, dtype=jnp.int32)
    return jnp.where(positions[:, None] == positions[None, :], diagonal[:, None], symmetric)


def draw_filter_blocks(key, part):
    key_lead = jax.random.fold_in(key, 21)
    key_taps = jax.random.fold_in(key, 22)
    leading = jax.random.uniform(key_lead, (1,), jnp.float32, 1.0, 1.5)
    scales = 0.5 / jnp.sqrt(jnp.arange(1, P_SIZE + 1, dtype=jnp.float32))
    later_taps = jax.random.truncated_normal(key_taps, -6.0, 6.0, (P_SIZE,), jnp.float32) * scales
    filter_taps = jnp.concatenate([leading, later_taps])
    row_pos = jnp.arange(P_SIZE, dtype=jnp.int32)[:, None]
    col_pos = jnp.arange(P_SIZE, dtype=jnp.int32)[None, :]
    lag_own = row_pos - col_pos
    lag_prior = P_SIZE + row_pos - col_pos
    own_block = jnp.where(lag_own >= 0, filter_taps[jnp.clip(lag_own, 0, P_SIZE)], 0.0)
    prior_block = jnp.where(col_pos >= row_pos, filter_taps[jnp.clip(lag_prior, 0, P_SIZE)], 0.0)
    return jnp.stack([own_block, prior_block]).astype(jnp.float32)


def steps_of(own_key, extent, shards, low, top_value):
    def one(dim, parts):
        steps = jax.random.uniform(jax.random.fold_in(jax.random.fold_in(own_key, 6), dim), (parts,), jnp.float32, low / len(shards), top_value / len(shards))
        return jnp.repeat(jnp.exp(steps), extent[dim] // parts).reshape((-1,) + (1,) * (len(extent) - dim - 1))

    factor_of = one(*shards[0])
    for cut in shards[1:]:
        factor_of = factor_of * one(*cut)
    return factor_of


def scatter_about(key, shape, scale, most, split=(), kind=jnp.bfloat16):
    drawn = scale * jax.random.normal(key, shape, jnp.float32)
    if split:
        drawn = drawn * steps_of(key, shape, split, -0.22, 0.18)
    return jnp.clip(drawn, -most, most).astype(kind)


def setup_inputs(seed: int = 0) -> dict:
    arg_keys = jax.random.split(jax.random.key(seed), 5)
    return {
        "normals": draw_normals(jax.random.fold_in(arg_keys[4], 71), 0),
        "design": scatter_about(arg_keys[1], (OBS, M), OBS ** -0.5, 0.5, ((0, 4), (1, 8)), jnp.float32),
        "filter_blocks": draw_filter_blocks(jax.random.fold_in(arg_keys[4], 71), 0),
        "regular": jnp.clip(jnp.exp(jax.random.uniform(arg_keys[3], (M,), jnp.float32, math.log(0.1), math.log(1.0))), 0.1, 1.0),
    }


def reference(normals, design, filter_blocks, regular):
    highest = lax.Precision.HIGHEST
    own_block = filter_blocks[0]
    prior_block = filter_blocks[1]
    blocks = design.reshape(OBS // P_SIZE, P_SIZE, M)
    before = jnp.concatenate([jnp.zeros((1, P_SIZE, M), jnp.float32), blocks[:-1]], axis=0)
    filtered = jnp.einsum('ij,bjc->bic', own_block, blocks, precision=highest)
    filtered = filtered + jnp.einsum('ij,bjc->bic', prior_block, before, precision=highest)
    filtered = filtered.reshape(OBS, M)
    gram_full = jnp.dot(filtered.T.astype(jnp.float32), filtered.astype(jnp.float32), precision=highest, preferred_element_type=jnp.float32)
    positions = jnp.arange(M, dtype=jnp.int32)
    system = (normals + gram_full).at[positions, positions].add(regular)
    corner = system[:B, :B]
    factor = jnp.linalg.cholesky(corner)
    inverse = jax.scipy.linalg.solve_triangular(factor, jnp.eye(B, dtype=jnp.float32), lower=True)
    panel_rows = jnp.dot(system[:, :B].astype(jnp.float32), inverse.T.astype(jnp.float32), precision=highest, preferred_element_type=jnp.float32)
    trailing = system[:, B:] - jnp.dot(panel_rows.astype(jnp.float32), panel_rows[B:].T.astype(jnp.float32), precision=highest, preferred_element_type=jnp.float32)
    return jnp.concatenate([panel_rows, trailing], axis=1)
```

```python
import functools

import jax
import jax.numpy as jnp
from jax import lax
from jax.experimental import pallas as pl
from jax.experimental.pallas import tpu as pltpu
from jax.sharding import PartitionSpec as P

B = 256
P_SIZE = 32
STRIP = 32
CHUNKS = 4
HIGHEST = lax.Precision.HIGHEST


def exact_dot(left, right, left_dim, right_dim):
    return lax.dot_general(
        left,
        right,
        (((left_dim,), (right_dim,)), ((), ())),
        precision=HIGHEST,
        preferred_element_type=jnp.float32,
    )


def split(value):
    high = value.astype(jnp.bfloat16)
    low = (value - high.astype(jnp.float32)).astype(jnp.bfloat16)
    return high, low


def split_dot(left, right):
    left_high, left_low = split(left)
    right_high, right_low = split(right)
    wide = functools.partial(jnp.dot, preferred_element_type=jnp.float32)
    return wide(left_high, right_high) + (wide(left_high, right_low) + wide(left_low, right_high))


def corner_kernel(corner_ref, design_ref, filter_ref, regular_ref, inverse_ref, lead_ref, upper):
    first = exact_dot(filter_ref[...], design_ref[...], 1, 0)
    row_pos = lax.broadcasted_iota(jnp.int32, (B, B), 0)
    col_pos = lax.broadcasted_iota(jnp.int32, (B, B), 1)
    system = corner_ref[...] + exact_dot(first, first, 0, 0)
    system = system + jnp.where(row_pos == col_pos, regular_ref[...], 0.0)
    identity = jnp.where(row_pos == col_pos, 1.0, 0.0)
    sub = lax.broadcasted_iota(jnp.int32, (STRIP, 1), 0)
    half = B // 2
    for start in range(0, B, STRIP):
        rows = slice(start, start + STRIP)
        strip = jnp.concatenate([system[rows, :], identity[rows, :]], axis=1)
        if start:
            done = upper[:start, :]
            strip = strip - exact_dot(done[:, rows], done, 0, 0)
        low = 0 if start < half else half
        wide = 3 * half
        held = strip[:, low : low + wide]
        for j in range(STRIP):
            at = start + j - low
            pivot = held[j : j + 1, at : at + 1]
            coef = jnp.where(sub > j, held[:, at : at + 1] / pivot, 0.0)
            held = held - coef * held[j : j + 1, :]
        lane = lax.broadcasted_iota(jnp.int32, (STRIP, wide), 1)
        on_diag = lane == sub + (start - low)
        diag = jnp.sum(jnp.where(on_diag, held, 0.0), axis=1, keepdims=True)
        held = held / jnp.sqrt(diag)
        zero = jnp.zeros((STRIP, half), jnp.float32)
        parts = [held, zero] if low == 0 else [zero, held]
        upper[rows, :] = jnp.concatenate(parts, axis=1)
    inverse = upper[:, B:]
    inverse_ref[...] = inverse
    lead_ref[...] = exact_dot(first, inverse, 1, 1)


def corner_factor(corner, design, filter_matrix, regular):
    obs = design.shape[0]
    return pl.pallas_call(
        corner_kernel,
        out_shape=[
            jax.ShapeDtypeStruct((B, B), jnp.float32),
            jax.ShapeDtypeStruct((obs, B), jnp.float32),
        ],
        scratch_shapes=[pltpu.VMEM((B, 2 * B), jnp.float32)],
        compiler_params=pltpu.CompilerParams(vmem_limit_bytes=24 * 2**20),
        cost_estimate=pl.CostEstimate(flops=4 * 10**9, bytes_accessed=2**20, transcendentals=0),
        name="corner_factor",
    )(corner, design, filter_matrix, regular)


def tile_kernel(count, place_ref, *refs):
    normals_ref, mine_ref, theirs_ref = refs[:3]
    row_parts = refs[3 : 3 + count]
    col_parts = refs[3 + count : 3 + 2 * count]
    strip_refs = refs[3 + 2 * count : 5 + 2 * count]
    filter_ref, inverse_ref, lead_ref, regular_ref, lead_reg_ref = refs[5 + 2 * count : 10 + 2 * count]
    out_ref, right_side = refs[10 + 2 * count :]
    step = pl.program_id(0)
    per_half = pl.num_programs(0) // 2
    row_index, col_index = place_ref[0], place_ref[1]
    block, cols = out_ref.shape
    obs = filter_ref.shape[0]
    rows_here = block * pl.num_programs(0)
    inverse = inverse_ref[...]
    lead = lead_ref[...]

    @pl.when(step == 0)
    def _():
        design = jnp.concatenate([part[...] for part in col_parts], axis=0)
        filtered = split_dot(filter_ref[...], design)
        strip = jnp.concatenate([part[...] for part in strip_refs], axis=0)
        row_pos = lax.broadcasted_iota(jnp.int32, (B, cols), 0)
        col_pos = lax.broadcasted_iota(jnp.int32, (B, cols), 1) + col_index * cols
        strip = strip + jnp.where(row_pos == col_pos, regular_ref[...], 0.0)
        panel = split_dot(inverse, strip) + split_dot(lead.T, filtered)
        filtered_high, filtered_low = split(filtered)
        panel_high, panel_low = split(-panel)
        right_side[:obs, :] = filtered_high
        right_side[obs : 2 * obs, :] = filtered_low
        right_side[2 * obs : 2 * obs + B, :] = panel_high
        right_side[2 * obs + B : 2 * obs + 2 * B, :] = panel_low
        right_side[2 * obs + 2 * B : 2 * obs + 3 * B, :] = panel_high
        right_side[2 * obs + 3 * B :, :] = filtered_high

    own_core = lax.rem(col_index, 2)
    half_index = jnp.where(step < per_half, own_core, 1 - own_core)
    row_block = half_index * per_half + lax.rem(step, per_half)
    first_row = row_index * rows_here + row_block * block
    first_col = col_index * cols
    design = jnp.concatenate([part[...] for part in row_parts], axis=0)
    filtered = split_dot(filter_ref[...], design).T
    system = jnp.where(step < per_half, mine_ref[...], theirs_ref[...])
    row_pos = lax.broadcasted_iota(jnp.int32, (block, B), 0) + first_row
    col_pos = lax.broadcasted_iota(jnp.int32, (block, B), 1)
    system = system + jnp.where(row_pos == col_pos, lead_reg_ref[...], 0.0)
    panel = split_dot(system, inverse.T) + split_dot(filtered, lead)
    filtered_high, filtered_low = split(filtered)
    panel_high, panel_low = split(panel)
    left_side = jnp.concatenate(
        [filtered_high, filtered_high, panel_high, panel_high, panel_low, filtered_low], axis=1
    )
    out_ref[...] = normals_ref[...] + jnp.dot(
        left_side, right_side[...], preferred_element_type=jnp.float32
    )

    @pl.when((first_row < first_col + cols) & (first_col < first_row + block))
    def _():
        row_pos = lax.broadcasted_iota(jnp.int32, (block, cols), 0) + first_row
        col_pos = lax.broadcasted_iota(jnp.int32, (block, cols), 1) + first_col
        out_ref[...] = out_ref[...] + jnp.where(row_pos == col_pos, regular_ref[...], 0.0)

    @pl.when(col_index == 0)
    def _():
        out_ref[:, :B] = panel


def tile_update(place, normals, mine, theirs, row_parts, col_parts, strips, filter_matrix, inverse, lead, regular, lead_reg):
    rows, cols = normals.shape
    block = 256 if cols % 256 == 0 else 128
    per_half = rows // 2 // block
    count = len(row_parts)
    obs_here = row_parts[0].shape[0]
    obs = filter_matrix.shape[0]

    def row_block(i, place):
        own_core = lax.rem(place[1], 2)
        half_index = jnp.where(i < per_half, own_core, 1 - own_core)
        return half_index * per_half + lax.rem(i, per_half)

    def whole(array):
        return pl.BlockSpec(array.shape, lambda i, place: (0,) * array.ndim)

    tile_spec = pl.BlockSpec((block, cols), lambda i, place: (row_block(i, place), 0))
    in_specs = [
        tile_spec,
        pl.BlockSpec((block, B), lambda i, place: (jnp.minimum(i, per_half - 1), 0)),
        pl.BlockSpec((block, B), lambda i, place: (jnp.maximum(i - per_half, 0), 0)),
    ]
    in_specs += [pl.BlockSpec((obs_here, block), lambda i, place: (0, row_block(i, place)))] * count
    rest = [*col_parts, *strips, filter_matrix, inverse, lead, regular, lead_reg]
    in_specs += [whole(array) for array in rest]
    return pl.pallas_call(
        functools.partial(tile_kernel, count),
        grid_spec=pltpu.PrefetchScalarGridSpec(
            num_scalar_prefetch=1,
            grid=(2 * per_half,),
            in_specs=in_specs,
            out_specs=tile_spec,
            scratch_shapes=[pltpu.VMEM((3 * (obs + B), cols), jnp.bfloat16)],
        ),
        out_shape=jax.ShapeDtypeStruct((rows, cols), jnp.float32),
        compiler_params=pltpu.CompilerParams(vmem_limit_bytes=48 * 2**20),
        cost_estimate=pl.CostEstimate(
            flops=6 * rows * cols * (obs + B), bytes_accessed=8 * rows * cols, transcendentals=0
        ),
        name="tile_update",
    )(place, normals, mine, theirs, *row_parts, *rest)


def shifted(value, axis, by):
    peers = lax.axis_size(axis)
    return lax.ppermute(value, axis, [(i, (i + by) % peers) for i in range(peers)])


def spread(value, axis, bits):
    peers = lax.axis_size(axis)
    me = lax.axis_index(axis)
    reached = [0]
    for bit in bits:
        pairs = [(i, i | bit) for i in reached if i | bit < peers]
        got = lax.ppermute(value, axis, pairs)
        value = jnp.where((me & bit) != 0, got, value)
        reached += [to for _, to in pairs]
    return value


def filter_matrix_of(filter_blocks, sources):
    count = sources.shape[0]
    lag = jnp.arange(count, dtype=jnp.int32)[:, None] - sources[None, :]
    lag = lag[:, None, :, None]
    own = filter_blocks[0][None, :, None, :]
    prior = filter_blocks[1][None, :, None, :]
    blocks = jnp.where(lag == 0, own, jnp.where(lag == 1, prior, 0.0))
    return blocks.reshape(count * P_SIZE, count * P_SIZE)


def row_strip_halves(normals):
    rows = normals.shape[0]
    half = rows // 2
    peers = lax.axis_size("col")
    col_index = lax.axis_index("col")
    chips = peers // 2
    chip = col_index // 2
    own = normals[:, :B]
    second = lax.ppermute(own[half:], "col", [(0, 1)])
    source = jnp.where(col_index == 0, own[:half], second)
    size = half // CHUNKS
    along = [(c, c + 2) for c in range(peers - 2)]
    received = []
    for step in range(CHUNKS + chips - 2):
        send = received[-1] if received else source[:size]
        if 0 < step < CHUNKS:
            send = jnp.where(chip == 0, source[step * size : (step + 1) * size], send)
        received.append(lax.ppermute(send, "col", along))
    arrived = lax.dynamic_slice_in_dim(
        jnp.concatenate(received, axis=0), jnp.maximum(chip - 1, 0) * size, half, axis=0
    )
    mine = jnp.where(chip == 0, source, arrived)
    theirs = lax.ppermute(mine, "col", [(c, c ^ 1) for c in range(peers)])
    return mine, theirs


def body(normals, design, filter_blocks, regular):
    rows_here, cols_here = normals.shape
    obs_here = design.shape[0]
    row_peers = lax.axis_size("row")
    row_index = lax.axis_index("row")
    col_index = lax.axis_index("col")
    blocks_here = obs_here // P_SIZE

    at_first = col_index == 0
    time_block = jnp.arange(row_peers, dtype=jnp.int32)[:, None, None]
    lead_design = jnp.where((time_block == row_index) & at_first, design[None, :, :B], 0.0)
    lead_corner = jnp.where(at_first & (row_index == 0), normals[:B, :B], 0.0)
    lead = jnp.concatenate([lead_design.reshape(row_peers * obs_here, B), lead_corner], axis=0)
    lead = lax.psum(lead, ("row", "col"))
    obs = row_peers * obs_here

    col_parts = [design] + [shifted(design, "row", s) for s in range(1, row_peers)]
    time_rows = lax.all_gather(design, "col", axis=1, tiled=True)
    row_parts = []
    for s in range(row_peers):
        to = (row_index + s) % row_peers
        part = lax.dynamic_slice_in_dim(time_rows, to * rows_here, rows_here, axis=1)
        row_parts.append(shifted(part, "row", s) if s else part)

    bits = [1 << i for i in range((row_peers - 1).bit_length())]
    strips = [
        spread(normals[: B // 2], "row", bits),
        spread(normals[B // 2 : B], "row", bits[::-1]),
    ]
    mine, theirs = row_strip_halves(normals)

    positions = jnp.arange(obs // P_SIZE, dtype=jnp.int32)
    plain = filter_matrix_of(filter_blocks, positions)
    passed = positions // blocks_here
    order = ((row_index - passed) % row_peers) * blocks_here + positions % blocks_here
    arranged = filter_matrix_of(filter_blocks, order)
    lead_reg = regular[:B].reshape(1, B)
    inverse, lead_filtered = corner_factor(lead[obs:], lead[:obs], plain, lead_reg)
    own_reg = lax.dynamic_slice_in_dim(regular, col_index * cols_here, cols_here).reshape(1, cols_here)
    place = jnp.stack([row_index, col_index]).astype(jnp.int32)
    return tile_update(
        place, normals, mine, theirs, row_parts, col_parts, strips, arranged, inverse, lead_filtered, own_reg, lead_reg
    )


def solution(mesh):
    in_specs = (P("row", "col"), P("row", "col"), P(), P())
    out_specs = P("row", "col")
    return jax.shard_map(body, mesh=mesh, in_specs=in_specs, out_specs=out_specs, check_vma=False)
```

```python
import functools

import jax
import jax.numpy as jnp
from jax import lax
from jax.experimental import pallas as pl
from jax.experimental.pallas import tpu as pltpu
from jax.sharding import PartitionSpec as P

B = 256
P_SIZE = 32
STRIP = 32
HIGHEST = lax.Precision.HIGHEST


def exact_dot(left, right, left_dim, right_dim):
    return lax.dot_general(
        left,
        right,
        (((left_dim,), (right_dim,)), ((), ())),
        precision=HIGHEST,
        preferred_element_type=jnp.float32,
    )


def split(value):
    high = value.astype(jnp.bfloat16)
    low = (value - high.astype(jnp.float32)).astype(jnp.bfloat16)
    return high, low


def split_dot(left, right):
    left_high, left_low = split(left)
    right_high, right_low = split(right)
    wide = functools.partial(jnp.dot, preferred_element_type=jnp.float32)
    return wide(left_high, right_high) + (wide(left_high, right_low) + wide(left_low, right_high))


def corner_kernel(joined_ref, filter_ref, regular_ref, inverse_ref, lead_ref, upper):
    obs = filter_ref.shape[0]
    first = exact_dot(filter_ref[...], joined_ref[:obs, :], 1, 0)
    row_pos = lax.broadcasted_iota(jnp.int32, (B, B), 0)
    col_pos = lax.broadcasted_iota(jnp.int32, (B, B), 1)
    system = joined_ref[obs:, :] + exact_dot(first, first, 0, 0)
    system = system + jnp.where(row_pos == col_pos, regular_ref[...], 0.0)
    identity = jnp.where(row_pos == col_pos, 1.0, 0.0)
    sub = lax.broadcasted_iota(jnp.int32, (STRIP, 1), 0)
    half = B // 2
    for start in range(0, B, STRIP):
        rows = slice(start, start + STRIP)
        strip = jnp.concatenate([system[rows, :], identity[rows, :]], axis=1)
        if start:
            done = upper[:start, :]
            strip = strip - exact_dot(done[:, rows], done, 0, 0)
        low = 0 if start < half else half
        wide = 3 * half
        held = strip[:, low : low + wide]
        for j in range(STRIP):
            at = start + j - low
            pivot = held[j : j + 1, at : at + 1]
            coef = jnp.where(sub > j, held[:, at : at + 1] / pivot, 0.0)
            held = held - coef * held[j : j + 1, :]
        lane = lax.broadcasted_iota(jnp.int32, (STRIP, wide), 1)
        on_diag = lane == sub + (start - low)
        diag = jnp.sum(jnp.where(on_diag, held, 0.0), axis=1, keepdims=True)
        held = held / jnp.sqrt(diag)
        zero = jnp.zeros((STRIP, half), jnp.float32)
        parts = [held, zero] if low == 0 else [zero, held]
        upper[rows, :] = jnp.concatenate(parts, axis=1)
    inverse = upper[:, B:]
    inverse_ref[...] = inverse.T
    lead_ref[...] = exact_dot(first, inverse, 1, 1)


def corner_factor(joined, filter_matrix, regular):
    obs = filter_matrix.shape[0]
    return pl.pallas_call(
        corner_kernel,
        out_shape=[
            jax.ShapeDtypeStruct((B, B), jnp.float32),
            jax.ShapeDtypeStruct((obs, B), jnp.float32),
        ],
        scratch_shapes=[pltpu.VMEM((B, 2 * B), jnp.float32)],
        compiler_params=pltpu.CompilerParams(vmem_limit_bytes=24 * 2**20),
        cost_estimate=pl.CostEstimate(flops=4 * 10**9, bytes_accessed=2**20, transcendentals=0),
        name="corner_factor",
    )(joined, filter_matrix, regular)


def right_kernel(count, place_ref, *refs):
    col_parts = refs[:count]
    high_ref, low_ref, filter_ref, inverse_ref, lead_ref, regular_ref, out_ref = refs[count:]
    cols = out_ref.shape[1]
    obs = filter_ref.shape[0]
    design = jnp.concatenate([part[...] for part in col_parts], axis=0)
    filtered = split_dot(filter_ref[...], design)
    strip = jnp.concatenate([high_ref[...], low_ref[...]], axis=0)
    row_pos = lax.broadcasted_iota(jnp.int32, (B, cols), 0)
    col_pos = lax.broadcasted_iota(jnp.int32, (B, cols), 1) + place_ref[1] * cols
    strip = strip + jnp.where(row_pos == col_pos, regular_ref[...], 0.0)
    panel = split_dot(inverse_ref[...].T, strip) + split_dot(lead_ref[...].T, filtered)
    filtered_high, filtered_low = split(filtered)
    panel_high, panel_low = split(-panel)
    out_ref[:obs, :] = filtered_high
    out_ref[obs : 2 * obs, :] = filtered_low
    out_ref[2 * obs : 2 * obs + B, :] = panel_high
    out_ref[2 * obs + B : 2 * obs + 2 * B, :] = panel_low
    out_ref[2 * obs + 2 * B : 2 * obs + 3 * B, :] = panel_high
    out_ref[2 * obs + 3 * B :, :] = filtered_high


def right_side(place, col_parts, strips, filter_matrix, inverse, lead, regular):
    count = len(col_parts)
    cols = strips[0].shape[1]
    depth = 3 * (filter_matrix.shape[0] + B)
    specs = [pl.BlockSpec(memory_space=pltpu.SMEM)]
    specs += [pl.BlockSpec(memory_space=pltpu.VMEM)] * (count + 6)
    return pl.pallas_call(
        functools.partial(right_kernel, count),
        in_specs=specs,
        out_specs=pl.BlockSpec(memory_space=pltpu.VMEM),
        out_shape=jax.ShapeDtypeStruct((depth, cols), jnp.bfloat16),
        compiler_params=pltpu.CompilerParams(vmem_limit_bytes=32 * 2**20),
        cost_estimate=pl.CostEstimate(
            flops=3 * 2 * cols * B * depth // 3, bytes_accessed=4 * cols * depth, transcendentals=0
        ),
        name="right_side",
    )(place, *col_parts, *strips, filter_matrix, inverse, lead, regular)


def tile_kernel(of_own, place_ref, *refs):
    if not of_own:
        refs = refs[1:]
    normals_ref, strip_ref, design_ref, right_ref = refs[:4]
    filter_ref, inverse_ref, lead_ref, regular_ref, lead_reg_ref, out_ref, left_ref = refs[4:]
    step = pl.program_id(0)
    steps = pl.num_programs(0)
    row_index, col_index = place_ref[0], place_ref[1]
    block, cols = out_ref.shape
    half = steps * block
    obs = filter_ref.shape[0]
    own_core = lax.rem(col_index, 2)
    half_index = own_core if of_own else 1 - own_core
    half_row = (2 * row_index + half_index) * half
    first_row = half_row + step * block
    first_col = col_index * cols

    @pl.when(step == 0)
    def _():
        filtered = split_dot(filter_ref[...], design_ref[...]).T
        row_pos = lax.broadcasted_iota(jnp.int32, (half, B), 0) + half_row
        col_pos = lax.broadcasted_iota(jnp.int32, (half, B), 1)
        system = strip_ref[...] + jnp.where(row_pos == col_pos, lead_reg_ref[...], 0.0)
        panel = split_dot(system, inverse_ref[...]) + split_dot(filtered, lead_ref[...])
        filtered_high, filtered_low = split(filtered)
        panel_high, panel_low = split(panel)
        left_ref[:, :obs] = filtered_high
        left_ref[:, obs : 2 * obs] = filtered_high
        left_ref[:, 2 * obs : 2 * obs + B] = panel_high
        left_ref[:, 2 * obs + B : 2 * obs + 2 * B] = panel_high
        left_ref[:, 2 * obs + 2 * B : 2 * obs + 3 * B] = panel_low
        left_ref[:, 2 * obs + 3 * B :] = filtered_low

    rows = pl.ds(pl.multiple_of(step * block, block), block)
    out_ref[...] = normals_ref[...] + jnp.dot(
        left_ref[rows, :], right_ref[...], preferred_element_type=jnp.float32
    )

    @pl.when((first_row < first_col + cols) & (first_col < first_row + block))
    def _():
        row_pos = lax.broadcasted_iota(jnp.int32, (block, cols), 0) + first_row
        col_pos = lax.broadcasted_iota(jnp.int32, (block, cols), 1) + first_col
        out_ref[...] = out_ref[...] + jnp.where(row_pos == col_pos, regular_ref[...], 0.0)

    @pl.when(col_index == 0)
    def _():
        panel_high = left_ref[rows, 2 * obs : 2 * obs + B].astype(jnp.float32)
        panel_low = left_ref[rows, 2 * obs + 2 * B : 2 * obs + 3 * B].astype(jnp.float32)
        out_ref[:, :B] = panel_high + panel_low


def block_rows(half):
    return max(size for size in range(128, 513, 128) if half % size == 0)


def tile_half(place, before, normals, strip, design, right, filter_matrix, inverse, lead, regular, lead_reg):
    rows, cols = normals.shape
    half = rows // 2
    block = block_rows(half)
    steps = half // block
    depth = right.shape[0]
    of_own = before is None

    def tile_block(i, place):
        own_core = lax.rem(place[1], 2)
        half_index = own_core if of_own else 1 - own_core
        return half_index * steps + i, 0

    def whole(array):
        return pl.BlockSpec(array.shape, lambda i, place: (0,) * array.ndim)

    tile_spec = pl.BlockSpec((block, cols), tile_block)
    rest = [strip, design, right, filter_matrix, inverse, lead, regular, lead_reg]
    in_specs = [tile_spec] + [whole(array) for array in rest]
    operands = [normals, *rest]
    if not of_own:
        in_specs = [pl.BlockSpec(memory_space=pl.ANY)] + in_specs
        operands = [before] + operands
    return pl.pallas_call(
        functools.partial(tile_kernel, of_own),
        grid_spec=pltpu.PrefetchScalarGridSpec(
            num_scalar_prefetch=1,
            grid=(steps,),
            in_specs=in_specs,
            out_specs=tile_spec,
            scratch_shapes=[pltpu.VMEM((half, depth), jnp.bfloat16)],
        ),
        out_shape=jax.ShapeDtypeStruct((rows, cols), jnp.float32),
        input_output_aliases={} if of_own else {1: 0},
        compiler_params=pltpu.CompilerParams(vmem_limit_bytes=44 * 2**20),
        cost_estimate=pl.CostEstimate(
            flops=2 * half * cols * depth, bytes_accessed=8 * half * cols, transcendentals=0
        ),
        name="tile_own" if of_own else "tile_other",
    )(place, *operands)


def shifted(value, axis, by):
    peers = lax.axis_size(axis)
    return lax.ppermute(value, axis, [(i, (i + by) % peers) for i in range(peers)])


def spread(value, axis, bits):
    peers = lax.axis_size(axis)
    me = lax.axis_index(axis)
    reached = [0]
    for bit in bits:
        pairs = [(i, i | bit) for i in reached if i | bit < peers]
        got = lax.ppermute(value, axis, pairs)
        value = jnp.where((me & bit) != 0, got, value)
        reached += [to for _, to in pairs]
    return value


def filter_matrix_of(filter_blocks, sources):
    count = sources.shape[0]
    lag = jnp.arange(count, dtype=jnp.int32)[:, None] - sources[None, :]
    lag = lag[:, None, :, None]
    own = filter_blocks[0][None, :, None, :]
    prior = filter_blocks[1][None, :, None, :]
    blocks = jnp.where(lag == 0, own, jnp.where(lag == 1, prior, 0.0))
    return blocks.reshape(count * P_SIZE, count * P_SIZE)


def row_strip_piece(normals):
    peers = lax.axis_size("col")
    chips = peers // 2
    half = normals.shape[0] // 2
    size = half // chips
    arrived = None
    for c in reversed(range(1, peers)):
        first = (c % 2) * half + (c // 2) * size
        got = lax.ppermute(normals[first : first + size, :B], "col", [(0, c)])
        arrived = got if arrived is None else arrived + got
    return jnp.where(lax.axis_index("col") == 0, normals[:size, :B], arrived)


def other_core(value):
    return lax.ppermute(value, "col", [(c, c ^ 1) for c in range(lax.axis_size("col"))])


def leading_parts(normals, design):
    row_peers, col_peers = lax.axis_size("row"), lax.axis_size("col")
    row_index, col_index = lax.axis_index("row"), lax.axis_index("col")
    obs_here = design.shape[0]
    held = jnp.concatenate([design[:, :B], normals[:B, :B]], axis=0)
    reached = [0]
    for bit in reversed([1 << i for i in range(1, (col_peers - 1).bit_length())]):
        pairs = [(i, i | bit) for i in reached if i | bit < col_peers]
        got = lax.ppermute(held, "col", pairs)
        held = jnp.where((col_index & bit) != 0, got, held)
        reached += [to for _, to in pairs]
    times, block = [held[:obs_here]], held[obs_here:]
    for s in range(1, row_peers):
        pairs = [
            (i * col_peers + c, (i + s) % row_peers * col_peers + c)
            for i in range(row_peers)
            for c in range(0, col_peers, 2)
        ]
        got = lax.ppermute(held, ("row", "col"), pairs)
        times.append(got[:obs_here])
        block = jnp.where(row_index == s, got[obs_here:], block)
    held = jnp.concatenate([*times, block], axis=0)
    got = lax.ppermute(held, "col", [(c, c + 1) for c in range(0, col_peers, 2)])
    return jnp.where(col_index % 2 == 1, got, held)


def body(normals, design, filter_blocks, regular):
    rows_here, cols_here = normals.shape
    obs_here = design.shape[0]
    row_peers = lax.axis_size("row")
    row_index = lax.axis_index("row")
    col_peers = lax.axis_size("col")
    col_index = lax.axis_index("col")
    blocks_here = obs_here // P_SIZE
    obs = row_peers * obs_here
    cores = [list(range(k, col_peers, 2)) for k in range(2)]

    lead = leading_parts(normals, design)
    piece = row_strip_piece(normals)

    time_rows = lax.all_gather(design, "col", axis=1, tiled=True, axis_index_groups=cores)
    col_parts = [design] + [shifted(design, "row", s) for s in range(1, row_peers)]

    bits = [1 << i for i in range((row_peers - 1).bit_length())]
    strips = [
        spread(normals[: B // 2], "row", bits),
        spread(normals[B // 2 : B], "row", bits[::-1]),
    ]
    row_parts = []
    for s in range(row_peers):
        to = (row_index + s) % row_peers
        part = lax.dynamic_slice_in_dim(time_rows, to * cols_here, cols_here, axis=1)
        row_parts.append(shifted(part, "row", s) if s else part)
    own_design = jnp.concatenate(row_parts, axis=0)
    other_design = other_core(own_design)
    own_strip = lax.all_gather(piece, "col", axis=0, tiled=True, axis_index_groups=cores)
    other_strip = other_core(own_strip)

    positions = jnp.arange(obs // P_SIZE, dtype=jnp.int32)
    passed = positions // blocks_here
    order = ((row_index - passed) % row_peers) * blocks_here + positions % blocks_here
    filters = filter_matrix_of(filter_blocks, order)
    lead_reg = regular[:B].reshape(1, B)
    own_reg = lax.dynamic_slice_in_dim(regular, col_index * cols_here, cols_here).reshape(1, cols_here)
    place = jnp.stack([row_index, col_index]).astype(jnp.int32)
    inverse, lead_filtered = corner_factor(lead, filters, lead_reg)
    right = right_side(place, col_parts, strips, filters, inverse, lead_filtered, own_reg)
    shared = [right, filters, inverse, lead_filtered, own_reg, lead_reg]
    out = tile_half(place, None, normals, own_strip, own_design, *shared)
    return tile_half(place, out, normals, other_strip, other_design, *shared)


def solution(mesh):
    in_specs = (P("row", "col"), P("row", "col"), P(), P())
    out_specs = P("row", "col")
    return jax.shard_map(body, mesh=mesh, in_specs=in_specs, out_specs=out_specs, check_vma=False)
```

```python
import functools

import jax
import jax.numpy as jnp
from jax import lax
from jax.experimental import pallas as pl
from jax.experimental.pallas import tpu as pltpu
from jax.sharding import PartitionSpec as P

B = 256
P_SIZE = 32
STRIP = 32
PIVOTS = 4
HIGHEST = lax.Precision.HIGHEST


def exact_dot(left, right, left_dim, right_dim):
    return lax.dot_general(
        left,
        right,
        (((left_dim,), (right_dim,)), ((), ())),
        precision=HIGHEST,
        preferred_element_type=jnp.float32,
    )


def split(value):
    high = value.astype(jnp.bfloat16)
    low = (value - high.astype(jnp.float32)).astype(jnp.bfloat16)
    return high, low


def split_dot(left, right):
    left_high, left_low = split(left)
    right_high, right_low = split(right)
    wide = functools.partial(jnp.dot, preferred_element_type=jnp.float32)
    return wide(left_high, right_high) + (wide(left_high, right_low) + wide(left_low, right_high))


def corner_kernel(joined_ref, filter_ref, regular_ref, inverse_ref, lead_ref, upper):
    obs = filter_ref.shape[0]
    filtered = exact_dot(filter_ref[...], joined_ref[:obs, :], 1, 0)
    row_pos = lax.broadcasted_iota(jnp.int32, (B, B), 0)
    col_pos = lax.broadcasted_iota(jnp.int32, (B, B), 1)
    system = joined_ref[obs:, :] + exact_dot(filtered, filtered, 0, 0)
    system = system + jnp.where(row_pos == col_pos, regular_ref[...], 0.0)
    identity = jnp.where(row_pos == col_pos, 1.0, 0.0)
    half = B // 2
    sub = lax.broadcasted_iota(jnp.int32, (STRIP, half), 0)
    lane = lax.broadcasted_iota(jnp.int32, (STRIP, half), 1)
    zero = jnp.zeros((STRIP, half), jnp.float32)
    for start in range(0, B, STRIP):
        rows = slice(start, start + STRIP)
        strip = jnp.concatenate([system[rows, :], identity[rows, :]], axis=1)
        if start:
            done = upper[:start, :]
            strip = strip - exact_dot(done[:, rows], done, 0, 0)
        low = 0 if start < half else half
        held = [strip[:, at : at + half] for at in range(low, low + 3 * half, half)]
        for first in range(0, STRIP, PIVOTS):
            at = start + first - low
            columns = [
                jnp.broadcast_to(held[0][:, at + q : at + q + 1], (STRIP, half)) for q in range(PIVOTS)
            ]
            pivot_rows = [[part[first + q : first + q + 1, :] for part in held] for q in range(PIVOTS)]
            for q in range(PIVOTS):
                j = first + q
                coef = jnp.where(sub > j, columns[q] * (1.0 / columns[q][j : j + 1, :]), 0.0)
                for m in range(q + 1, PIVOTS):
                    columns[m] = columns[m] - coef * columns[m][j : j + 1, :]
                    scale = coef[first + m : first + m + 1, :]
                    pivot_rows[m] = [
                        row - scale * other for row, other in zip(pivot_rows[m], pivot_rows[q])
                    ]
                held = [part - coef * row for part, row in zip(held, pivot_rows[q])]
        diag = jnp.sum(jnp.where(lane == sub + (start - low), held[0], 0.0), axis=1, keepdims=True)
        held = [part / jnp.sqrt(diag) for part in held]
        upper[rows, :] = jnp.concatenate([*held, zero] if low == 0 else [zero, *held], axis=1)
    inverse = upper[:, B:]
    inverse_ref[...] = inverse.T
    lead_ref[...] = exact_dot(filtered, inverse, 1, 1)


def corner_factor(joined, filter_matrix, regular):
    obs = filter_matrix.shape[0]
    return pl.pallas_call(
        corner_kernel,
        out_shape=[
            jax.ShapeDtypeStruct((B, B), jnp.float32),
            jax.ShapeDtypeStruct((obs, B), jnp.float32),
        ],
        scratch_shapes=[pltpu.VMEM((B, 2 * B), jnp.float32)],
        compiler_params=pltpu.CompilerParams(vmem_limit_bytes=24 * 2**20),
        cost_estimate=pl.CostEstimate(flops=4 * 10**9, bytes_accessed=2**20, transcendentals=0),
        name="corner_factor",
    )(joined, filter_matrix, regular)


def right_kernel(count, place_ref, *refs):
    col_parts = refs[:count]
    high_ref, low_ref, filter_ref, inverse_ref, lead_ref, regular_ref, out_ref = refs[count:]
    cols = out_ref.shape[1]
    obs = filter_ref.shape[0]
    obs_here = obs // count
    design = jnp.concatenate([part[:obs_here, :] for part in col_parts], axis=0)
    filtered = split_dot(filter_ref[...], design)
    strip = jnp.concatenate([high_ref[...], low_ref[...]], axis=0)
    row_pos = lax.broadcasted_iota(jnp.int32, (B, cols), 0)
    col_pos = lax.broadcasted_iota(jnp.int32, (B, cols), 1) + place_ref[1] * cols
    strip = strip + jnp.where(row_pos == col_pos, regular_ref[...], 0.0)
    panel = split_dot(inverse_ref[...].T, strip) + split_dot(lead_ref[...].T, filtered)
    filtered_high, filtered_low = split(filtered)
    panel_high, panel_low = split(-panel)
    out_ref[:obs, :] = filtered_high
    out_ref[obs : 2 * obs, :] = filtered_low
    out_ref[2 * obs : 2 * obs + B, :] = panel_high
    out_ref[2 * obs + B : 2 * obs + 2 * B, :] = panel_low
    out_ref[2 * obs + 2 * B : 2 * obs + 3 * B, :] = panel_high
    out_ref[2 * obs + 3 * B :, :] = filtered_high

    @pl.when(place_ref[1] == 0)
    def _():
        out_ref[:, :B] = jnp.zeros((out_ref.shape[0], B), jnp.bfloat16)
        row_pos = lax.broadcasted_iota(jnp.int32, (B, B), 0)
        identity = jnp.where(row_pos == lax.broadcasted_iota(jnp.int32, (B, B), 1), 1.0, 0.0)
        identity = identity.astype(jnp.bfloat16)
        out_ref[2 * obs : 2 * obs + B, :B] = identity
        out_ref[2 * obs + 2 * B : 2 * obs + 3 * B, :B] = identity


def right_side(place, col_parts, strips, filter_matrix, inverse, lead, regular):
    count = len(col_parts)
    cols = strips[0].shape[1]
    depth = 3 * (filter_matrix.shape[0] + B)
    specs = [pl.BlockSpec(memory_space=pltpu.SMEM)]
    specs += [pl.BlockSpec(memory_space=pltpu.VMEM)] * (count + 6)
    return pl.pallas_call(
        functools.partial(right_kernel, count),
        in_specs=specs,
        out_specs=pl.BlockSpec(memory_space=pltpu.VMEM),
        out_shape=jax.ShapeDtypeStruct((depth, cols), jnp.bfloat16),
        compiler_params=pltpu.CompilerParams(vmem_limit_bytes=32 * 2**20),
        cost_estimate=pl.CostEstimate(
            flops=2 * cols * B * depth, bytes_accessed=4 * cols * depth, transcendentals=0
        ),
        name="right_side",
    )(place, *col_parts, *strips, filter_matrix, inverse, lead, regular)


def tile_kernel(units, again, place_ref, blocks_ref, *refs):
    if again:
        refs = refs[1:]
    count = len(units)
    normals_ref = refs[0]
    strip_refs = refs[1 : 1 + count]
    design_refs = refs[1 + count : 3 + count]
    right_ref, filter_ref, inverse_ref, lead_ref, regular_ref, lead_reg_ref = refs[3 + count : 9 + count]
    out_ref, left_ref = refs[9 + count :]
    step = pl.program_id(0)
    row_index, col_index = place_ref[0], place_ref[1]
    block, cols = out_ref.shape
    row_blocks = 2 * cols // block
    obs = filter_ref.shape[0]
    first_col = col_index * cols

    @pl.when(step == 0)
    def _():
        for unit, other in enumerate(units):
            in_half = lax.rem(blocks_ref[unit], row_blocks // 2)
            here = pl.ds(pl.multiple_of(in_half * block, block), block)
            filtered = split_dot(filter_ref[...], design_refs[other][:, here]).T
            first_row = (row_index * row_blocks + blocks_ref[unit]) * block
            row_pos = lax.broadcasted_iota(jnp.int32, (block, B), 0) + first_row
            col_pos = lax.broadcasted_iota(jnp.int32, (block, B), 1)
            system = strip_refs[unit][...] + jnp.where(row_pos == col_pos, lead_reg_ref[...], 0.0)
            panel = split_dot(system, inverse_ref[...]) + split_dot(filtered, lead_ref[...])
            filtered_high, filtered_low = split(filtered)
            panel_high, panel_low = split(panel)
            rows = slice(unit * block, (unit + 1) * block)
            left_ref[rows, :obs] = filtered_high
            left_ref[rows, obs : 2 * obs] = filtered_high
            left_ref[rows, 2 * obs : 2 * obs + B] = panel_high
            left_ref[rows, 2 * obs + B : 2 * obs + 2 * B] = panel_high
            left_ref[rows, 2 * obs + 2 * B : 2 * obs + 3 * B] = panel_low
            left_ref[rows, 2 * obs + 3 * B :] = filtered_low

    first_row = (row_index * row_blocks + blocks_ref[step]) * block
    rows = pl.ds(pl.multiple_of(step * block, block), block)
    col_pos = lax.broadcasted_iota(jnp.int32, (1, cols), 1) + first_col
    keep = jnp.where(col_pos < B, 0.0, 1.0)
    out_ref[...] = normals_ref[...] * keep + jnp.dot(
        left_ref[rows, :], right_ref[...], preferred_element_type=jnp.float32
    )

    @pl.when((first_row < first_col + cols) & (first_col < first_row + block))
    def _():
        row_pos = lax.broadcasted_iota(jnp.int32, (block, cols), 0) + first_row
        on_diag = (row_pos == col_pos) & (col_pos >= B)
        out_ref[...] = out_ref[...] + jnp.where(on_diag, regular_ref[...], 0.0)


def tile_rows(place, blocks, before, normals, units, strips, designs, right, filter_matrix, inverse, lead, regular, lead_reg):
    rows, cols = normals.shape
    block = strips[0].shape[0]
    depth = right.shape[0]
    again = before is not None

    def whole(array):
        return pl.BlockSpec(array.shape, lambda i, place, blocks: (0,) * array.ndim)

    tile_spec = pl.BlockSpec((block, cols), lambda i, place, blocks: (blocks[i], 0))
    rest = [*strips, *designs, right, filter_matrix, inverse, lead, regular, lead_reg]
    in_specs = [tile_spec] + [whole(array) for array in rest]
    operands = [normals, *rest]
    if again:
        in_specs = [pl.BlockSpec(memory_space=pl.ANY)] + in_specs
        operands = [before] + operands
    count = len(units)
    return pl.pallas_call(
        functools.partial(tile_kernel, units, again),
        grid_spec=pltpu.PrefetchScalarGridSpec(
            num_scalar_prefetch=2,
            grid=(count,),
            in_specs=in_specs,
            out_specs=tile_spec,
            scratch_shapes=[pltpu.VMEM((count * block, depth), jnp.bfloat16)],
        ),
        out_shape=jax.ShapeDtypeStruct((rows, cols), jnp.float32),
        input_output_aliases={2: 0} if again else {},
        compiler_params=pltpu.CompilerParams(vmem_limit_bytes=44 * 2**20),
        cost_estimate=pl.CostEstimate(
            flops=2 * count * block * cols * depth, bytes_accessed=8 * count * block * cols, transcendentals=0
        ),
        name="tile_rest" if again else "tile_first",
    )(place, blocks, *operands)


def shifted(value, axis, by):
    peers = lax.axis_size(axis)
    return lax.ppermute(value, axis, [(i, (i + by) % peers) for i in range(peers)])


def spread(value, axis, bits):
    peers = lax.axis_size(axis)
    me = lax.axis_index(axis)
    reached = [0]
    for bit in bits:
        pairs = [(i, i | bit) for i in reached if i | bit < peers]
        got = lax.ppermute(value, axis, pairs)
        value = jnp.where((me & bit) != 0, got, value)
        reached += [to for _, to in pairs]
    return value


def filter_matrix_of(filter_blocks, sources):
    count = sources.shape[0]
    lag = jnp.arange(count, dtype=jnp.int32)[:, None] - sources[None, :]
    lag = lag[:, None, :, None]
    own = filter_blocks[0][None, :, None, :]
    prior = filter_blocks[1][None, :, None, :]
    blocks = jnp.where(lag == 0, own, jnp.where(lag == 1, prior, 0.0))
    return blocks.reshape(count * P_SIZE, count * P_SIZE)


def other_core(value):
    return lax.ppermute(value, "col", [(c, c ^ 1) for c in range(lax.axis_size("col"))])


def row_strip(normals):
    peers = lax.axis_size("col")
    chips = peers // 2
    half = normals.shape[0] // 2
    col_index = lax.axis_index("col")
    chip = col_index // 2
    own = normals[:half, :B]
    second = lax.ppermute(normals[half:, :B], "col", [(0, 1)])
    if chips > 4:
        cores = [list(range(k, peers, 2)) for k in range(2)]
        size = half // chips
        arrived = own[:size]
        for c in range(1, peers):
            first = (c % 2) * half + (c // 2) * size
            got = lax.ppermute(normals[first : first + size, :B], "col", [(0, c)])
            arrived = jnp.where(col_index == c, got, arrived)
        return [(jnp.int32(0), lax.all_gather(arrived, "col", axis=0, tiled=True, axis_index_groups=cores))]
    count = chips - 1
    size = half // count
    arrived = None
    for c in reversed(range(2, peers)):
        first = (c % 2) * half + (c // 2 - 1) * size
        got = lax.ppermute(normals[first : first + size, :B], "col", [(0, c)])
        arrived = got if arrived is None else arrived + got
    local = jnp.where(col_index == 0, own, second)
    at_source = chip == 0
    mine = jnp.where(at_source, local[:size], arrived)
    pieces = [(jnp.where(at_source, 0, chip - 1), mine)]
    for s in range(1, count):
        pairs = [
            (2 * (1 + i) + k, 2 * (1 + (i + s) % count) + k) for i in range(count) for k in range(2)
        ]
        got = lax.ppermute(mine, "col", pairs)
        which = -s % count
        piece = jnp.where(at_source, local[which * size : (which + 1) * size], got)
        pieces.append((jnp.where(at_source, which, (chip - 1 - s) % count), piece))
    return pieces


def leading_parts(normals, design):
    row_peers, col_peers = lax.axis_size("row"), lax.axis_size("col")
    row_index, col_index = lax.axis_index("row"), lax.axis_index("col")
    obs_here = design.shape[0]
    held = jnp.concatenate([design[:, :B], normals[:B, :B]], axis=0)
    reached = [0]
    for bit in reversed([1 << i for i in range(1, (col_peers - 1).bit_length())]):
        pairs = [(i, i | bit) for i in reached if i | bit < col_peers]
        got = lax.ppermute(held, "col", pairs)
        held = jnp.where((col_index & bit) != 0, got, held)
        reached += [to for _, to in pairs]
    times, block = [held[:obs_here]], held[obs_here:]
    for s in range(1, row_peers):
        pairs = [
            (i * col_peers + c, (i + s) % row_peers * col_peers + c)
            for i in range(row_peers)
            for c in range(0, col_peers, 2)
        ]
        got = lax.ppermute(held, ("row", "col"), pairs)
        times.append(got[:obs_here])
        block = jnp.where(row_index == s, got[obs_here:], block)
    held = jnp.concatenate([*times, block], axis=0)
    got = lax.ppermute(held, "col", [(c, c + 1) for c in range(0, col_peers, 2)])
    return jnp.where(col_index % 2 == 1, got, held)


def body(normals, design, filter_blocks, regular):
    cols_here = normals.shape[1]
    obs_here = design.shape[0]
    row_peers = lax.axis_size("row")
    row_index = lax.axis_index("row")
    chips = lax.axis_size("col") // 2
    col_index = lax.axis_index("col")
    blocks_here = obs_here // P_SIZE
    obs = row_peers * obs_here

    lead = leading_parts(normals, design)
    pieces = row_strip(normals)

    along = [design] + [shifted(design, "col", 2 * s) for s in range(1, chips)]
    along = jnp.stack(along)
    parts = []
    for s in range(row_peers):
        back = (col_index // 2 - (row_index + s)) % chips
        far = lax.dynamic_index_in_dim(along, back, 0, keepdims=False)
        part = jnp.concatenate([design, far], axis=0)
        parts.append(shifted(part, "row", s) if s else part)
    own_design = jnp.concatenate([part[obs_here:] for part in parts], axis=0)
    designs = [own_design, other_core(own_design)]

    bits = [1 << i for i in range((row_peers - 1).bit_length())]
    strips = [
        spread(normals[: B // 2], "row", bits),
        spread(normals[B // 2 : B], "row", bits[::-1]),
    ]

    positions = jnp.arange(obs // P_SIZE, dtype=jnp.int32)
    passed = positions // blocks_here
    order = ((row_index - passed) % row_peers) * blocks_here + positions % blocks_here
    filters = filter_matrix_of(filter_blocks, order)
    lead_reg = regular[:B].reshape(1, B)
    own_reg = lax.dynamic_slice_in_dim(regular, col_index * cols_here, cols_here).reshape(1, cols_here)
    place = jnp.stack([row_index, col_index]).astype(jnp.int32)
    inverse, lead_filtered = corner_factor(lead, filters, lead_reg)
    right = right_side(place, parts, strips, filters, inverse, lead_filtered, own_reg)
    shared = [right, filters, inverse, lead_filtered, own_reg, lead_reg]

    core = col_index % 2
    out = None
    for group in (pieces[:1], pieces[1:]):
        if group:
            rows, blocks = [], []
            for other in range(2):
                for which, piece in group:
                    rows.append(other_core(piece) if other else piece)
                    blocks.append(((1 - core) if other else core) * len(pieces) + which)
            units = [0] * len(group) + [1] * len(group)
            blocks = jnp.stack(blocks).astype(jnp.int32)
            out = tile_rows(place, blocks, out, normals, units, rows, designs, *shared)
    return out


def solution(mesh):
    in_specs = (P("row", "col"), P("row", "col"), P(), P())
    out_specs = P("row", "col")
    return jax.shard_map(body, mesh=mesh, in_specs=in_specs, out_specs=out_specs, check_vma=False)
```

```python
import functools

import jax
import jax.numpy as jnp
from jax import lax
from jax.experimental import pallas as pl
from jax.experimental.pallas import tpu as pltpu
from jax.sharding import PartitionSpec as P

B = 256
P_SIZE = 32
STRIP = 32
PIVOTS = 4
HIGHEST = lax.Precision.HIGHEST


def exact_dot(left, right, left_dim, right_dim):
    return lax.dot_general(
        left,
        right,
        (((left_dim,), (right_dim,)), ((), ())),
        precision=HIGHEST,
        preferred_element_type=jnp.float32,
    )


def split(value):
    high = value.astype(jnp.bfloat16)
    low = (value - high.astype(jnp.float32)).astype(jnp.bfloat16)
    return high, low


def split_dot(left, right):
    left_high, left_low = split(left)
    right_high, right_low = split(right)
    wide = functools.partial(jnp.dot, preferred_element_type=jnp.float32)
    return wide(left_high, right_high) + (wide(left_high, right_low) + wide(left_low, right_high))


def corner_kernel(block_ref, design_ref, filter_ref, regular_ref, inverse_ref, upper):
    filtered = exact_dot(filter_ref[...], design_ref[...], 1, 0)
    row_pos = lax.broadcasted_iota(jnp.int32, (B, B), 0)
    col_pos = lax.broadcasted_iota(jnp.int32, (B, B), 1)
    system = block_ref[...] + exact_dot(filtered, filtered, 0, 0)
    system = system + jnp.where(row_pos == col_pos, regular_ref[...], 0.0)
    identity = jnp.where(row_pos == col_pos, 1.0, 0.0)
    half = B // 2
    sub = lax.broadcasted_iota(jnp.int32, (STRIP, half), 0)
    lane = lax.broadcasted_iota(jnp.int32, (STRIP, half), 1)
    zero = jnp.zeros((STRIP, half), jnp.float32)
    for start in range(0, B, STRIP):
        rows = slice(start, start + STRIP)
        strip = jnp.concatenate([system[rows, :], identity[rows, :]], axis=1)
        if start:
            done = upper[:start, :]
            strip = strip - exact_dot(done[:, rows], done, 0, 0)
        low = 0 if start < half else half
        held = [strip[:, at : at + half] for at in range(low, low + 3 * half, half)]
        for first in range(0, STRIP, PIVOTS):
            at = start + first - low
            columns = [
                jnp.broadcast_to(held[0][:, at + q : at + q + 1], (STRIP, half)) for q in range(PIVOTS)
            ]
            pivot_rows = [[part[first + q : first + q + 1, :] for part in held] for q in range(PIVOTS)]
            for q in range(PIVOTS):
                j = first + q
                coef = jnp.where(sub > j, columns[q] * (1.0 / columns[q][j : j + 1, :]), 0.0)
                for m in range(q + 1, PIVOTS):
                    columns[m] = columns[m] - coef * columns[m][j : j + 1, :]
                    scale = coef[first + m : first + m + 1, :]
                    pivot_rows[m] = [
                        row - scale * other for row, other in zip(pivot_rows[m], pivot_rows[q])
                    ]
                held = [part - coef * row for part, row in zip(held, pivot_rows[q])]
        diag = jnp.sum(jnp.where(lane == sub + (start - low), held[0], 0.0), axis=1, keepdims=True)
        held = [part / jnp.sqrt(diag) for part in held]
        upper[rows, :] = jnp.concatenate([*held, zero] if low == 0 else [zero, *held], axis=1)
    inverse_ref[...] = upper[:, B:].T


def corner_factor(block, design, filter_matrix, regular):
    return pl.pallas_call(
        corner_kernel,
        out_shape=jax.ShapeDtypeStruct((B, B), jnp.float32),
        scratch_shapes=[pltpu.VMEM((B, 2 * B), jnp.float32)],
        compiler_params=pltpu.CompilerParams(vmem_limit_bytes=4 * 2**20),
        cost_estimate=pl.CostEstimate(flops=10**9, bytes_accessed=2**20, transcendentals=0),
        name="corner_factor",
    )(block, design, filter_matrix, regular)


def right_kernel(place_ref, high_ref, low_ref, gram_ref, inverse_ref, out_ref):
    strip = jnp.concatenate([high_ref[...], low_ref[...]], axis=0) + gram_ref[...]
    panel_high, panel_low = split(-split_dot(inverse_ref[...].T, strip))
    out_ref[:B, :] = panel_high
    out_ref[B : 2 * B, :] = panel_low
    out_ref[2 * B :, :] = panel_high

    @pl.when(place_ref[1] == 0)
    def _():
        row_pos = lax.broadcasted_iota(jnp.int32, (B, B), 0)
        identity = jnp.where(row_pos == lax.broadcasted_iota(jnp.int32, (B, B), 1), 1.0, 0.0)
        identity = identity.astype(jnp.bfloat16)
        out_ref[:B, :B] = identity
        out_ref[B : 2 * B, :B] = jnp.zeros((B, B), jnp.bfloat16)
        out_ref[2 * B :, :B] = identity


def right_side(place, strips, gram_rows, inverse):
    cols = gram_rows.shape[1]
    return pl.pallas_call(
        right_kernel,
        in_specs=[pl.BlockSpec(memory_space=pltpu.SMEM)] + [pl.BlockSpec(memory_space=pltpu.VMEM)] * 4,
        out_specs=pl.BlockSpec(memory_space=pltpu.VMEM),
        out_shape=jax.ShapeDtypeStruct((3 * B, cols), jnp.bfloat16),
        compiler_params=pltpu.CompilerParams(vmem_limit_bytes=20 * 2**20),
        cost_estimate=pl.CostEstimate(
            flops=6 * cols * B * B, bytes_accessed=12 * cols * B, transcendentals=0
        ),
        name="right_side",
    )(place, *strips, gram_rows, inverse)


def filter_kernel(count, place_ref, *refs):
    parts = refs[:count]
    other_ref, filter_ref, regular_ref, lead_reg_ref = refs[count : count + 4]
    left_ref, right_ref, gram_rows_ref, gram_cols_ref = refs[count + 4 :]
    row_index, col_index = place_ref[0], place_ref[1]
    cols = right_ref.shape[1]
    obs = filter_ref.shape[0]
    core = lax.rem(col_index, 2)
    design = jnp.concatenate([part[...] for part in parts], axis=0)
    filtered = split_dot(filter_ref[...], design)
    here, rows_own, lead = filtered[:, :cols], filtered[:, cols : 2 * cols], filtered[:, 2 * cols :]
    row_pos = lax.broadcasted_iota(jnp.int32, (B, cols), 0)
    col_pos = lax.broadcasted_iota(jnp.int32, (1, cols), 1) + col_index * cols
    gram_rows_ref[...] = split_dot(lead.T, here) + jnp.where(row_pos == col_pos, regular_ref[...], 0.0)
    high, low = split(jnp.where(col_pos < B, 0.0, here))
    right_ref[:obs, :] = high
    right_ref[obs : 2 * obs, :] = low
    right_ref[2 * obs :, :] = high
    rows_other = split_dot(filter_ref[...], other_ref[...])
    for half, value in ((core, rows_own), (1 - core, rows_other)):
        value = value.T
        high, low = split(value)
        rows = pl.ds(pl.multiple_of(half * cols, cols), cols)
        left_ref[rows, :obs] = high
        left_ref[rows, obs : 2 * obs] = high
        left_ref[rows, 2 * obs :] = low
        row_pos = lax.broadcasted_iota(jnp.int32, (cols, B), 0) + (2 * row_index + half) * cols
        lead_pos = lax.broadcasted_iota(jnp.int32, (cols, B), 1)
        gram_cols_ref[rows, :] = split_dot(value, lead) + jnp.where(
            row_pos == lead_pos, lead_reg_ref[...], 0.0
        )


def filter_sides(place, parts, other, filter_matrix, regular, lead_reg):
    cols = other.shape[1]
    obs = filter_matrix.shape[0]
    vmem = pl.BlockSpec(memory_space=pltpu.VMEM)
    return pl.pallas_call(
        functools.partial(filter_kernel, len(parts)),
        in_specs=[pl.BlockSpec(memory_space=pltpu.SMEM)] + [vmem] * (len(parts) + 4),
        out_specs=[vmem] * 4,
        out_shape=[
            jax.ShapeDtypeStruct((2 * cols, 3 * obs), jnp.bfloat16),
            jax.ShapeDtypeStruct((3 * obs, cols), jnp.bfloat16),
            jax.ShapeDtypeStruct((B, cols), jnp.float32),
            jax.ShapeDtypeStruct((2 * cols, B), jnp.float32),
        ],
        compiler_params=pltpu.CompilerParams(vmem_limit_bytes=20 * 2**20),
        cost_estimate=pl.CostEstimate(
            flops=18 * cols * obs * B, bytes_accessed=24 * cols * B, transcendentals=0
        ),
        name="filter_sides",
    )(place, *parts, other, filter_matrix, regular, lead_reg)


def gram_kernel(place_ref, normals_ref, left_ref, right_ref, regular_ref, out_ref):
    step = pl.program_id(0)
    block, cols = out_ref.shape
    first_col = place_ref[1] * cols
    col_pos = lax.broadcasted_iota(jnp.int32, (1, cols), 1) + first_col
    keep = jnp.where(col_pos < B, 0.0, 1.0)
    out_ref[...] = normals_ref[...] * keep + jnp.dot(
        left_ref[...], right_ref[...], preferred_element_type=jnp.float32
    )
    first_row = (place_ref[0] * pl.num_programs(0) + step) * block

    @pl.when((first_row < first_col + cols) & (first_col < first_row + block))
    def _():
        row_pos = lax.broadcasted_iota(jnp.int32, (block, cols), 0) + first_row
        on_diag = (row_pos == col_pos) & (col_pos >= B)
        out_ref[...] = out_ref[...] + jnp.where(on_diag, regular_ref[...], 0.0)


def block_rows(half):
    return max(size for size in range(128, 513, 128) if half % size == 0)


def gram_tile(place, normals, left, right, regular):
    rows, cols = normals.shape
    block = block_rows(rows // 2)
    depth = right.shape[0]
    tile_spec = pl.BlockSpec((block, cols), lambda i, place: (i, 0))
    return pl.pallas_call(
        gram_kernel,
        grid_spec=pltpu.PrefetchScalarGridSpec(
            num_scalar_prefetch=1,
            grid=(rows // block,),
            in_specs=[
                tile_spec,
                pl.BlockSpec((block, depth), lambda i, place: (i, 0)),
                pl.BlockSpec((depth, cols), lambda i, place: (0, 0), pipeline_mode=pl.Buffered(1)),
                pl.BlockSpec((1, cols), lambda i, place: (0, 0)),
            ],
            out_specs=tile_spec,
        ),
        out_shape=pltpu.VMEM((rows, cols), jnp.float32),
        compiler_params=pltpu.CompilerParams(vmem_limit_bytes=8 * 2**20),
        cost_estimate=pl.CostEstimate(
            flops=2 * rows * cols * depth, bytes_accessed=4 * rows * cols, transcendentals=0
        ),
        name="gram_tile",
    )(place, normals, left, right, regular)


def tile_kernel(count, block_ids_ref, place_ref, system_ref, *refs):
    here_refs, sent_refs = refs[:count], refs[count : 2 * count]
    gram_ref, right_ref, inverse_ref, out_ref = refs[2 * count :]
    step = pl.program_id(0)
    block = out_ref.shape[0]
    per_piece = pl.num_programs(0) // count
    even = lax.rem(place_ref[1], 2) == 0
    slot = step // per_piece
    rows = pl.ds(pl.multiple_of(lax.rem(step, per_piece) * block, block), block)
    strip = jnp.where(even, here_refs[0][rows, :], sent_refs[0][rows, :])
    for i in range(1, count):
        strip = jnp.where(slot == i, jnp.where(even, here_refs[i][rows, :], sent_refs[i][rows, :]), strip)
    panel = split_dot(strip + gram_ref[...], inverse_ref[...])
    high, low = split(panel)
    left = jnp.concatenate([high, high, low], axis=1)
    out_ref[...] = system_ref[...] + jnp.dot(left, right_ref[...], preferred_element_type=jnp.float32)


def tile_rows(place, block_ids, system, here, sent, gram_cols, right, inverse):
    rows, cols = system.shape
    count = len(here)
    block = rows // block_ids.shape[0]

    def whole(array):
        return pl.BlockSpec(
            array.shape, lambda i, ids, place: (0,) * array.ndim, pipeline_mode=pl.Buffered(1)
        )

    tile_spec = pl.BlockSpec((block, cols), lambda i, ids, place: (ids[i], 0))
    gram_spec = pl.BlockSpec((block, B), lambda i, ids, place: (ids[i], 0))
    return pl.pallas_call(
        functools.partial(tile_kernel, count),
        grid_spec=pltpu.PrefetchScalarGridSpec(
            num_scalar_prefetch=2,
            grid=(block_ids.shape[0],),
            in_specs=[tile_spec]
            + [whole(array) for array in [*here, *sent]]
            + [gram_spec, whole(right), whole(inverse)],
            out_specs=tile_spec,
        ),
        out_shape=jax.ShapeDtypeStruct((rows, cols), jnp.float32),
        compiler_params=pltpu.CompilerParams(vmem_limit_bytes=16 * 2**20),
        cost_estimate=pl.CostEstimate(
            flops=6 * rows * cols * B, bytes_accessed=4 * rows * cols, transcendentals=0
        ),
        name="tile_rows",
    )(block_ids, place, system, *here, *sent, gram_cols, right, inverse)


def shifted(value, axis, by):
    peers = lax.axis_size(axis)
    return lax.ppermute(value, axis, [(i, (i + by) % peers) for i in range(peers)])


def spread(value, axis, bits):
    peers = lax.axis_size(axis)
    me = lax.axis_index(axis)
    reached = [0]
    for bit in bits:
        pairs = [(i, i | bit) for i in reached if i | bit < peers]
        got = lax.ppermute(value, axis, pairs)
        value = jnp.where((me & bit) != 0, got, value)
        reached += [to for _, to in pairs]
    return value


def filter_matrix_of(filter_blocks, sources):
    count = sources.shape[0]
    lag = jnp.arange(count, dtype=jnp.int32)[:, None] - sources[None, :]
    lag = lag[:, None, :, None]
    own = filter_blocks[0][None, :, None, :]
    prior = filter_blocks[1][None, :, None, :]
    blocks = jnp.where(lag == 0, own, jnp.where(lag == 1, prior, 0.0))
    return blocks.reshape(count * P_SIZE, count * P_SIZE)


def to_odd_core(value):
    return lax.ppermute(value, "col", [(c, c + 1) for c in range(0, lax.axis_size("col"), 2)])


def row_strip(normals):
    peers = lax.axis_size("col")
    chips = peers // 2
    rows = normals.shape[0]
    col_index = lax.axis_index("col")
    chip = col_index // 2
    if chips > 4:
        size = rows // chips
        share = normals[:size, :B]
        for z in range(1, chips):
            got = lax.ppermute(normals[z * size : (z + 1) * size, :B], "col", [(0, 2 * z)])
            share = jnp.where(chip == z, got, share)
        cores = [list(range(k, peers, 2)) for k in range(2)]
        return [(jnp.int32(0), lax.all_gather(share, "col", axis=0, tiled=True, axis_index_groups=cores))]
    count = chips - 1
    size = rows // count
    local = [normals[i * size : (i + 1) * size, :B] for i in range(count)]
    arrived = None
    for i in reversed(range(count)):
        got = lax.ppermute(local[i], "col", [(0, 2 * (1 + i))])
        arrived = got if arrived is None else arrived + got
    at_source = chip == 0
    mine = jnp.where(at_source, local[0], arrived)
    pieces = [(jnp.where(at_source, 0, chip - 1), mine)]
    for s in range(1, count):
        pairs = [(2 * (1 + i), 2 * (1 + (i + s) % count)) for i in range(count)]
        got = lax.ppermute(mine, "col", pairs)
        which = -s % count
        piece = jnp.where(at_source, local[which], got)
        pieces.append((jnp.where(at_source, which, (chip - 1 - s) % count), piece))
    return pieces


def leading_block(normals):
    row_peers, col_peers = lax.axis_size("row"), lax.axis_size("col")
    here = lax.axis_index("row") * col_peers + lax.axis_index("col")
    total = row_peers * col_peers
    held = normals[:B, :B]
    reached = [0]
    bits = [1 << i for i in range((total - 1).bit_length())]
    bits = [b for b in reversed(bits) if 1 < b < col_peers] + [b for b in bits if b >= col_peers] + [1]
    for bit in bits:
        pairs = [(i, i | bit) for i in reached if i | bit < total]
        got = lax.ppermute(held, ("row", "col"), pairs)
        held = jnp.where((here & bit) != 0, got, held)
        reached += [to for _, to in pairs]
    return held


def body(normals, design, filter_blocks, regular):
    rows_here, cols_here = normals.shape
    obs_here = design.shape[0]
    row_peers = lax.axis_size("row")
    row_index = lax.axis_index("row")
    col_index = lax.axis_index("col")
    blocks_here = obs_here // P_SIZE
    obs = row_peers * obs_here
    core = col_index % 2

    corner = leading_block(normals)
    pieces = row_strip(normals)

    along = lax.all_gather(design, "col", axis=1, tiled=True)
    parts = []
    for s in range(row_peers):
        to = (row_index + s) % row_peers
        far = lax.dynamic_slice_in_dim(along, to * rows_here + core * cols_here, cols_here, axis=1)
        part = jnp.concatenate([design, far, along[:, :B]], axis=1)
        parts.append(shifted(part, "row", s) if s else part)
    own = jnp.concatenate([part[:, cols_here : 2 * cols_here] for part in parts], axis=0)
    other = lax.ppermute(own, "col", [(c, c ^ 1) for c in range(lax.axis_size("col"))])
    lead = jnp.concatenate([part[:, 2 * cols_here :] for part in parts], axis=0)

    bits = [1 << i for i in range((row_peers - 1).bit_length())]
    strips = [
        spread(normals[: B // 2], "row", bits),
        spread(normals[B // 2 : B], "row", bits[::-1]),
    ]

    positions = jnp.arange(obs // P_SIZE, dtype=jnp.int32)
    passed = positions // blocks_here
    order = ((row_index - passed) % row_peers) * blocks_here + positions % blocks_here
    filters = filter_matrix_of(filter_blocks, order)
    lead_reg = regular[:B].reshape(1, B)
    own_reg = lax.dynamic_slice_in_dim(regular, col_index * cols_here, cols_here).reshape(1, cols_here)
    place = jnp.stack([row_index, col_index]).astype(jnp.int32)
    inverse = corner_factor(corner, lead, filters, lead_reg)
    gram_left, gram_right, gram_rows, gram_cols = filter_sides(place, parts, other, filters, own_reg, lead_reg)
    system = gram_tile(place, normals, gram_left, gram_right, own_reg)
    system = pltpu.with_memory_space_constraint(system, pltpu.VMEM)
    right = right_side(place, strips, gram_rows, inverse)

    here = [piece for _, piece in pieces]
    sent = [to_odd_core(piece) for piece in here]
    per_piece = here[0].shape[0] // block_rows(rows_here // 2)
    which = jnp.stack([index for index, _ in pieces])
    block_ids = which[:, None] * per_piece + jnp.arange(per_piece, dtype=jnp.int32)[None, :]
    block_ids = block_ids.reshape(-1).astype(jnp.int32)
    return tile_rows(place, block_ids, system, here, sent, gram_cols, right, inverse)


def solution(mesh):
    in_specs = (P("row", "col"), P("row", "col"), P(), P())
    out_specs = P("row", "col")
    return jax.shard_map(body, mesh=mesh, in_specs=in_specs, out_specs=out_specs, check_vma=False)
```

```python
import functools

import jax
import jax.numpy as jnp
from jax import lax
from jax.experimental import pallas as pl
from jax.experimental.pallas import tpu as pltpu
from jax.sharding import PartitionSpec as P

B = 256
P_SIZE = 32
STRIP = 32
PIVOTS = 4
HIGHEST = lax.Precision.HIGHEST


def exact_dot(left, right, left_dim, right_dim):
    return lax.dot_general(
        left,
        right,
        (((left_dim,), (right_dim,)), ((), ())),
        precision=HIGHEST,
        preferred_element_type=jnp.float32,
    )


def split(value):
    high = value.astype(jnp.bfloat16)
    low = (value - high.astype(jnp.float32)).astype(jnp.bfloat16)
    return high, low


def split_dot(left, right):
    left_high, left_low = split(left)
    right_high, right_low = split(right)
    wide = functools.partial(jnp.dot, preferred_element_type=jnp.float32)
    return wide(left_high, right_high) + (wide(left_high, right_low) + wide(left_low, right_high))


def corner_kernel(block_ref, design_ref, filter_ref, regular_ref, inverse_ref, upper):
    filtered = exact_dot(filter_ref[...], design_ref[...], 1, 0)
    row_pos = lax.broadcasted_iota(jnp.int32, (B, B), 0)
    col_pos = lax.broadcasted_iota(jnp.int32, (B, B), 1)
    system = block_ref[...] + exact_dot(filtered, filtered, 0, 0)
    system = system + jnp.where(row_pos == col_pos, regular_ref[...], 0.0)
    identity = jnp.where(row_pos == col_pos, 1.0, 0.0)
    half = B // 2
    sub = lax.broadcasted_iota(jnp.int32, (STRIP, half), 0)
    lane = lax.broadcasted_iota(jnp.int32, (STRIP, half), 1)
    zero = jnp.zeros((STRIP, half), jnp.float32)
    for start in range(0, B, STRIP):
        rows = slice(start, start + STRIP)
        strip = jnp.concatenate([system[rows, :], identity[rows, :]], axis=1)
        if start:
            done = upper[:start, :]
            strip = strip - exact_dot(done[:, rows], done, 0, 0)
        low = 0 if start < half else half
        held = [strip[:, at : at + half] for at in range(low, low + 3 * half, half)]
        for first in range(0, STRIP, PIVOTS):
            at = start + first - low
            columns = [
                jnp.broadcast_to(held[0][:, at + q : at + q + 1], (STRIP, half)) for q in range(PIVOTS)
            ]
            pivot_rows = [[part[first + q : first + q + 1, :] for part in held] for q in range(PIVOTS)]
            for q in range(PIVOTS):
                j = first + q
                coef = jnp.where(sub > j, columns[q] * (1.0 / columns[q][j : j + 1, :]), 0.0)
                for m in range(q + 1, PIVOTS):
                    columns[m] = columns[m] - coef * columns[m][j : j + 1, :]
                    scale = coef[first + m : first + m + 1, :]
                    pivot_rows[m] = [
                        row - scale * other for row, other in zip(pivot_rows[m], pivot_rows[q])
                    ]
                held = [part - coef * row for part, row in zip(held, pivot_rows[q])]
        diag = jnp.sum(jnp.where(lane == sub + (start - low), held[0], 0.0), axis=1, keepdims=True)
        held = [part / jnp.sqrt(diag) for part in held]
        upper[rows, :] = jnp.concatenate([*held, zero] if low == 0 else [zero, *held], axis=1)
    inverse_ref[...] = upper[:, B:].T


def corner_factor(block, design, filter_matrix, regular):
    return pl.pallas_call(
        corner_kernel,
        out_shape=jax.ShapeDtypeStruct((B, B), jnp.float32),
        scratch_shapes=[pltpu.VMEM((B, 2 * B), jnp.float32)],
        compiler_params=pltpu.CompilerParams(vmem_limit_bytes=4 * 2**20),
        cost_estimate=pl.CostEstimate(flops=10**9, bytes_accessed=2**20, transcendentals=0),
        name="corner_factor",
    )(block, design, filter_matrix, regular)


def right_kernel(place_ref, high_ref, low_ref, gram_ref, inverse_ref, out_ref):
    strip = jnp.concatenate([high_ref[...], low_ref[...]], axis=0) + gram_ref[...]
    panel_high, panel_low = split(-split_dot(inverse_ref[...].T, strip))
    out_ref[:B, :] = panel_high
    out_ref[B : 2 * B, :] = panel_low
    out_ref[2 * B :, :] = panel_high

    @pl.when(place_ref[1] == 0)
    def _():
        row_pos = lax.broadcasted_iota(jnp.int32, (B, B), 0)
        identity = jnp.where(row_pos == lax.broadcasted_iota(jnp.int32, (B, B), 1), 1.0, 0.0)
        identity = identity.astype(jnp.bfloat16)
        out_ref[:B, :B] = identity
        out_ref[B : 2 * B, :B] = jnp.zeros((B, B), jnp.bfloat16)
        out_ref[2 * B :, :B] = identity


def right_side(place, strips, gram_rows, inverse):
    cols = gram_rows.shape[1]
    return pl.pallas_call(
        right_kernel,
        in_specs=[pl.BlockSpec(memory_space=pltpu.SMEM)] + [pl.BlockSpec(memory_space=pltpu.VMEM)] * 4,
        out_specs=pl.BlockSpec(memory_space=pltpu.VMEM),
        out_shape=jax.ShapeDtypeStruct((3 * B, cols), jnp.bfloat16),
        compiler_params=pltpu.CompilerParams(vmem_limit_bytes=20 * 2**20),
        cost_estimate=pl.CostEstimate(
            flops=6 * cols * B * B, bytes_accessed=12 * cols * B, transcendentals=0
        ),
        name="right_side",
    )(place, *strips, gram_rows, inverse)


def filter_kernel(count, place_ref, *refs):
    parts = refs[:count]
    other_ref, filter_ref, regular_ref, lead_reg_ref = refs[count : count + 4]
    left_ref, right_ref, gram_rows_ref, gram_cols_ref = refs[count + 4 :]
    row_index, col_index = place_ref[0], place_ref[1]
    cols = right_ref.shape[1]
    obs = filter_ref.shape[0]
    core = lax.rem(col_index, 2)
    design = jnp.concatenate([part[...] for part in parts], axis=0)
    filtered = split_dot(filter_ref[...], design)
    here, rows_own, lead = filtered[:, :cols], filtered[:, cols : 2 * cols], filtered[:, 2 * cols :]
    row_pos = lax.broadcasted_iota(jnp.int32, (B, cols), 0)
    col_pos = lax.broadcasted_iota(jnp.int32, (1, cols), 1) + col_index * cols
    gram_rows_ref[...] = split_dot(lead.T, here) + jnp.where(row_pos == col_pos, regular_ref[...], 0.0)
    high, low = split(jnp.where(col_pos < B, 0.0, here))
    right_ref[:obs, :] = high
    right_ref[obs : 2 * obs, :] = low
    right_ref[2 * obs :, :] = high
    rows_other = split_dot(filter_ref[...], other_ref[...])
    for half, value in ((core, rows_own), (1 - core, rows_other)):
        value = value.T
        high, low = split(value)
        rows = pl.ds(pl.multiple_of(half * cols, cols), cols)
        left_ref[rows, :obs] = high
        left_ref[rows, obs : 2 * obs] = high
        left_ref[rows, 2 * obs :] = low
        row_pos = lax.broadcasted_iota(jnp.int32, (cols, B), 0) + (2 * row_index + half) * cols
        lead_pos = lax.broadcasted_iota(jnp.int32, (cols, B), 1)
        gram_cols_ref[rows, :] = split_dot(value, lead) + jnp.where(
            row_pos == lead_pos, lead_reg_ref[...], 0.0
        )


def filter_sides(place, parts, other, filter_matrix, regular, lead_reg):
    cols = other.shape[1]
    obs = filter_matrix.shape[0]
    vmem = pl.BlockSpec(memory_space=pltpu.VMEM)
    return pl.pallas_call(
        functools.partial(filter_kernel, len(parts)),
        in_specs=[pl.BlockSpec(memory_space=pltpu.SMEM)] + [vmem] * (len(parts) + 4),
        out_specs=[vmem] * 4,
        out_shape=[
            jax.ShapeDtypeStruct((2 * cols, 3 * obs), jnp.bfloat16),
            jax.ShapeDtypeStruct((3 * obs, cols), jnp.bfloat16),
            jax.ShapeDtypeStruct((B, cols), jnp.float32),
            jax.ShapeDtypeStruct((2 * cols, B), jnp.float32),
        ],
        compiler_params=pltpu.CompilerParams(vmem_limit_bytes=20 * 2**20),
        cost_estimate=pl.CostEstimate(
            flops=18 * cols * obs * B, bytes_accessed=24 * cols * B, transcendentals=0
        ),
        name="filter_sides",
    )(place, *parts, other, filter_matrix, regular, lead_reg)


def gram_kernel(place_ref, normals_ref, left_ref, right_ref, regular_ref, out_ref):
    step = pl.program_id(0)
    block, cols = out_ref.shape
    first_col = place_ref[1] * cols
    col_pos = lax.broadcasted_iota(jnp.int32, (1, cols), 1) + first_col
    keep = jnp.where(col_pos < B, 0.0, 1.0)
    out_ref[...] = normals_ref[...] * keep + jnp.dot(
        left_ref[...], right_ref[...], preferred_element_type=jnp.float32
    )
    first_row = (place_ref[0] * pl.num_programs(0) + step) * block

    @pl.when((first_row < first_col + cols) & (first_col < first_row + block))
    def _():
        row_pos = lax.broadcasted_iota(jnp.int32, (block, cols), 0) + first_row
        on_diag = (row_pos == col_pos) & (col_pos >= B)
        out_ref[...] = out_ref[...] + jnp.where(on_diag, regular_ref[...], 0.0)


def block_rows(half):
    return max(size for size in range(128, 513, 128) if half % size == 0)


def gram_tile(place, normals, left, right, regular):
    rows, cols = normals.shape
    block = block_rows(rows // 2)
    depth = right.shape[0]
    tile_spec = pl.BlockSpec((block, cols), lambda i, place: (i, 0))
    return pl.pallas_call(
        gram_kernel,
        grid_spec=pltpu.PrefetchScalarGridSpec(
            num_scalar_prefetch=1,
            grid=(rows // block,),
            in_specs=[
                tile_spec,
                pl.BlockSpec((block, depth), lambda i, place: (i, 0)),
                pl.BlockSpec((depth, cols), lambda i, place: (0, 0), pipeline_mode=pl.Buffered(1)),
                pl.BlockSpec((1, cols), lambda i, place: (0, 0)),
            ],
            out_specs=tile_spec,
        ),
        out_shape=pltpu.VMEM((rows, cols), jnp.float32),
        compiler_params=pltpu.CompilerParams(vmem_limit_bytes=8 * 2**20),
        cost_estimate=pl.CostEstimate(
            flops=2 * rows * cols * depth, bytes_accessed=4 * rows * cols, transcendentals=0
        ),
        name="gram_tile",
    )(place, normals, left, right, regular)


def tile_kernel(count, block_ids_ref, place_ref, system_ref, *refs):
    here_refs, sent_refs = refs[:count], refs[count : 2 * count]
    gram_ref, right_ref, inverse_ref, out_ref = refs[2 * count :]
    step = pl.program_id(0)
    block = out_ref.shape[0]
    per_piece = pl.num_programs(0) // count
    even = lax.rem(place_ref[1], 2) == 0
    slot = step // per_piece
    rows = pl.ds(pl.multiple_of(lax.rem(step, per_piece) * block, block), block)
    strip = jnp.where(even, here_refs[0][rows, :], sent_refs[0][rows, :])
    for i in range(1, count):
        strip = jnp.where(slot == i, jnp.where(even, here_refs[i][rows, :], sent_refs[i][rows, :]), strip)
    panel = split_dot(strip + gram_ref[...], inverse_ref[...])
    high, low = split(panel)
    left = jnp.concatenate([high, high, low], axis=1)
    out_ref[...] = system_ref[...] + jnp.dot(left, right_ref[...], preferred_element_type=jnp.float32)


def tile_rows(place, block_ids, system, here, sent, gram_cols, right, inverse):
    rows, cols = system.shape
    count = len(here)
    block = rows // block_ids.shape[0]

    def whole(array):
        return pl.BlockSpec(
            array.shape, lambda i, ids, place: (0,) * array.ndim, pipeline_mode=pl.Buffered(1)
        )

    tile_spec = pl.BlockSpec((block, cols), lambda i, ids, place: (ids[i], 0))
    gram_spec = pl.BlockSpec((block, B), lambda i, ids, place: (ids[i], 0))
    return pl.pallas_call(
        functools.partial(tile_kernel, count),
        grid_spec=pltpu.PrefetchScalarGridSpec(
            num_scalar_prefetch=2,
            grid=(block_ids.shape[0],),
            in_specs=[tile_spec]
            + [whole(array) for array in [*here, *sent]]
            + [gram_spec, whole(right), whole(inverse)],
            out_specs=tile_spec,
        ),
        out_shape=jax.ShapeDtypeStruct((rows, cols), jnp.float32),
        compiler_params=pltpu.CompilerParams(vmem_limit_bytes=16 * 2**20),
        cost_estimate=pl.CostEstimate(
            flops=6 * rows * cols * B, bytes_accessed=4 * rows * cols, transcendentals=0
        ),
        name="tile_rows",
    )(block_ids, place, system, *here, *sent, gram_cols, right, inverse)


def after(value, earlier):
    return lax.optimization_barrier((value, earlier))[0]


def shifted(value, axis, by):
    peers = lax.axis_size(axis)
    return lax.ppermute(value, axis, [(i, (i + by) % peers) for i in range(peers)])


def spread(value, axis, bits):
    peers = lax.axis_size(axis)
    me = lax.axis_index(axis)
    reached = [0]
    for bit in bits:
        pairs = [(i, i | bit) for i in reached if i | bit < peers]
        got = lax.ppermute(value, axis, pairs)
        value = jnp.where((me & bit) != 0, got, value)
        reached += [to for _, to in pairs]
    return value


def filter_matrix_of(filter_blocks, sources):
    count = sources.shape[0]
    lag = jnp.arange(count, dtype=jnp.int32)[:, None] - sources[None, :]
    lag = lag[:, None, :, None]
    own = filter_blocks[0][None, :, None, :]
    prior = filter_blocks[1][None, :, None, :]
    blocks = jnp.where(lag == 0, own, jnp.where(lag == 1, prior, 0.0))
    return blocks.reshape(count * P_SIZE, count * P_SIZE)


def to_odd_core(value):
    return lax.ppermute(value, "col", [(c, c + 1) for c in range(0, lax.axis_size("col"), 2)])


def row_strip(normals, earlier):
    peers = lax.axis_size("col")
    chips = peers // 2
    rows = normals.shape[0]
    col_index = lax.axis_index("col")
    chip = col_index // 2
    if chips > 4:
        size = rows // chips
        share = normals[:size, :B]
        for z in range(1, chips):
            got = lax.ppermute(normals[z * size : (z + 1) * size, :B], "col", [(0, 2 * z)])
            share = jnp.where(chip == z, got, share)
        cores = [list(range(k, peers, 2)) for k in range(2)]
        return [(jnp.int32(0), lax.all_gather(share, "col", axis=0, tiled=True, axis_index_groups=cores))]
    count = chips - 1
    size = rows // count
    local = [normals[i * size : (i + 1) * size, :B] for i in range(count)]
    local = after(local, earlier)
    arrived = None
    for i in reversed(range(count)):
        got = lax.ppermute(local[i], "col", [(0, 2 * (1 + i))])
        arrived = got if arrived is None else arrived + got
    at_source = chip == 0
    mine = jnp.where(at_source, local[0], arrived)
    pieces = [(jnp.where(at_source, 0, chip - 1), mine)]
    for s in range(1, count):
        pairs = [(2 * (1 + i), 2 * (1 + (i + s) % count)) for i in range(count)]
        got = lax.ppermute(mine, "col", pairs)
        which = -s % count
        piece = jnp.where(at_source, local[which], got)
        pieces.append((jnp.where(at_source, which, (chip - 1 - s) % count), piece))
    return pieces


def doubled(value, bits, reached):
    row_peers, col_peers = lax.axis_size("row"), lax.axis_size("col")
    here = lax.axis_index("row") * col_peers + lax.axis_index("col")
    for bit in bits:
        pairs = [(i, i | bit) for i in reached if i | bit < row_peers * col_peers]
        got = lax.ppermute(value, ("row", "col"), pairs)
        value = jnp.where((here & bit) != 0, got, value)
        reached = reached + [to for _, to in pairs]
    return value, reached


def body(normals, design, filter_blocks, regular):
    rows_here, cols_here = normals.shape
    obs_here = design.shape[0]
    row_peers = lax.axis_size("row")
    row_index = lax.axis_index("row")
    col_index = lax.axis_index("col")
    blocks_here = obs_here // P_SIZE
    obs = row_peers * obs_here
    core = col_index % 2

    col_peers = lax.axis_size("col")
    index_bits = [1 << i for i in range((row_peers * col_peers - 1).bit_length())]
    along_z = [bit for bit in reversed(index_bits) if 1 < bit < col_peers]
    block, reached = doubled(normals[:B, :B], along_z, [0])
    even_corner, reached = doubled(block, [bit for bit in index_bits if bit >= col_peers], reached)
    corner, _ = doubled(even_corner, [1], reached)
    pieces = row_strip(normals, block)

    along = lax.all_gather(design, "col", axis=1, tiled=True)
    parts = []
    for s in range(row_peers):
        to = (row_index + s) % row_peers
        far = lax.dynamic_slice_in_dim(along, to * rows_here + core * cols_here, cols_here, axis=1)
        part = jnp.concatenate([design, far, along[:, :B]], axis=1)
        parts.append(shifted(part, "row", s) if s else part)
    own = jnp.concatenate([part[:, cols_here : 2 * cols_here] for part in parts], axis=0)
    other = lax.ppermute(own, "col", [(c, c ^ 1) for c in range(lax.axis_size("col"))])
    lead = jnp.concatenate([part[:, 2 * cols_here :] for part in parts], axis=0)

    bits = [1 << i for i in range((row_peers - 1).bit_length())]
    halves = after([normals[: B // 2], normals[B // 2 : B]], even_corner)
    strips = [spread(halves[0], "row", bits), spread(halves[1], "row", bits[::-1])]

    positions = jnp.arange(obs // P_SIZE, dtype=jnp.int32)
    passed = positions // blocks_here
    order = ((row_index - passed) % row_peers) * blocks_here + positions % blocks_here
    filters = filter_matrix_of(filter_blocks, order)
    lead_reg = regular[:B].reshape(1, B)
    own_reg = lax.dynamic_slice_in_dim(regular, col_index * cols_here, cols_here).reshape(1, cols_here)
    place = jnp.stack([row_index, col_index]).astype(jnp.int32)
    inverse = corner_factor(corner, lead, filters, lead_reg)
    gram_left, gram_right, gram_rows, gram_cols = filter_sides(place, parts, other, filters, own_reg, lead_reg)
    system = gram_tile(place, normals, gram_left, gram_right, own_reg)
    system = pltpu.with_memory_space_constraint(system, pltpu.VMEM)
    right = right_side(place, strips, gram_rows, inverse)

    here = [piece for _, piece in pieces]
    sent = [to_odd_core(piece) for piece in here]
    per_piece = here[0].shape[0] // block_rows(rows_here // 2)
    which = jnp.stack([index for index, _ in pieces])
    block_ids = which[:, None] * per_piece + jnp.arange(per_piece, dtype=jnp.int32)[None, :]
    block_ids = block_ids.reshape(-1).astype(jnp.int32)
    return tile_rows(place, block_ids, system, here, sent, gram_cols, right, inverse)


def solution(mesh):
    in_specs = (P("row", "col"), P("row", "col"), P(), P())
    out_specs = P("row", "col")
    return jax.shard_map(body, mesh=mesh, in_specs=in_specs, out_specs=out_specs, check_vma=False)
```

```python
import functools

import jax
import jax.numpy as jnp
from jax import lax
from jax.experimental import pallas as pl
from jax.experimental.pallas import tpu as pltpu
from jax.sharding import PartitionSpec as P

B = 256
P_SIZE = 32
STRIP = 32
PIVOTS = 4
HIGHEST = lax.Precision.HIGHEST


def exact_dot(left, right, left_dim, right_dim):
    return lax.dot_general(
        left,
        right,
        (((left_dim,), (right_dim,)), ((), ())),
        precision=HIGHEST,
        preferred_element_type=jnp.float32,
    )


def split(value):
    high = value.astype(jnp.bfloat16)
    low = (value - high.astype(jnp.float32)).astype(jnp.bfloat16)
    return high, low


def split_dot(left, right):
    left_high, left_low = split(left)
    right_high, right_low = split(right)
    wide = functools.partial(jnp.dot, preferred_element_type=jnp.float32)
    return wide(left_high, right_high) + (wide(left_high, right_low) + wide(left_low, right_high))


def corner_kernel(block_ref, design_ref, filter_ref, regular_ref, inverse_ref, upper):
    filtered = exact_dot(filter_ref[...], design_ref[...], 1, 0)
    row_pos = lax.broadcasted_iota(jnp.int32, (B, B), 0)
    col_pos = lax.broadcasted_iota(jnp.int32, (B, B), 1)
    system = block_ref[...] + exact_dot(filtered, filtered, 0, 0)
    system = system + jnp.where(row_pos == col_pos, regular_ref[...], 0.0)
    identity = jnp.where(row_pos == col_pos, 1.0, 0.0)
    half = B // 2
    sub = lax.broadcasted_iota(jnp.int32, (STRIP, half), 0)
    lane = lax.broadcasted_iota(jnp.int32, (STRIP, half), 1)
    zero = jnp.zeros((STRIP, half), jnp.float32)
    for start in range(0, B, STRIP):
        rows = slice(start, start + STRIP)
        strip = jnp.concatenate([system[rows, :], identity[rows, :]], axis=1)
        if start:
            done = upper[:start, :]
            strip = strip - exact_dot(done[:, rows], done, 0, 0)
        low = 0 if start < half else half
        held = [strip[:, at : at + half] for at in range(low, low + 3 * half, half)]
        for first in range(0, STRIP, PIVOTS):
            at = start + first - low
            columns = [
                jnp.broadcast_to(held[0][:, at + q : at + q + 1], (STRIP, half)) for q in range(PIVOTS)
            ]
            pivot_rows = [[part[first + q : first + q + 1, :] for part in held] for q in range(PIVOTS)]
            for q in range(PIVOTS):
                j = first + q
                coef = jnp.where(sub > j, columns[q] * (1.0 / columns[q][j : j + 1, :]), 0.0)
                for m in range(q + 1, PIVOTS):
                    columns[m] = columns[m] - coef * columns[m][j : j + 1, :]
                    scale = coef[first + m : first + m + 1, :]
                    pivot_rows[m] = [
                        row - scale * other for row, other in zip(pivot_rows[m], pivot_rows[q])
                    ]
                held = [part - coef * row for part, row in zip(held, pivot_rows[q])]
        diag = jnp.sum(jnp.where(lane == sub + (start - low), held[0], 0.0), axis=1, keepdims=True)
        held = [part / jnp.sqrt(diag) for part in held]
        upper[rows, :] = jnp.concatenate([*held, zero] if low == 0 else [zero, *held], axis=1)
    inverse_ref[...] = upper[:, B:].T


def corner_factor(block, design, filter_matrix, regular):
    return pl.pallas_call(
        corner_kernel,
        out_shape=jax.ShapeDtypeStruct((B, B), jnp.float32),
        scratch_shapes=[pltpu.VMEM((B, 2 * B), jnp.float32)],
        compiler_params=pltpu.CompilerParams(vmem_limit_bytes=4 * 2**20),
        cost_estimate=pl.CostEstimate(flops=10**9, bytes_accessed=2**20, transcendentals=0),
        name="corner_factor",
    )(block, design, filter_matrix, regular)


def right_kernel(place_ref, strip_ref, gram_ref, inverse_ref, out_ref):
    strip = strip_ref[...] + gram_ref[...]
    panel_high, panel_low = split(-split_dot(inverse_ref[...].T, strip))
    out_ref[:B, :] = panel_high
    out_ref[B : 2 * B, :] = panel_low
    out_ref[2 * B :, :] = panel_high

    @pl.when(place_ref[1] == 0)
    def _():
        row_pos = lax.broadcasted_iota(jnp.int32, (B, B), 0)
        identity = jnp.where(row_pos == lax.broadcasted_iota(jnp.int32, (B, B), 1), 1.0, 0.0)
        identity = identity.astype(jnp.bfloat16)
        out_ref[:B, :B] = identity
        out_ref[B : 2 * B, :B] = jnp.zeros((B, B), jnp.bfloat16)
        out_ref[2 * B :, :B] = identity


def right_side(place, strip, gram_rows, inverse):
    cols = gram_rows.shape[1]
    return pl.pallas_call(
        right_kernel,
        in_specs=[pl.BlockSpec(memory_space=pltpu.SMEM)] + [pl.BlockSpec(memory_space=pltpu.VMEM)] * 3,
        out_specs=pl.BlockSpec(memory_space=pltpu.VMEM),
        out_shape=jax.ShapeDtypeStruct((3 * B, cols), jnp.bfloat16),
        compiler_params=pltpu.CompilerParams(vmem_limit_bytes=20 * 2**20),
        cost_estimate=pl.CostEstimate(
            flops=6 * cols * B * B, bytes_accessed=12 * cols * B, transcendentals=0
        ),
        name="right_side",
    )(place, strip, gram_rows, inverse)


def filter_kernel(count, place_ref, *refs):
    parts = refs[:count]
    other_ref, filter_ref, regular_ref, lead_reg_ref = refs[count : count + 4]
    left_ref, right_ref, gram_rows_ref, gram_cols_ref = refs[count + 4 :]
    row_index, col_index = place_ref[0], place_ref[1]
    cols = right_ref.shape[1]
    obs = filter_ref.shape[0]
    core = lax.rem(col_index, 2)
    design = jnp.concatenate([part[...] for part in parts], axis=0)
    filtered = split_dot(filter_ref[...], design)
    here, rows_own, lead = filtered[:, :cols], filtered[:, cols : 2 * cols], filtered[:, 2 * cols :]
    row_pos = lax.broadcasted_iota(jnp.int32, (B, cols), 0)
    col_pos = lax.broadcasted_iota(jnp.int32, (1, cols), 1) + col_index * cols
    gram_rows_ref[...] = split_dot(lead.T, here) + jnp.where(row_pos == col_pos, regular_ref[...], 0.0)
    high, low = split(jnp.where(col_pos < B, 0.0, here))
    right_ref[:obs, :] = high
    right_ref[obs : 2 * obs, :] = low
    right_ref[2 * obs :, :] = high
    rows_other = split_dot(filter_ref[...], other_ref[...])
    for half, value in ((core, rows_own), (1 - core, rows_other)):
        value = value.T
        high, low = split(value)
        rows = pl.ds(pl.multiple_of(half * cols, cols), cols)
        left_ref[rows, :obs] = high
        left_ref[rows, obs : 2 * obs] = high
        left_ref[rows, 2 * obs :] = low
        row_pos = lax.broadcasted_iota(jnp.int32, (cols, B), 0) + (2 * row_index + half) * cols
        lead_pos = lax.broadcasted_iota(jnp.int32, (cols, B), 1)
        gram_cols_ref[rows, :] = split_dot(value, lead) + jnp.where(
            row_pos == lead_pos, lead_reg_ref[...], 0.0
        )


def filter_sides(place, parts, other, filter_matrix, regular, lead_reg):
    cols = other.shape[1]
    obs = filter_matrix.shape[0]
    vmem = pl.BlockSpec(memory_space=pltpu.VMEM)
    return pl.pallas_call(
        functools.partial(filter_kernel, len(parts)),
        in_specs=[pl.BlockSpec(memory_space=pltpu.SMEM)] + [vmem] * (len(parts) + 4),
        out_specs=[vmem] * 4,
        out_shape=[
            jax.ShapeDtypeStruct((2 * cols, 3 * obs), jnp.bfloat16),
            jax.ShapeDtypeStruct((3 * obs, cols), jnp.bfloat16),
            jax.ShapeDtypeStruct((B, cols), jnp.float32),
            jax.ShapeDtypeStruct((2 * cols, B), jnp.float32),
        ],
        compiler_params=pltpu.CompilerParams(vmem_limit_bytes=20 * 2**20),
        cost_estimate=pl.CostEstimate(
            flops=18 * cols * obs * B, bytes_accessed=24 * cols * B, transcendentals=0
        ),
        name="filter_sides",
    )(place, *parts, other, filter_matrix, regular, lead_reg)


def gram_kernel(place_ref, normals_ref, left_ref, right_ref, regular_ref, out_ref):
    step = pl.program_id(0)
    block, cols = out_ref.shape
    first_col = place_ref[1] * cols
    col_pos = lax.broadcasted_iota(jnp.int32, (1, cols), 1) + first_col
    keep = jnp.where(col_pos < B, 0.0, 1.0)
    out_ref[...] = normals_ref[...] * keep + jnp.dot(
        left_ref[...], right_ref[...], preferred_element_type=jnp.float32
    )
    first_row = (place_ref[0] * pl.num_programs(0) + step) * block

    @pl.when((first_row < first_col + cols) & (first_col < first_row + block))
    def _():
        row_pos = lax.broadcasted_iota(jnp.int32, (block, cols), 0) + first_row
        on_diag = (row_pos == col_pos) & (col_pos >= B)
        out_ref[...] = out_ref[...] + jnp.where(on_diag, regular_ref[...], 0.0)


def block_rows(half):
    return max(size for size in range(128, 513, 128) if half % size == 0)


def gram_tile(place, normals, left, right, regular):
    rows, cols = normals.shape
    block = block_rows(rows // 2)
    depth = right.shape[0]
    tile_spec = pl.BlockSpec((block, cols), lambda i, place: (i, 0))
    return pl.pallas_call(
        gram_kernel,
        grid_spec=pltpu.PrefetchScalarGridSpec(
            num_scalar_prefetch=1,
            grid=(rows // block,),
            in_specs=[
                tile_spec,
                pl.BlockSpec((block, depth), lambda i, place: (i, 0)),
                pl.BlockSpec((depth, cols), lambda i, place: (0, 0), pipeline_mode=pl.Buffered(1)),
                pl.BlockSpec((1, cols), lambda i, place: (0, 0)),
            ],
            out_specs=tile_spec,
        ),
        out_shape=jax.ShapeDtypeStruct((rows, cols), jnp.float32),
        compiler_params=pltpu.CompilerParams(vmem_limit_bytes=8 * 2**20),
        cost_estimate=pl.CostEstimate(
            flops=2 * rows * cols * depth, bytes_accessed=4 * rows * cols, transcendentals=0
        ),
        name="gram_tile",
    )(place, normals, left, right, regular)


def tile_kernel(system_ref, strip_ref, gram_ref, right_ref, inverse_ref, out_ref):
    panel = split_dot(strip_ref[...] + gram_ref[...], inverse_ref[...])
    high, low = split(panel)
    left = jnp.concatenate([high, high, low], axis=1)
    out_ref[...] = system_ref[...] + jnp.dot(left, right_ref[...], preferred_element_type=jnp.float32)


def tile_rows(system, strip, gram_cols, right, inverse):
    rows, cols = system.shape
    block = block_rows(rows // 2)
    tile_spec = pl.BlockSpec((block, cols), lambda i: (i, 0))
    lead_spec = pl.BlockSpec((block, B), lambda i: (i, 0))
    return pl.pallas_call(
        tile_kernel,
        grid=(rows // block,),
        in_specs=[
            tile_spec,
            lead_spec,
            lead_spec,
            pl.BlockSpec(right.shape, lambda i: (0, 0), pipeline_mode=pl.Buffered(1)),
            pl.BlockSpec(inverse.shape, lambda i: (0, 0), pipeline_mode=pl.Buffered(1)),
        ],
        out_specs=tile_spec,
        out_shape=jax.ShapeDtypeStruct((rows, cols), jnp.float32),
        compiler_params=pltpu.CompilerParams(vmem_limit_bytes=22 * 2**20),
        cost_estimate=pl.CostEstimate(
            flops=6 * rows * cols * B, bytes_accessed=4 * rows * cols, transcendentals=0
        ),
        name="tile_rows",
    )(system, strip, gram_cols, right, inverse)


def after(value, earlier):
    return lax.optimization_barrier((value, earlier))[0]


def shifted(value, axis, by):
    peers = lax.axis_size(axis)
    return lax.ppermute(value, axis, [(i, (i + by) % peers) for i in range(peers)])


def filter_matrix_of(filter_blocks, sources):
    count = sources.shape[0]
    lag = jnp.arange(count, dtype=jnp.int32)[:, None] - sources[None, :]
    lag = lag[:, None, :, None]
    own = filter_blocks[0][None, :, None, :]
    prior = filter_blocks[1][None, :, None, :]
    blocks = jnp.where(lag == 0, own, jnp.where(lag == 1, prior, 0.0))
    return blocks.reshape(count * P_SIZE, count * P_SIZE)


def row_strip_piece(normals):
    peers = lax.axis_size("col")
    chips = peers // 2
    size = normals.shape[0] // chips
    col_index = lax.axis_index("col")
    arrived = None
    for z in reversed(range(1, chips)):
        got = lax.ppermute(normals[z * size : (z + 1) * size, :B], "col", [(0, 2 * z)])
        arrived = got if arrived is None else arrived + got
    piece = jnp.where(col_index == 0, normals[:size, :B], arrived)
    second = lax.ppermute(piece[size // 2 :], "col", [(c, c + 1) for c in range(0, peers, 2)])
    return jnp.where(col_index % 2 == 0, piece[: size // 2], second)


def doubled(value, bits, reached):
    row_peers, col_peers = lax.axis_size("row"), lax.axis_size("col")
    here = lax.axis_index("row") * col_peers + lax.axis_index("col")
    for bit in bits:
        pairs = [(i, i | bit) for i in reached if i | bit < row_peers * col_peers]
        got = lax.ppermute(value, ("row", "col"), pairs)
        value = jnp.where((here & bit) != 0, got, value)
        reached = reached + [to for _, to in pairs]
    return value, reached


def body(normals, design, filter_blocks, regular):
    rows_here, cols_here = normals.shape
    obs_here = design.shape[0]
    row_peers = lax.axis_size("row")
    row_index = lax.axis_index("row")
    col_index = lax.axis_index("col")
    blocks_here = obs_here // P_SIZE
    obs = row_peers * obs_here
    core = col_index % 2

    col_peers = lax.axis_size("col")
    piece = row_strip_piece(normals)
    strip = lax.all_gather(piece, "col", axis=0, tiled=True)

    index_bits = [1 << i for i in range((row_peers * col_peers - 1).bit_length())]
    block, reached = doubled(normals[:B, :B], [bit for bit in index_bits if bit >= col_peers], [0])
    block = after(block, piece)
    corner, _ = doubled(block, [bit for bit in reversed(index_bits) if bit < col_peers], reached)

    col_strip = lax.psum(jnp.where(row_index == 0, normals[:B], 0.0), "row")

    along = lax.all_gather(design, "col", axis=1, tiled=True)
    parts = []
    for s in range(row_peers):
        to = (row_index + s) % row_peers
        far = lax.dynamic_slice_in_dim(along, to * rows_here + core * cols_here, cols_here, axis=1)
        part = jnp.concatenate([design, far, along[:, :B]], axis=1)
        parts.append(shifted(part, "row", s) if s else part)
    own = jnp.concatenate([part[:, cols_here : 2 * cols_here] for part in parts], axis=0)
    other = lax.ppermute(own, "col", [(c, c ^ 1) for c in range(lax.axis_size("col"))])
    lead = jnp.concatenate([part[:, 2 * cols_here :] for part in parts], axis=0)

    positions = jnp.arange(obs // P_SIZE, dtype=jnp.int32)
    passed = positions // blocks_here
    order = ((row_index - passed) % row_peers) * blocks_here + positions % blocks_here
    filters = filter_matrix_of(filter_blocks, order)
    lead_reg = regular[:B].reshape(1, B)
    own_reg = lax.dynamic_slice_in_dim(regular, col_index * cols_here, cols_here).reshape(1, cols_here)
    place = jnp.stack([row_index, col_index]).astype(jnp.int32)
    inverse = corner_factor(corner, lead, filters, lead_reg)
    gram_left, gram_right, gram_rows, gram_cols = filter_sides(place, parts, other, filters, own_reg, lead_reg)
    system = gram_tile(place, normals, gram_left, gram_right, own_reg)
    right = right_side(place, col_strip, gram_rows, inverse)
    return tile_rows(system, strip, gram_cols, right, inverse)


def solution(mesh):
    in_specs = (P("row", "col"), P("row", "col"), P(), P())
    out_specs = P("row", "col")
    return jax.shard_map(body, mesh=mesh, in_specs=in_specs, out_specs=out_specs, check_vma=False)
```

```python
import functools

import jax
import jax.numpy as jnp
from jax import lax
from jax.experimental import pallas as pl
from jax.experimental.pallas import tpu as pltpu
from jax.sharding import PartitionSpec as P

B = 256
P_SIZE = 32
STRIP = 32
PIVOTS = 4
HIGHEST = lax.Precision.HIGHEST


def exact_dot(left, right, left_dim, right_dim):
    return lax.dot_general(
        left,
        right,
        (((left_dim,), (right_dim,)), ((), ())),
        precision=HIGHEST,
        preferred_element_type=jnp.float32,
    )


def split(value):
    high = value.astype(jnp.bfloat16)
    low = (value - high.astype(jnp.float32)).astype(jnp.bfloat16)
    return high, low


def split_dot(left, right):
    left_high, left_low = split(left)
    right_high, right_low = split(right)
    wide = functools.partial(jnp.dot, preferred_element_type=jnp.float32)
    return wide(left_high, right_high) + (wide(left_high, right_low) + wide(left_low, right_high))


def corner_kernel(block_ref, design_ref, filter_ref, regular_ref, inverse_ref, upper):
    filtered = exact_dot(filter_ref[...], design_ref[...], 1, 0)
    row_pos = lax.broadcasted_iota(jnp.int32, (B, B), 0)
    col_pos = lax.broadcasted_iota(jnp.int32, (B, B), 1)
    system = block_ref[...] + exact_dot(filtered, filtered, 0, 0)
    system = system + jnp.where(row_pos == col_pos, regular_ref[...], 0.0)
    identity = jnp.where(row_pos == col_pos, 1.0, 0.0)
    half = B // 2
    sub = lax.broadcasted_iota(jnp.int32, (STRIP, half), 0)
    lane = lax.broadcasted_iota(jnp.int32, (STRIP, half), 1)
    zero = jnp.zeros((STRIP, half), jnp.float32)
    for start in range(0, B, STRIP):
        rows = slice(start, start + STRIP)
        strip = jnp.concatenate([system[rows, :], identity[rows, :]], axis=1)
        if start:
            done = upper[:start, :]
            strip = strip - exact_dot(done[:, rows], done, 0, 0)
        low = 0 if start < half else half
        held = [strip[:, at : at + half] for at in range(low, low + 3 * half, half)]
        for first in range(0, STRIP, PIVOTS):
            at = start + first - low
            columns = [
                jnp.broadcast_to(held[0][:, at + q : at + q + 1], (STRIP, half)) for q in range(PIVOTS)
            ]
            pivot_rows = [[part[first + q : first + q + 1, :] for part in held] for q in range(PIVOTS)]
            for q in range(PIVOTS):
                j = first + q
                coef = jnp.where(sub > j, columns[q] * (1.0 / columns[q][j : j + 1, :]), 0.0)
                for m in range(q + 1, PIVOTS):
                    columns[m] = columns[m] - coef * columns[m][j : j + 1, :]
                    scale = coef[first + m : first + m + 1, :]
                    pivot_rows[m] = [
                        row - scale * other for row, other in zip(pivot_rows[m], pivot_rows[q])
                    ]
                held = [part - coef * row for part, row in zip(held, pivot_rows[q])]
        diag = jnp.sum(jnp.where(lane == sub + (start - low), held[0], 0.0), axis=1, keepdims=True)
        held = [part / jnp.sqrt(diag) for part in held]
        upper[rows, :] = jnp.concatenate([*held, zero] if low == 0 else [zero, *held], axis=1)
    inverse_ref[...] = upper[:, B:].T


def corner_factor(block, design, filter_matrix, regular):
    return pl.pallas_call(
        corner_kernel,
        out_shape=jax.ShapeDtypeStruct((B, B), jnp.float32),
        scratch_shapes=[pltpu.VMEM((B, 2 * B), jnp.float32)],
        compiler_params=pltpu.CompilerParams(vmem_limit_bytes=8 * 2**20),
        cost_estimate=pl.CostEstimate(flops=10**9, bytes_accessed=2**20, transcendentals=0),
        name="corner_factor",
    )(block, design, filter_matrix, regular)


def right_kernel(place_ref, strip_ref, gram_ref, inverse_ref, out_ref):
    strip = strip_ref[...] + gram_ref[...]
    panel_high, panel_low = split(-split_dot(inverse_ref[...].T, strip))
    out_ref[:B, :] = panel_high
    out_ref[B : 2 * B, :] = panel_low
    out_ref[2 * B :, :] = panel_high

    @pl.when(place_ref[1] == 0)
    def _():
        row_pos = lax.broadcasted_iota(jnp.int32, (B, B), 0)
        identity = jnp.where(row_pos == lax.broadcasted_iota(jnp.int32, (B, B), 1), 1.0, 0.0)
        identity = identity.astype(jnp.bfloat16)
        out_ref[:B, :B] = identity
        out_ref[B : 2 * B, :B] = jnp.zeros((B, B), jnp.bfloat16)
        out_ref[2 * B :, :B] = identity


def right_side(place, strip, gram_rows, inverse):
    cols = gram_rows.shape[1]
    return pl.pallas_call(
        right_kernel,
        in_specs=[pl.BlockSpec(memory_space=pltpu.SMEM)] + [pl.BlockSpec(memory_space=pltpu.VMEM)] * 3,
        out_specs=pl.BlockSpec(memory_space=pltpu.VMEM),
        out_shape=jax.ShapeDtypeStruct((3 * B, cols), jnp.bfloat16),
        compiler_params=pltpu.CompilerParams(vmem_limit_bytes=24 * 2**20),
        cost_estimate=pl.CostEstimate(
            flops=6 * cols * B * B, bytes_accessed=12 * cols * B, transcendentals=0
        ),
        name="right_side",
    )(place, strip, gram_rows, inverse)


def filter_kernel(
    place_ref,
    joined_ref,
    other_ref,
    filter_ref,
    regular_ref,
    lead_reg_ref,
    left_ref,
    right_ref,
    gram_rows_ref,
    gram_cols_ref,
):
    row_index, col_index = place_ref[0], place_ref[1]
    cols = right_ref.shape[1]
    obs = filter_ref.shape[0]
    core = lax.rem(col_index, 2)
    filtered = split_dot(filter_ref[...], joined_ref[...])
    here, rows_own, lead = filtered[:, :cols], filtered[:, cols : 2 * cols], filtered[:, 2 * cols :]
    row_pos = lax.broadcasted_iota(jnp.int32, (B, cols), 0)
    col_pos = lax.broadcasted_iota(jnp.int32, (1, cols), 1) + col_index * cols
    gram_rows_ref[...] = split_dot(lead.T, here) + jnp.where(row_pos == col_pos, regular_ref[...], 0.0)
    high, low = split(jnp.where(col_pos < B, 0.0, here))
    right_ref[:obs, :] = high
    right_ref[obs : 2 * obs, :] = low
    right_ref[2 * obs :, :] = high
    rows_other = split_dot(filter_ref[...], other_ref[...])
    for half, value in ((core, rows_own), (1 - core, rows_other)):
        value = value.T
        high, low = split(value)
        rows = pl.ds(pl.multiple_of(half * cols, cols), cols)
        left_ref[rows, :obs] = high
        left_ref[rows, obs : 2 * obs] = high
        left_ref[rows, 2 * obs :] = low
        row_pos = lax.broadcasted_iota(jnp.int32, (cols, B), 0) + (2 * row_index + half) * cols
        lead_pos = lax.broadcasted_iota(jnp.int32, (cols, B), 1)
        gram_cols_ref[rows, :] = split_dot(value, lead) + jnp.where(
            row_pos == lead_pos, lead_reg_ref[...], 0.0
        )


def filter_sides(place, joined, other, filter_matrix, regular, lead_reg):
    cols = other.shape[1]
    obs = filter_matrix.shape[0]
    vmem = pl.BlockSpec(memory_space=pltpu.VMEM)
    return pl.pallas_call(
        filter_kernel,
        in_specs=[pl.BlockSpec(memory_space=pltpu.SMEM)] + [vmem] * 5,
        out_specs=[vmem] * 4,
        out_shape=[
            jax.ShapeDtypeStruct((2 * cols, 3 * obs), jnp.bfloat16),
            jax.ShapeDtypeStruct((3 * obs, cols), jnp.bfloat16),
            jax.ShapeDtypeStruct((B, cols), jnp.float32),
            jax.ShapeDtypeStruct((2 * cols, B), jnp.float32),
        ],
        compiler_params=pltpu.CompilerParams(vmem_limit_bytes=32 * 2**20),
        cost_estimate=pl.CostEstimate(
            flops=18 * cols * obs * B, bytes_accessed=24 * cols * B, transcendentals=0
        ),
        name="filter_sides",
    )(place, joined, other, filter_matrix, regular, lead_reg)


def gram_kernel(place_ref, normals_ref, left_ref, right_ref, regular_ref, out_ref):
    step = pl.program_id(0)
    block, cols = out_ref.shape
    first_col = place_ref[1] * cols
    col_pos = lax.broadcasted_iota(jnp.int32, (1, cols), 1) + first_col
    keep = jnp.where(col_pos < B, 0.0, 1.0)
    out_ref[...] = normals_ref[...] * keep + jnp.dot(
        left_ref[...], right_ref[...], preferred_element_type=jnp.float32
    )
    first_row = (place_ref[0] * pl.num_programs(0) + step) * block

    @pl.when((first_row < first_col + cols) & (first_col < first_row + block))
    def _():
        row_pos = lax.broadcasted_iota(jnp.int32, (block, cols), 0) + first_row
        on_diag = (row_pos == col_pos) & (col_pos >= B)
        out_ref[...] = out_ref[...] + jnp.where(on_diag, regular_ref[...], 0.0)


def block_rows(half):
    return max(size for size in range(128, 513, 128) if half % size == 0)


def gram_tile(place, normals, left, right, regular):
    rows, cols = normals.shape
    block = block_rows(rows // 2)
    depth = right.shape[0]
    tile_spec = pl.BlockSpec((block, cols), lambda i, place: (i, 0))
    return pl.pallas_call(
        gram_kernel,
        grid_spec=pltpu.PrefetchScalarGridSpec(
            num_scalar_prefetch=1,
            grid=(rows // block,),
            in_specs=[
                tile_spec,
                pl.BlockSpec((block, depth), lambda i, place: (i, 0)),
                pl.BlockSpec((depth, cols), lambda i, place: (0, 0), pipeline_mode=pl.Buffered(1)),
                pl.BlockSpec((1, cols), lambda i, place: (0, 0)),
            ],
            out_specs=tile_spec,
        ),
        out_shape=pltpu.HBM((rows, cols), jnp.float32),
        compiler_params=pltpu.CompilerParams(vmem_limit_bytes=16 * 2**20),
        cost_estimate=pl.CostEstimate(
            flops=2 * rows * cols * depth, bytes_accessed=4 * rows * cols, transcendentals=0
        ),
        name="gram_tile",
    )(place, normals, left, right, regular)


def tile_kernel(system_ref, strip_ref, gram_ref, right_ref, inverse_ref, out_ref):
    panel = split_dot(strip_ref[...] + gram_ref[...], inverse_ref[...])
    high, low = split(panel)
    left = jnp.concatenate([high, high, low], axis=1)
    out_ref[...] = system_ref[...] + jnp.dot(left, right_ref[...], preferred_element_type=jnp.float32)


def tile_rows(system, strip, gram_cols, right, inverse):
    rows, cols = system.shape
    block = block_rows(rows // 2)
    tile_spec = pl.BlockSpec((block, cols), lambda i: (i, 0))
    lead_spec = pl.BlockSpec((block, B), lambda i: (i, 0))
    return pl.pallas_call(
        tile_kernel,
        grid=(rows // block,),
        in_specs=[
            tile_spec,
            lead_spec,
            lead_spec,
            pl.BlockSpec(right.shape, lambda i: (0, 0), pipeline_mode=pl.Buffered(1)),
            pl.BlockSpec(inverse.shape, lambda i: (0, 0), pipeline_mode=pl.Buffered(1)),
        ],
        out_specs=tile_spec,
        out_shape=jax.ShapeDtypeStruct((rows, cols), jnp.float32),
        compiler_params=pltpu.CompilerParams(vmem_limit_bytes=32 * 2**20),
        cost_estimate=pl.CostEstimate(
            flops=6 * rows * cols * B, bytes_accessed=4 * rows * cols, transcendentals=0
        ),
        name="tile_rows",
    )(system, strip, gram_cols, right, inverse)


def after(value, earlier):
    return lax.optimization_barrier((value, earlier))[0]


def filter_matrix_of(filter_blocks, count):
    positions = jnp.arange(count, dtype=jnp.int32)
    lag = (positions[:, None] - positions[None, :])[:, None, :, None]
    own = filter_blocks[0][None, :, None, :]
    prior = filter_blocks[1][None, :, None, :]
    blocks = jnp.where(lag == 0, own, jnp.where(lag == 1, prior, 0.0))
    return blocks.reshape(count * P_SIZE, count * P_SIZE)


def row_strip_piece(normals, earlier):
    peers = lax.axis_size("col")
    chips = peers // 2
    size = normals.shape[0] // chips
    col_index = lax.axis_index("col")
    arrived = [
        lax.ppermute(normals[z * size : (z + 1) * size, :B], "col", [(0, 2 * z)]) for z in range(1, chips)
    ]
    arrived = sum(after(arrived, earlier))
    piece = jnp.where(col_index == 0, normals[:size, :B], arrived)
    second = lax.ppermute(piece[size // 2 :], "col", [(c, c + 1) for c in range(0, peers, 2)])
    return jnp.where(col_index % 2 == 0, piece[: size // 2], second)


def doubled(value, bits, reached):
    row_peers, col_peers = lax.axis_size("row"), lax.axis_size("col")
    here = lax.axis_index("row") * col_peers + lax.axis_index("col")
    for bit in bits:
        pairs = [(i, i | bit) for i in reached if i | bit < row_peers * col_peers]
        got = lax.ppermute(value, ("row", "col"), pairs)
        value = jnp.where((here & bit) != 0, got, value)
        reached = reached + [to for _, to in pairs]
    return value, reached


def body(normals, design, filter_blocks, regular):
    rows_here, cols_here = normals.shape
    obs_here = design.shape[0]
    row_peers = lax.axis_size("row")
    row_index = lax.axis_index("row")
    col_index = lax.axis_index("col")
    obs = row_peers * obs_here
    core = col_index % 2

    col_peers = lax.axis_size("col")
    col_strip = lax.psum(jnp.where(row_index == 0, normals[:B], 0.0), "row")

    index_bits = [1 << i for i in range((row_peers * col_peers - 1).bit_length())]
    block, reached = doubled(normals[:B, :B], [bit for bit in index_bits if bit >= col_peers], [0])

    along = lax.all_gather(design, "col", axis=1, tiled=True)
    along = along.reshape(obs_here, row_peers, 2, cols_here)
    far = lax.dynamic_index_in_dim(along, core, 2, keepdims=False)
    sent = [
        jnp.concatenate([design, far[:, to], along[:, 0, 0, :B]], axis=1) for to in range(row_peers)
    ]
    joined = lax.all_to_all(jnp.stack(sent), "row", 0, 0, tiled=True)
    joined = joined.reshape(obs, 2 * cols_here + B)

    piece = row_strip_piece(normals, (block, joined))
    strip = lax.all_gather(piece, "col", axis=0, tiled=True)

    corner, _ = doubled(after(block, piece), [bit for bit in reversed(index_bits) if bit < col_peers], reached)

    other = lax.ppermute(
        joined[:, cols_here : 2 * cols_here], "col", [(c, c ^ 1) for c in range(col_peers)]
    )
    lead = joined[:, 2 * cols_here :]
    filters = filter_matrix_of(filter_blocks, obs // P_SIZE)
    lead_reg = regular[:B].reshape(1, B)
    own_reg = lax.dynamic_slice_in_dim(regular, col_index * cols_here, cols_here).reshape(1, cols_here)
    place = jnp.stack([row_index, col_index]).astype(jnp.int32)
    inverse = corner_factor(corner, lead, filters, lead_reg)
    gram_left, gram_right, gram_rows, gram_cols = filter_sides(place, joined, other, filters, own_reg, lead_reg)
    in_hbm = functools.partial(pltpu.with_memory_space_constraint, memory_space=pltpu.HBM)
    system = gram_tile(place, in_hbm(normals), gram_left, gram_right, own_reg)
    right = right_side(place, col_strip, gram_rows, inverse)
    return tile_rows(in_hbm(system), strip, gram_cols, right, inverse)


def solution(mesh):
    in_specs = (P("row", "col"), P("row", "col"), P(), P())
    out_specs = P("row", "col")
    return jax.shard_map(body, mesh=mesh, in_specs=in_specs, out_specs=out_specs, check_vma=False)
```

```python
import functools

import jax
import jax.numpy as jnp
from jax import lax
from jax.experimental import pallas as pl
from jax.experimental.pallas import tpu as pltpu
from jax.sharding import PartitionSpec as P

B = 256
P_SIZE = 32
STRIP = 32
PIVOTS = 4
HIGHEST = lax.Precision.HIGHEST


def exact_dot(left, right, left_dim, right_dim):
    return lax.dot_general(
        left,
        right,
        (((left_dim,), (right_dim,)), ((), ())),
        precision=HIGHEST,
        preferred_element_type=jnp.float32,
    )


def split(value):
    high = value.astype(jnp.bfloat16)
    low = (value - high.astype(jnp.float32)).astype(jnp.bfloat16)
    return high, low


def split_dot(left, right):
    left_high, left_low = split(left)
    right_high, right_low = split(right)
    wide = functools.partial(jnp.dot, preferred_element_type=jnp.float32)
    return wide(left_high, right_high) + (wide(left_high, right_low) + wide(left_low, right_high))


def corner_kernel(block_ref, design_ref, filter_ref, regular_ref, inverse_ref, upper):
    filtered = exact_dot(filter_ref[...], design_ref[...], 1, 0)
    row_pos = lax.broadcasted_iota(jnp.int32, (B, B), 0)
    col_pos = lax.broadcasted_iota(jnp.int32, (B, B), 1)
    system = block_ref[...] + exact_dot(filtered, filtered, 0, 0)
    system = system + jnp.where(row_pos == col_pos, regular_ref[...], 0.0)
    identity = jnp.where(row_pos == col_pos, 1.0, 0.0)
    half = B // 2
    sub = lax.broadcasted_iota(jnp.int32, (STRIP, half), 0)
    lane = lax.broadcasted_iota(jnp.int32, (STRIP, half), 1)
    zero = jnp.zeros((STRIP, half), jnp.float32)
    for start in range(0, B, STRIP):
        rows = slice(start, start + STRIP)
        strip = jnp.concatenate([system[rows, :], identity[rows, :]], axis=1)
        if start:
            done = upper[:start, :]
            strip = strip - exact_dot(done[:, rows], done, 0, 0)
        low = 0 if start < half else half
        held = [strip[:, at : at + half] for at in range(low, low + 3 * half, half)]
        for first in range(0, STRIP, PIVOTS):
            at = start + first - low
            columns = [
                jnp.broadcast_to(held[0][:, at + q : at + q + 1], (STRIP, half)) for q in range(PIVOTS)
            ]
            pivot_rows = [[part[first + q : first + q + 1, :] for part in held] for q in range(PIVOTS)]
            for q in range(PIVOTS):
                j = first + q
                coef = jnp.where(sub > j, columns[q] * (1.0 / columns[q][j : j + 1, :]), 0.0)
                for m in range(q + 1, PIVOTS):
                    columns[m] = columns[m] - coef * columns[m][j : j + 1, :]
                    scale = coef[first + m : first + m + 1, :]
                    pivot_rows[m] = [
                        row - scale * other for row, other in zip(pivot_rows[m], pivot_rows[q])
                    ]
                held = [part - coef * row for part, row in zip(held, pivot_rows[q])]
        diag = jnp.sum(jnp.where(lane == sub + (start - low), held[0], 0.0), axis=1, keepdims=True)
        held = [part / jnp.sqrt(diag) for part in held]
        upper[rows, :] = jnp.concatenate([*held, zero] if low == 0 else [zero, *held], axis=1)
    inverse_ref[...] = upper[:, B:].T


def corner_factor(block, design, filter_matrix, regular):
    return pl.pallas_call(
        corner_kernel,
        out_shape=jax.ShapeDtypeStruct((B, B), jnp.float32),
        scratch_shapes=[pltpu.VMEM((B, 2 * B), jnp.float32)],
        compiler_params=pltpu.CompilerParams(vmem_limit_bytes=8 * 2**20),
        cost_estimate=pl.CostEstimate(flops=10**9, bytes_accessed=2**20, transcendentals=0),
        name="corner_factor",
    )(block, design, filter_matrix, regular)


def right_kernel(place_ref, strip_ref, gram_ref, inverse_ref, side_ref, out_ref):
    strip = strip_ref[...] + gram_ref[...]
    panel_high, panel_low = split(-split_dot(inverse_ref[...].T, strip))
    out_ref[:B, :] = panel_high
    out_ref[B : 2 * B, :] = panel_low
    out_ref[2 * B : 3 * B, :] = panel_high
    out_ref[3 * B :, :] = side_ref[...]

    @pl.when(place_ref[1] == 0)
    def _():
        row_pos = lax.broadcasted_iota(jnp.int32, (B, B), 0)
        identity = jnp.where(row_pos == lax.broadcasted_iota(jnp.int32, (B, B), 1), 1.0, 0.0)
        identity = identity.astype(jnp.bfloat16)
        out_ref[:B, :B] = identity
        out_ref[B : 2 * B, :B] = jnp.zeros((B, B), jnp.bfloat16)
        out_ref[2 * B : 3 * B, :B] = identity


def right_side(place, strip, gram_rows, inverse, side):
    cols = gram_rows.shape[1]
    depth = 3 * B + side.shape[0]
    return pl.pallas_call(
        right_kernel,
        in_specs=[pl.BlockSpec(memory_space=pltpu.SMEM)] + [pl.BlockSpec(memory_space=pltpu.VMEM)] * 4,
        out_specs=pl.BlockSpec(memory_space=pltpu.VMEM),
        out_shape=jax.ShapeDtypeStruct((depth, cols), jnp.bfloat16),
        compiler_params=pltpu.CompilerParams(vmem_limit_bytes=24 * 2**20),
        cost_estimate=pl.CostEstimate(
            flops=6 * cols * B * B, bytes_accessed=12 * cols * B, transcendentals=0
        ),
        name="right_side",
    )(place, strip, gram_rows, inverse, side)


def filter_kernel(
    place_ref,
    joined_ref,
    other_ref,
    filter_ref,
    regular_ref,
    lead_reg_ref,
    left_ref,
    right_ref,
    gram_rows_ref,
    gram_cols_ref,
):
    row_index, col_index = place_ref[0], place_ref[1]
    cols = right_ref.shape[1]
    obs = filter_ref.shape[0]
    core = lax.rem(col_index, 2)
    filtered = split_dot(filter_ref[...], joined_ref[...])
    here, rows_own, lead = filtered[:, :cols], filtered[:, cols : 2 * cols], filtered[:, 2 * cols :]
    row_pos = lax.broadcasted_iota(jnp.int32, (B, cols), 0)
    col_pos = lax.broadcasted_iota(jnp.int32, (1, cols), 1) + col_index * cols
    gram_rows_ref[...] = split_dot(lead.T, here) + jnp.where(row_pos == col_pos, regular_ref[...], 0.0)
    high, low = split(jnp.where(col_pos < B, 0.0, here))
    right_ref[:obs, :] = high
    right_ref[obs : 2 * obs, :] = low
    right_ref[2 * obs :, :] = high
    rows_other = split_dot(filter_ref[...], other_ref[...])
    for half, value in ((core, rows_own), (1 - core, rows_other)):
        value = value.T
        high, low = split(value)
        rows = pl.ds(pl.multiple_of(half * cols, cols), cols)
        left_ref[rows, :obs] = high
        left_ref[rows, obs : 2 * obs] = high
        left_ref[rows, 2 * obs :] = low
        row_pos = lax.broadcasted_iota(jnp.int32, (cols, B), 0) + (2 * row_index + half) * cols
        lead_pos = lax.broadcasted_iota(jnp.int32, (cols, B), 1)
        gram_cols_ref[rows, :] = split_dot(value, lead) + jnp.where(
            row_pos == lead_pos, lead_reg_ref[...], 0.0
        )


def filter_sides(place, joined, other, filter_matrix, regular, lead_reg):
    cols = other.shape[1]
    obs = filter_matrix.shape[0]
    vmem = pl.BlockSpec(memory_space=pltpu.VMEM)
    return pl.pallas_call(
        filter_kernel,
        in_specs=[pl.BlockSpec(memory_space=pltpu.SMEM)] + [vmem] * 5,
        out_specs=[vmem] * 4,
        out_shape=[
            jax.ShapeDtypeStruct((2 * cols, 3 * obs), jnp.bfloat16),
            jax.ShapeDtypeStruct((3 * obs, cols), jnp.bfloat16),
            jax.ShapeDtypeStruct((B, cols), jnp.float32),
            jax.ShapeDtypeStruct((2 * cols, B), jnp.float32),
        ],
        compiler_params=pltpu.CompilerParams(vmem_limit_bytes=32 * 2**20),
        cost_estimate=pl.CostEstimate(
            flops=18 * cols * obs * B, bytes_accessed=24 * cols * B, transcendentals=0
        ),
        name="filter_sides",
    )(place, joined, other, filter_matrix, regular, lead_reg)


def block_rows(half):
    return max(size for size in range(128, 513, 128) if half % size == 0)


def tile_kernel(count, block_ids_ref, place_ref, normals_ref, *refs):
    here_refs, sent_refs = refs[:count], refs[count : 2 * count]
    gram_ref, left_ref, right_ref, inverse_ref, regular_ref, out_ref = refs[2 * count :]
    step = pl.program_id(0)
    block, cols = out_ref.shape
    per_piece = pl.num_programs(0) // count
    even = lax.rem(place_ref[1], 2) == 0
    slot = step // per_piece
    rows = pl.ds(pl.multiple_of(lax.rem(step, per_piece) * block, block), block)
    strip = jnp.where(even, here_refs[0][rows, :], sent_refs[0][rows, :])
    for i in range(1, count):
        strip = jnp.where(slot == i, jnp.where(even, here_refs[i][rows, :], sent_refs[i][rows, :]), strip)
    high, low = split(split_dot(strip + gram_ref[...], inverse_ref[...]))
    left = jnp.concatenate([high, high, low, left_ref[...]], axis=1)
    first_row = (place_ref[0] * pl.num_programs(0) + block_ids_ref[step]) * block
    first_col = place_ref[1] * cols
    col_pos = lax.broadcasted_iota(jnp.int32, (1, cols), 1) + first_col
    keep = jnp.where(col_pos < B, 0.0, 1.0)
    out_ref[...] = normals_ref[...] * keep + jnp.dot(
        left, right_ref[...], preferred_element_type=jnp.float32
    )

    @pl.when((first_row < first_col + cols) & (first_col < first_row + block))
    def _():
        row_pos = lax.broadcasted_iota(jnp.int32, (block, cols), 0) + first_row
        on_diag = (row_pos == col_pos) & (col_pos >= B)
        out_ref[...] = out_ref[...] + jnp.where(on_diag, regular_ref[...], 0.0)


def tile_rows(place, block_ids, normals, here, sent, gram_cols, left, right, inverse, regular):
    rows, cols = normals.shape
    count = len(here)
    block = rows // block_ids.shape[0]

    def whole(array):
        return pl.BlockSpec(
            array.shape, lambda i, ids, place: (0,) * array.ndim, pipeline_mode=pl.Buffered(1)
        )

    def listed(width):
        return pl.BlockSpec((block, width), lambda i, ids, place: (ids[i], 0))

    return pl.pallas_call(
        functools.partial(tile_kernel, count),
        grid_spec=pltpu.PrefetchScalarGridSpec(
            num_scalar_prefetch=2,
            grid=(block_ids.shape[0],),
            in_specs=[listed(cols)]
            + [whole(array) for array in [*here, *sent]]
            + [listed(B), listed(left.shape[1]), whole(right), whole(inverse), whole(regular)],
            out_specs=listed(cols),
        ),
        out_shape=jax.ShapeDtypeStruct((rows, cols), jnp.float32),
        compiler_params=pltpu.CompilerParams(vmem_limit_bytes=40 * 2**20),
        cost_estimate=pl.CostEstimate(
            flops=2 * rows * cols * right.shape[0], bytes_accessed=8 * rows * cols, transcendentals=0
        ),
        name="tile_rows",
    )(block_ids, place, normals, *here, *sent, gram_cols, left, right, inverse, regular)


def after(value, earlier):
    return lax.optimization_barrier((value, earlier))[0]


def filter_matrix_of(filter_blocks, count):
    positions = jnp.arange(count, dtype=jnp.int32)
    lag = (positions[:, None] - positions[None, :])[:, None, :, None]
    own = filter_blocks[0][None, :, None, :]
    prior = filter_blocks[1][None, :, None, :]
    blocks = jnp.where(lag == 0, own, jnp.where(lag == 1, prior, 0.0))
    return blocks.reshape(count * P_SIZE, count * P_SIZE)


def to_odd_core(value):
    return lax.ppermute(value, "col", [(c, c + 1) for c in range(0, lax.axis_size("col"), 2)])


def row_strip(normals, earlier, later):
    peers = lax.axis_size("col")
    chips = peers // 2
    rows = normals.shape[0]
    col_index = lax.axis_index("col")
    chip = col_index // 2
    if chips > 4:
        size = rows // chips
        share = normals[:size, :B]
        for z in range(1, chips):
            got = lax.ppermute(normals[z * size : (z + 1) * size, :B], "col", [(0, 2 * z)])
            share = jnp.where(chip == z, got, share)
        cores = [list(range(k, peers, 2)) for k in range(2)]
        return [(jnp.int32(0), lax.all_gather(share, "col", axis=0, tiled=True, axis_index_groups=cores))]
    count = chips - 1
    size = rows // count
    local = after([normals[i * size : (i + 1) * size, :B] for i in range(count)], earlier)
    arrived = [lax.ppermute(value, "col", [(0, 2 * (1 + i))]) for i, value in enumerate(local)]
    arrived = sum(after(arrived, later))
    at_source = chip == 0
    mine = jnp.where(at_source, local[0], arrived)
    pieces = [(jnp.where(at_source, 0, chip - 1), mine)]
    for s in range(1, count):
        pairs = [(2 * (1 + i), 2 * (1 + (i + s) % count)) for i in range(count)]
        got = lax.ppermute(mine, "col", pairs)
        which = -s % count
        piece = jnp.where(at_source, local[which], got)
        pieces.append((jnp.where(at_source, which, (chip - 1 - s) % count), piece))
    return pieces


def doubled(value, bits, reached):
    row_peers, col_peers = lax.axis_size("row"), lax.axis_size("col")
    here = lax.axis_index("row") * col_peers + lax.axis_index("col")
    for bit in bits:
        pairs = [(i, i | bit) for i in reached if i | bit < row_peers * col_peers]
        got = lax.ppermute(value, ("row", "col"), pairs)
        value = jnp.where((here & bit) != 0, got, value)
        reached = reached + [to for _, to in pairs]
    return value, reached


def body(normals, design, filter_blocks, regular):
    rows_here, cols_here = normals.shape
    obs_here = design.shape[0]
    row_peers = lax.axis_size("row")
    row_index = lax.axis_index("row")
    col_index = lax.axis_index("col")
    obs = row_peers * obs_here
    core = col_index % 2

    col_peers = lax.axis_size("col")
    col_strip = lax.psum(jnp.where(row_index == 0, normals[:B], 0.0), "row")

    top = jnp.where(row_index == 0, normals[:B], 0.0)
    col_strip = lax.psum(top, "row")

    index_bits = [1 << i for i in range((row_peers * col_peers - 1).bit_length())]
    block, reached = doubled(normals[:B, :B], [bit for bit in index_bits if bit >= col_peers], [0])

    along = after(lax.all_gather(design, "col", axis=1, tiled=True), block)
    along = along.reshape(obs_here, row_peers, 2, cols_here)
    far = lax.dynamic_index_in_dim(along, core, 2, keepdims=False)
    sent = [
        jnp.concatenate([design, far[:, to], along[:, 0, 0, :B]], axis=1) for to in range(row_peers)
    ]
    sent = jnp.stack(sent)
    joined = lax.all_to_all(sent, "row", 0, 0, tiled=True)
    joined = joined.reshape(obs, 2 * cols_here + B)

    pieces = row_strip(normals, top, sent)
    here = [piece for _, piece in pieces]
    passed = [to_odd_core(piece) for piece in here]

    z_and_core = [bit for bit in reversed(index_bits) if bit < col_peers]
    corner, _ = doubled(after(block, here[0]), z_and_core, reached)

    other = lax.ppermute(
        joined[:, cols_here : 2 * cols_here], "col", [(c, c ^ 1) for c in range(col_peers)]
    )
    lead = joined[:, 2 * cols_here :]
    filters = filter_matrix_of(filter_blocks, obs // P_SIZE)
    lead_reg = regular[:B].reshape(1, B)
    own_reg = lax.dynamic_slice_in_dim(regular, col_index * cols_here, cols_here).reshape(1, cols_here)
    place = jnp.stack([row_index, col_index]).astype(jnp.int32)
    inverse = corner_factor(corner, lead, filters, lead_reg)
    gram_left, gram_right, gram_rows, gram_cols = filter_sides(place, joined, other, filters, own_reg, lead_reg)
    right = right_side(place, col_strip, gram_rows, inverse, gram_right)
    per_piece = here[0].shape[0] // block_rows(rows_here // 2)
    which = jnp.stack([index for index, _ in pieces])
    block_ids = which[:, None] * per_piece + jnp.arange(per_piece, dtype=jnp.int32)[None, :]
    block_ids = block_ids.reshape(-1).astype(jnp.int32)
    return tile_rows(
        place, block_ids, normals, here, passed, gram_cols, gram_left, right, inverse, own_reg
    )


def solution(mesh):
    in_specs = (P("row", "col"), P("row", "col"), P(), P())
    out_specs = P("row", "col")
    return jax.shard_map(body, mesh=mesh, in_specs=in_specs, out_specs=out_specs, check_vma=False)
```

```python
import functools

import jax
import jax.numpy as jnp
from jax import lax
from jax.experimental import pallas as pl
from jax.experimental.pallas import tpu as pltpu
from jax.sharding import PartitionSpec as P

B = 256
P_SIZE = 32
STRIP = 32
PIVOTS = 4
HIGHEST = lax.Precision.HIGHEST


def exact_dot(left, right, left_dim, right_dim):
    return lax.dot_general(
        left,
        right,
        (((left_dim,), (right_dim,)), ((), ())),
        precision=HIGHEST,
        preferred_element_type=jnp.float32,
    )


def split(value):
    high = value.astype(jnp.bfloat16)
    low = (value - high.astype(jnp.float32)).astype(jnp.bfloat16)
    return high, low


def split_dot(left, right):
    left_high, left_low = split(left)
    right_high, right_low = split(right)
    wide = functools.partial(jnp.dot, preferred_element_type=jnp.float32)
    return wide(left_high, right_high) + (wide(left_high, right_low) + wide(left_low, right_high))


def corner_kernel(block_ref, design_ref, filter_ref, regular_ref, inverse_ref, upper):
    filtered = exact_dot(filter_ref[...], design_ref[...], 1, 0)
    row_pos = lax.broadcasted_iota(jnp.int32, (B, B), 0)
    col_pos = lax.broadcasted_iota(jnp.int32, (B, B), 1)
    system = block_ref[...] + exact_dot(filtered, filtered, 0, 0)
    system = system + jnp.where(row_pos == col_pos, regular_ref[...], 0.0)
    identity = jnp.where(row_pos == col_pos, 1.0, 0.0)
    half = B // 2
    sub = lax.broadcasted_iota(jnp.int32, (STRIP, half), 0)
    lane = lax.broadcasted_iota(jnp.int32, (STRIP, half), 1)
    zero = jnp.zeros((STRIP, half), jnp.float32)
    for start in range(0, B, STRIP):
        rows = slice(start, start + STRIP)
        strip = jnp.concatenate([system[rows, :], identity[rows, :]], axis=1)
        if start:
            done = upper[:start, :]
            strip = strip - exact_dot(done[:, rows], done, 0, 0)
        low = 0 if start < half else half
        held = [strip[:, at : at + half] for at in range(low, low + 3 * half, half)]
        for first in range(0, STRIP, PIVOTS):
            at = start + first - low
            columns = [
                jnp.broadcast_to(held[0][:, at + q : at + q + 1], (STRIP, half)) for q in range(PIVOTS)
            ]
            pivot_rows = [[part[first + q : first + q + 1, :] for part in held] for q in range(PIVOTS)]
            for q in range(PIVOTS):
                j = first + q
                coef = jnp.where(sub > j, columns[q] * (1.0 / columns[q][j : j + 1, :]), 0.0)
                for m in range(q + 1, PIVOTS):
                    columns[m] = columns[m] - coef * columns[m][j : j + 1, :]
                    scale = coef[first + m : first + m + 1, :]
                    pivot_rows[m] = [
                        row - scale * other for row, other in zip(pivot_rows[m], pivot_rows[q])
                    ]
                held = [part - coef * row for part, row in zip(held, pivot_rows[q])]
        diag = jnp.sum(jnp.where(lane == sub + (start - low), held[0], 0.0), axis=1, keepdims=True)
        held = [part / jnp.sqrt(diag) for part in held]
        upper[rows, :] = jnp.concatenate([*held, zero] if low == 0 else [zero, *held], axis=1)
    inverse_ref[...] = upper[:, B:].T


def corner_factor(block, design, filter_matrix, regular):
    return pl.pallas_call(
        corner_kernel,
        out_shape=jax.ShapeDtypeStruct((B, B), jnp.float32),
        scratch_shapes=[pltpu.VMEM((B, 2 * B), jnp.float32)],
        compiler_params=pltpu.CompilerParams(vmem_limit_bytes=8 * 2**20),
        cost_estimate=pl.CostEstimate(flops=10**9, bytes_accessed=2**20, transcendentals=0),
        name="corner_factor",
    )(block, design, filter_matrix, regular)


def right_kernel(place_ref, strip_ref, gram_ref, inverse_ref, out_ref):
    strip = strip_ref[...] + gram_ref[...]
    panel_high, panel_low = split(-split_dot(inverse_ref[...].T, strip))
    out_ref[:B, :] = panel_high
    out_ref[B : 2 * B, :] = panel_low
    out_ref[2 * B :, :] = panel_high

    @pl.when(place_ref[1] == 0)
    def _():
        row_pos = lax.broadcasted_iota(jnp.int32, (B, B), 0)
        identity = jnp.where(row_pos == lax.broadcasted_iota(jnp.int32, (B, B), 1), 1.0, 0.0)
        identity = identity.astype(jnp.bfloat16)
        out_ref[:B, :B] = identity
        out_ref[B : 2 * B, :B] = jnp.zeros((B, B), jnp.bfloat16)
        out_ref[2 * B :, :B] = identity


def right_side(place, strip, gram_rows, inverse):
    cols = gram_rows.shape[1]
    return pl.pallas_call(
        right_kernel,
        in_specs=[pl.BlockSpec(memory_space=pltpu.SMEM)] + [pl.BlockSpec(memory_space=pltpu.VMEM)] * 3,
        out_specs=pl.BlockSpec(memory_space=pltpu.VMEM),
        out_shape=jax.ShapeDtypeStruct((3 * B, cols), jnp.bfloat16),
        compiler_params=pltpu.CompilerParams(vmem_limit_bytes=24 * 2**20),
        cost_estimate=pl.CostEstimate(
            flops=6 * cols * B * B, bytes_accessed=12 * cols * B, transcendentals=0
        ),
        name="right_side",
    )(place, strip, gram_rows, inverse)


def filter_kernel(
    place_ref,
    joined_ref,
    lead_ref,
    other_ref,
    filter_ref,
    regular_ref,
    lead_reg_ref,
    left_ref,
    right_ref,
    gram_rows_ref,
    gram_cols_ref,
):
    row_index, col_index = place_ref[0], place_ref[1]
    cols = right_ref.shape[1]
    obs = filter_ref.shape[0]
    core = lax.rem(col_index, 2)
    filtered = split_dot(filter_ref[...], joined_ref[:, : 2 * cols])
    here, rows_own = filtered[:, :cols], filtered[:, cols : 2 * cols]
    lead = split_dot(filter_ref[...], lead_ref[...])
    row_pos = lax.broadcasted_iota(jnp.int32, (B, cols), 0)
    col_pos = lax.broadcasted_iota(jnp.int32, (1, cols), 1) + col_index * cols
    gram_rows_ref[...] = split_dot(lead.T, here) + jnp.where(row_pos == col_pos, regular_ref[...], 0.0)
    high, low = split(jnp.where(col_pos < B, 0.0, here))
    right_ref[:obs, :] = high
    right_ref[obs : 2 * obs, :] = low
    right_ref[2 * obs :, :] = high
    rows_other = split_dot(filter_ref[...], other_ref[...])
    for half, value in ((core, rows_own), (1 - core, rows_other)):
        value = value.T
        high, low = split(value)
        rows = pl.ds(pl.multiple_of(half * cols, cols), cols)
        left_ref[rows, :obs] = high
        left_ref[rows, obs : 2 * obs] = high
        left_ref[rows, 2 * obs :] = low
        row_pos = lax.broadcasted_iota(jnp.int32, (cols, B), 0) + (2 * row_index + half) * cols
        lead_pos = lax.broadcasted_iota(jnp.int32, (cols, B), 1)
        gram_cols_ref[rows, :] = split_dot(value, lead) + jnp.where(
            row_pos == lead_pos, lead_reg_ref[...], 0.0
        )


def filter_sides(place, joined, lead, other, filter_matrix, regular, lead_reg):
    cols = other.shape[1]
    obs = filter_matrix.shape[0]
    vmem = pl.BlockSpec(memory_space=pltpu.VMEM)
    return pl.pallas_call(
        filter_kernel,
        in_specs=[pl.BlockSpec(memory_space=pltpu.SMEM)] + [vmem] * 6,
        out_specs=[vmem] * 4,
        out_shape=[
            jax.ShapeDtypeStruct((2 * cols, 3 * obs), jnp.bfloat16),
            jax.ShapeDtypeStruct((3 * obs, cols), jnp.bfloat16),
            jax.ShapeDtypeStruct((B, cols), jnp.float32),
            jax.ShapeDtypeStruct((2 * cols, B), jnp.float32),
        ],
        compiler_params=pltpu.CompilerParams(vmem_limit_bytes=32 * 2**20),
        cost_estimate=pl.CostEstimate(
            flops=18 * cols * obs * B, bytes_accessed=24 * cols * B, transcendentals=0
        ),
        name="filter_sides",
    )(place, joined, lead, other, filter_matrix, regular, lead_reg)


def gram_kernel(place_ref, normals_ref, left_ref, right_ref, regular_ref, out_ref):
    step = pl.program_id(0)
    block, cols = out_ref.shape
    first_col = place_ref[1] * cols
    col_pos = lax.broadcasted_iota(jnp.int32, (1, cols), 1) + first_col
    keep = jnp.where(col_pos < B, 0.0, 1.0)
    out_ref[...] = normals_ref[...] * keep + jnp.dot(
        left_ref[...], right_ref[...], preferred_element_type=jnp.float32
    )
    first_row = (place_ref[0] * pl.num_programs(0) + step) * block

    @pl.when((first_row < first_col + cols) & (first_col < first_row + block))
    def _():
        row_pos = lax.broadcasted_iota(jnp.int32, (block, cols), 0) + first_row
        on_diag = (row_pos == col_pos) & (col_pos >= B)
        out_ref[...] = out_ref[...] + jnp.where(on_diag, regular_ref[...], 0.0)


def block_rows(half):
    return max(size for size in range(128, 513, 128) if half % size == 0)


def gram_tile(place, normals, left, right, regular):
    rows, cols = normals.shape
    block = block_rows(rows // 2)
    depth = right.shape[0]
    tile_spec = pl.BlockSpec((block, cols), lambda i, place: (i, 0))
    return pl.pallas_call(
        gram_kernel,
        grid_spec=pltpu.PrefetchScalarGridSpec(
            num_scalar_prefetch=1,
            grid=(rows // block,),
            in_specs=[
                tile_spec,
                pl.BlockSpec((block, depth), lambda i, place: (i, 0)),
                pl.BlockSpec((depth, cols), lambda i, place: (0, 0), pipeline_mode=pl.Buffered(1)),
                pl.BlockSpec((1, cols), lambda i, place: (0, 0)),
            ],
            out_specs=tile_spec,
        ),
        out_shape=pltpu.HBM((rows, cols), jnp.float32),
        compiler_params=pltpu.CompilerParams(vmem_limit_bytes=16 * 2**20),
        cost_estimate=pl.CostEstimate(
            flops=2 * rows * cols * depth, bytes_accessed=4 * rows * cols, transcendentals=0
        ),
        name="gram_tile",
    )(place, normals, left, right, regular)


def tile_kernel(system_ref, strip_ref, gram_ref, right_ref, inverse_ref, out_ref):
    panel = split_dot(strip_ref[...] + gram_ref[...], inverse_ref[...])
    high, low = split(panel)
    left = jnp.concatenate([high, high, low], axis=1)
    out_ref[...] = system_ref[...] + jnp.dot(left, right_ref[...], preferred_element_type=jnp.float32)


def tile_rows(system, strip, gram_cols, right, inverse):
    rows, cols = system.shape
    block = block_rows(rows // 2)
    tile_spec = pl.BlockSpec((block, cols), lambda i: (i, 0))
    lead_spec = pl.BlockSpec((block, B), lambda i: (i, 0))
    return pl.pallas_call(
        tile_kernel,
        grid=(rows // block,),
        in_specs=[
            tile_spec,
            lead_spec,
            lead_spec,
            pl.BlockSpec(right.shape, lambda i: (0, 0), pipeline_mode=pl.Buffered(1)),
            pl.BlockSpec(inverse.shape, lambda i: (0, 0), pipeline_mode=pl.Buffered(1)),
        ],
        out_specs=tile_spec,
        out_shape=jax.ShapeDtypeStruct((rows, cols), jnp.float32),
        compiler_params=pltpu.CompilerParams(vmem_limit_bytes=32 * 2**20),
        cost_estimate=pl.CostEstimate(
            flops=6 * rows * cols * B, bytes_accessed=4 * rows * cols, transcendentals=0
        ),
        name="tile_rows",
    )(system, strip, gram_cols, right, inverse)


def after(value, earlier):
    return lax.optimization_barrier((value, earlier))[0]


def filter_matrix_of(filter_blocks, count):
    positions = jnp.arange(count, dtype=jnp.int32)
    lag = (positions[:, None] - positions[None, :])[:, None, :, None]
    own = filter_blocks[0][None, :, None, :]
    prior = filter_blocks[1][None, :, None, :]
    blocks = jnp.where(lag == 0, own, jnp.where(lag == 1, prior, 0.0))
    return blocks.reshape(count * P_SIZE, count * P_SIZE)


def doubled(value, bits, reached):
    row_peers, col_peers = lax.axis_size("row"), lax.axis_size("col")
    here = lax.axis_index("row") * col_peers + lax.axis_index("col")
    for bit in bits:
        pairs = [(i, i | bit) for i in reached if i | bit < row_peers * col_peers]
        got = lax.ppermute(value, ("row", "col"), pairs)
        value = jnp.where((here & bit) != 0, got, value)
        reached = reached + [to for _, to in pairs]
    return value, reached


def body(normals, design, filter_blocks, regular):
    rows_here, cols_here = normals.shape
    obs_here = design.shape[0]
    row_peers = lax.axis_size("row")
    row_index = lax.axis_index("row")
    col_index = lax.axis_index("col")
    obs = row_peers * obs_here
    core = col_index % 2

    col_peers = lax.axis_size("col")
    col_strip = lax.psum(jnp.where(row_index == 0, normals[:B], 0.0), "row")

    left_strip = jnp.where(col_index == 0, normals[:, :B], 0.0)
    top_strip = jnp.where(row_index == 0, normals[:B], 0.0)
    strip = lax.psum(left_strip, "col")
    col_strip = lax.psum(top_strip, "row")

    index_bits = [1 << i for i in range((row_peers * col_peers - 1).bit_length())]
    hops = [bit for bit in index_bits if bit >= col_peers]
    hops += [bit for bit in reversed(index_bits) if 1 < bit < col_peers]
    leading, reached = doubled(normals[:B, :B], hops, [0])

    chips = col_peers // 2
    design = after(design, (left_strip, top_strip))
    along = [design]
    for s in range(1, chips):
        along.append(lax.ppermute(design, "col", [(c, (c + 2 * s) % col_peers) for c in range(col_peers)]))
    along = jnp.stack(along)
    lead = lax.dynamic_index_in_dim(along, col_index // 2, 0, keepdims=False)[:, :B]
    sent = []
    for to in range(row_peers):
        far = lax.dynamic_index_in_dim(along, (col_index // 2 - to) % chips, 0, keepdims=False)
        sent.append(jnp.concatenate([design, far, lead], axis=1))
    joined = lax.all_to_all(jnp.stack(sent), "row", 0, 0, tiled=True)
    joined = joined.reshape(obs, 2 * cols_here + B)

    leading = jnp.concatenate([joined[:, 2 * cols_here :], leading], axis=0)
    leading, _ = doubled(leading, [1], reached)
    lead, corner = leading[:obs], leading[obs:]
    other = lax.ppermute(
        joined[:, cols_here : 2 * cols_here], "col", [(c, c ^ 1) for c in range(col_peers)]
    )
    filters = filter_matrix_of(filter_blocks, obs // P_SIZE)
    lead_reg = regular[:B].reshape(1, B)
    own_reg = lax.dynamic_slice_in_dim(regular, col_index * cols_here, cols_here).reshape(1, cols_here)
    place = jnp.stack([row_index, col_index]).astype(jnp.int32)
    inverse = corner_factor(corner, lead, filters, lead_reg)
    gram_left, gram_right, gram_rows, gram_cols = filter_sides(place, joined, lead, other, filters, own_reg, lead_reg)
    in_hbm = functools.partial(pltpu.with_memory_space_constraint, memory_space=pltpu.HBM)
    system = gram_tile(place, in_hbm(normals), gram_left, gram_right, own_reg)
    right = right_side(place, col_strip, gram_rows, inverse)
    return tile_rows(in_hbm(system), strip, gram_cols, right, inverse)


def solution(mesh):
    in_specs = (P("row", "col"), P("row", "col"), P(), P())
    out_specs = P("row", "col")
    return jax.shard_map(body, mesh=mesh, in_specs=in_specs, out_specs=out_specs, check_vma=False)
```

```python
import functools

import jax
import jax.numpy as jnp
from jax import lax
from jax.experimental import pallas as pl
from jax.experimental.pallas import tpu as pltpu
from jax.sharding import PartitionSpec as P

B = 256
P_SIZE = 32
STRIP = 32
PIVOTS = 4
HIGHEST = lax.Precision.HIGHEST


def exact_dot(left, right, left_dim, right_dim):
    return lax.dot_general(
        left,
        right,
        (((left_dim,), (right_dim,)), ((), ())),
        precision=HIGHEST,
        preferred_element_type=jnp.float32,
    )


def split(value):
    high = value.astype(jnp.bfloat16)
    low = (value - high.astype(jnp.float32)).astype(jnp.bfloat16)
    return high, low


def split_dot(left, right):
    left_high, left_low = split(left)
    right_high, right_low = split(right)
    wide = functools.partial(jnp.dot, preferred_element_type=jnp.float32)
    return wide(left_high, right_high) + (wide(left_high, right_low) + wide(left_low, right_high))


def corner_kernel(block_ref, design_ref, filter_ref, regular_ref, inverse_ref, upper):
    filtered = exact_dot(filter_ref[...], design_ref[...], 1, 0)
    row_pos = lax.broadcasted_iota(jnp.int32, (B, B), 0)
    col_pos = lax.broadcasted_iota(jnp.int32, (B, B), 1)
    system = block_ref[...] + exact_dot(filtered, filtered, 0, 0)
    system = system + jnp.where(row_pos == col_pos, regular_ref[...], 0.0)
    identity = jnp.where(row_pos == col_pos, 1.0, 0.0)
    half = B // 2
    sub = lax.broadcasted_iota(jnp.int32, (STRIP, half), 0)
    lane = lax.broadcasted_iota(jnp.int32, (STRIP, half), 1)
    zero = jnp.zeros((STRIP, half), jnp.float32)
    for start in range(0, B, STRIP):
        rows = slice(start, start + STRIP)
        strip = jnp.concatenate([system[rows, :], identity[rows, :]], axis=1)
        if start:
            done = upper[:start, :]
            strip = strip - exact_dot(done[:, rows], done, 0, 0)
        low = 0 if start < half else half
        held = [strip[:, at : at + half] for at in range(low, low + 3 * half, half)]
        for first in range(0, STRIP, PIVOTS):
            at = start + first - low
            columns = [
                jnp.broadcast_to(held[0][:, at + q : at + q + 1], (STRIP, half)) for q in range(PIVOTS)
            ]
            pivot_rows = [[part[first + q : first + q + 1, :] for part in held] for q in range(PIVOTS)]
            for q in range(PIVOTS):
                j = first + q
                coef = jnp.where(sub > j, columns[q] * (1.0 / columns[q][j : j + 1, :]), 0.0)
                for m in range(q + 1, PIVOTS):
                    columns[m] = columns[m] - coef * columns[m][j : j + 1, :]
                    scale = coef[first + m : first + m + 1, :]
                    pivot_rows[m] = [
                        row - scale * other for row, other in zip(pivot_rows[m], pivot_rows[q])
                    ]
                held = [part - coef * row for part, row in zip(held, pivot_rows[q])]
        diag = jnp.sum(jnp.where(lane == sub + (start - low), held[0], 0.0), axis=1, keepdims=True)
        held = [part / jnp.sqrt(diag) for part in held]
        upper[rows, :] = jnp.concatenate([*held, zero] if low == 0 else [zero, *held], axis=1)
    inverse_ref[...] = upper[:, B:].T


def corner_factor(block, design, filter_matrix, regular):
    return pl.pallas_call(
        corner_kernel,
        out_shape=jax.ShapeDtypeStruct((B, B), jnp.float32),
        scratch_shapes=[pltpu.VMEM((B, 2 * B), jnp.float32)],
        compiler_params=pltpu.CompilerParams(vmem_limit_bytes=8 * 2**20),
        cost_estimate=pl.CostEstimate(flops=10**9, bytes_accessed=2**20, transcendentals=0),
        name="corner_factor",
    )(block, design, filter_matrix, regular)


def right_kernel(place_ref, high_ref, low_ref, gram_ref, inverse_ref, side_ref, out_ref):
    strip = jnp.concatenate([high_ref[...], low_ref[...]], axis=0) + gram_ref[...]
    panel_high, panel_low = split(-split_dot(inverse_ref[...].T, strip))
    out_ref[:B, :] = panel_high
    out_ref[B : 2 * B, :] = panel_low
    out_ref[2 * B : 3 * B, :] = panel_high
    out_ref[3 * B :, :] = side_ref[...]

    @pl.when(place_ref[1] == 0)
    def _():
        row_pos = lax.broadcasted_iota(jnp.int32, (B, B), 0)
        identity = jnp.where(row_pos == lax.broadcasted_iota(jnp.int32, (B, B), 1), 1.0, 0.0)
        identity = identity.astype(jnp.bfloat16)
        out_ref[:B, :B] = identity
        out_ref[B : 2 * B, :B] = jnp.zeros((B, B), jnp.bfloat16)
        out_ref[2 * B : 3 * B, :B] = identity


def right_side(place, strips, gram_rows, inverse, side):
    cols = gram_rows.shape[1]
    depth = 3 * B + side.shape[0]
    return pl.pallas_call(
        right_kernel,
        in_specs=[pl.BlockSpec(memory_space=pltpu.SMEM)] + [pl.BlockSpec(memory_space=pltpu.VMEM)] * 5,
        out_specs=pl.BlockSpec(memory_space=pltpu.VMEM),
        out_shape=jax.ShapeDtypeStruct((depth, cols), jnp.bfloat16),
        compiler_params=pltpu.CompilerParams(vmem_limit_bytes=24 * 2**20),
        cost_estimate=pl.CostEstimate(
            flops=6 * cols * B * B, bytes_accessed=12 * cols * B, transcendentals=0
        ),
        name="right_side",
    )(place, *strips, gram_rows, inverse, side)


def filter_kernel(
    place_ref,
    joined_ref,
    lead_ref,
    other_ref,
    filter_ref,
    regular_ref,
    lead_reg_ref,
    left_ref,
    right_ref,
    gram_rows_ref,
    gram_cols_ref,
):
    row_index, col_index = place_ref[0], place_ref[1]
    cols = right_ref.shape[1]
    obs = filter_ref.shape[0]
    core = lax.rem(col_index, 2)
    filtered = split_dot(filter_ref[...], joined_ref[:, : 2 * cols])
    here, rows_own = filtered[:, :cols], filtered[:, cols : 2 * cols]
    lead = split_dot(filter_ref[...], lead_ref[...])
    row_pos = lax.broadcasted_iota(jnp.int32, (B, cols), 0)
    col_pos = lax.broadcasted_iota(jnp.int32, (1, cols), 1) + col_index * cols
    gram_rows_ref[...] = split_dot(lead.T, here) + jnp.where(row_pos == col_pos, regular_ref[...], 0.0)
    high, low = split(jnp.where(col_pos < B, 0.0, here))
    right_ref[:obs, :] = high
    right_ref[obs : 2 * obs, :] = low
    right_ref[2 * obs :, :] = high
    rows_other = split_dot(filter_ref[...], other_ref[...])
    for half, value in ((core, rows_own), (1 - core, rows_other)):
        value = value.T
        high, low = split(value)
        rows = pl.ds(pl.multiple_of(half * cols, cols), cols)
        left_ref[rows, :obs] = high
        left_ref[rows, obs : 2 * obs] = high
        left_ref[rows, 2 * obs :] = low
        row_pos = lax.broadcasted_iota(jnp.int32, (cols, B), 0) + (2 * row_index + half) * cols
        lead_pos = lax.broadcasted_iota(jnp.int32, (cols, B), 1)
        gram_cols_ref[rows, :] = split_dot(value, lead) + jnp.where(
            row_pos == lead_pos, lead_reg_ref[...], 0.0
        )


def filter_sides(place, joined, lead, other, filter_matrix, regular, lead_reg):
    cols = other.shape[1]
    obs = filter_matrix.shape[0]
    vmem = pl.BlockSpec(memory_space=pltpu.VMEM)
    return pl.pallas_call(
        filter_kernel,
        in_specs=[pl.BlockSpec(memory_space=pltpu.SMEM)] + [vmem] * 6,
        out_specs=[vmem] * 4,
        out_shape=[
            jax.ShapeDtypeStruct((2 * cols, 3 * obs), jnp.bfloat16),
            jax.ShapeDtypeStruct((3 * obs, cols), jnp.bfloat16),
            jax.ShapeDtypeStruct((B, cols), jnp.float32),
            jax.ShapeDtypeStruct((2 * cols, B), jnp.float32),
        ],
        compiler_params=pltpu.CompilerParams(vmem_limit_bytes=32 * 2**20),
        cost_estimate=pl.CostEstimate(
            flops=18 * cols * obs * B, bytes_accessed=24 * cols * B, transcendentals=0
        ),
        name="filter_sides",
    )(place, joined, lead, other, filter_matrix, regular, lead_reg)


def block_rows(half):
    return max(size for size in range(128, 513, 128) if half % size == 0)


def tile_kernel(place_ref, normals_ref, strip_ref, gram_ref, left_ref, right_ref, inverse_ref, regular_ref, out_ref):
    step = pl.program_id(0)
    block, cols = out_ref.shape
    high, low = split(split_dot(strip_ref[...] + gram_ref[...], inverse_ref[...]))
    left = jnp.concatenate([high, high, low, left_ref[...]], axis=1)
    first_row = (place_ref[0] * pl.num_programs(0) + step) * block
    first_col = place_ref[1] * cols
    col_pos = lax.broadcasted_iota(jnp.int32, (1, cols), 1) + first_col
    keep = jnp.where(col_pos < B, 0.0, 1.0)
    out_ref[...] = normals_ref[...] * keep + jnp.dot(
        left, right_ref[...], preferred_element_type=jnp.float32
    )

    @pl.when((first_row < first_col + cols) & (first_col < first_row + block))
    def _():
        row_pos = lax.broadcasted_iota(jnp.int32, (block, cols), 0) + first_row
        on_diag = (row_pos == col_pos) & (col_pos >= B)
        out_ref[...] = out_ref[...] + jnp.where(on_diag, regular_ref[...], 0.0)


def tile_rows(place, normals, strip, gram_cols, left, right, inverse, regular):
    rows, cols = normals.shape
    block = block_rows(rows // 2)

    def whole(array):
        return pl.BlockSpec(array.shape, lambda i, place: (0,) * array.ndim, pipeline_mode=pl.Buffered(1))

    def blocks(width):
        return pl.BlockSpec((block, width), lambda i, place: (i, 0))

    return pl.pallas_call(
        tile_kernel,
        grid_spec=pltpu.PrefetchScalarGridSpec(
            num_scalar_prefetch=1,
            grid=(rows // block,),
            in_specs=[blocks(cols), blocks(B), blocks(B), blocks(left.shape[1])]
            + [whole(array) for array in [right, inverse, regular]],
            out_specs=blocks(cols),
        ),
        out_shape=jax.ShapeDtypeStruct((rows, cols), jnp.float32),
        compiler_params=pltpu.CompilerParams(vmem_limit_bytes=32 * 2**20),
        cost_estimate=pl.CostEstimate(
            flops=2 * rows * cols * right.shape[0], bytes_accessed=8 * rows * cols, transcendentals=0
        ),
        name="tile_rows",
    )(place, normals, strip, gram_cols, left, right, inverse, regular)


def after(value, earlier):
    return lax.optimization_barrier((value, earlier))[0]


def spread(value, axis, bits):
    peers = lax.axis_size(axis)
    me = lax.axis_index(axis)
    reached = [0]
    for bit in bits:
        pairs = [(i, i | bit) for i in reached if i | bit < peers]
        got = lax.ppermute(value, axis, pairs)
        value = jnp.where((me & bit) != 0, got, value)
        reached += [to for _, to in pairs]
    return value


def filter_matrix_of(filter_blocks, count):
    positions = jnp.arange(count, dtype=jnp.int32)
    lag = (positions[:, None] - positions[None, :])[:, None, :, None]
    own = filter_blocks[0][None, :, None, :]
    prior = filter_blocks[1][None, :, None, :]
    blocks = jnp.where(lag == 0, own, jnp.where(lag == 1, prior, 0.0))
    return blocks.reshape(count * P_SIZE, count * P_SIZE)


def doubled(value, bits, reached):
    row_peers, col_peers = lax.axis_size("row"), lax.axis_size("col")
    here = lax.axis_index("row") * col_peers + lax.axis_index("col")
    for bit in bits:
        pairs = [(i, i | bit) for i in reached if i | bit < row_peers * col_peers]
        got = lax.ppermute(value, ("row", "col"), pairs)
        value = jnp.where((here & bit) != 0, got, value)
        reached = reached + [to for _, to in pairs]
    return value, reached


def body(normals, design, filter_blocks, regular):
    rows_here, cols_here = normals.shape
    obs_here = design.shape[0]
    row_peers = lax.axis_size("row")
    row_index = lax.axis_index("row")
    col_index = lax.axis_index("col")
    obs = row_peers * obs_here
    core = col_index % 2

    col_peers = lax.axis_size("col")
    col_strip = lax.psum(jnp.where(row_index == 0, normals[:B], 0.0), "row")

    left_strip = jnp.where(col_index == 0, normals[:, :B], 0.0)
    strip = lax.psum(left_strip, "col")

    bits = [1 << i for i in range((row_peers - 1).bit_length())]
    halves = after([normals[: B // 2], normals[B // 2 : B]], left_strip)
    strips = [spread(halves[0], "row", bits), spread(halves[1], "row", bits[::-1])]

    leading = jnp.concatenate([half[:, :B] for half in strips], axis=0)
    reached = [row * col_peers for row in range(row_peers)]
    z_bits = [1 << i for i in range(1, (col_peers - 1).bit_length())]
    leading, reached = doubled(leading, z_bits[::-1], reached)

    chips = col_peers // 2
    design = after(design, left_strip)
    along = [design]
    for s in range(1, chips):
        along.append(lax.ppermute(design, "col", [(c, (c + 2 * s) % col_peers) for c in range(col_peers)]))
    along = jnp.stack(along)
    lead = lax.dynamic_index_in_dim(along, col_index // 2, 0, keepdims=False)[:, :B]
    sent = []
    for to in range(row_peers):
        far = lax.dynamic_index_in_dim(along, (col_index // 2 - to) % chips, 0, keepdims=False)
        sent.append(jnp.concatenate([design, far, lead], axis=1))
    joined = lax.all_to_all(jnp.stack(sent), "row", 0, 0, tiled=True)
    joined = joined.reshape(obs, 2 * cols_here + B)

    leading = jnp.concatenate([joined[:, 2 * cols_here :], leading], axis=0)
    leading, _ = doubled(leading, [1], reached)
    lead, corner = leading[:obs], leading[obs:]
    other = lax.ppermute(
        joined[:, cols_here : 2 * cols_here], "col", [(c, c ^ 1) for c in range(col_peers)]
    )
    filters = filter_matrix_of(filter_blocks, obs // P_SIZE)
    lead_reg = regular[:B].reshape(1, B)
    own_reg = lax.dynamic_slice_in_dim(regular, col_index * cols_here, cols_here).reshape(1, cols_here)
    place = jnp.stack([row_index, col_index]).astype(jnp.int32)
    inverse = corner_factor(corner, lead, filters, lead_reg)
    gram_left, gram_right, gram_rows, gram_cols = filter_sides(place, joined, lead, other, filters, own_reg, lead_reg)
    right = right_side(place, strips, gram_rows, inverse, gram_right)
    return tile_rows(place, normals, strip, gram_cols, gram_left, right, inverse, own_reg)


def solution(mesh):
    in_specs = (P("row", "col"), P("row", "col"), P(), P())
    out_specs = P("row", "col")
    return jax.shard_map(body, mesh=mesh, in_specs=in_specs, out_specs=out_specs, check_vma=False)
```

```python
import functools

import jax
import jax.numpy as jnp
from jax import lax
from jax.experimental import pallas as pl
from jax.experimental.pallas import tpu as pltpu
from jax.sharding import PartitionSpec as P

B = 256
P_SIZE = 32
STRIP = 32
PIVOTS = 4
HIGHEST = lax.Precision.HIGHEST


def exact_dot(left, right, left_dim, right_dim):
    return lax.dot_general(
        left,
        right,
        (((left_dim,), (right_dim,)), ((), ())),
        precision=HIGHEST,
        preferred_element_type=jnp.float32,
    )


def split(value):
    high = value.astype(jnp.bfloat16)
    low = (value - high.astype(jnp.float32)).astype(jnp.bfloat16)
    return high, low


def split_dot(left, right):
    left_high, left_low = split(left)
    right_high, right_low = split(right)
    wide = functools.partial(jnp.dot, preferred_element_type=jnp.float32)
    return wide(left_high, right_high) + (wide(left_high, right_low) + wide(left_low, right_high))


def corner_kernel(block_ref, design_ref, filter_ref, regular_ref, inverse_ref, upper):
    filtered = exact_dot(filter_ref[...], design_ref[...], 1, 0)
    row_pos = lax.broadcasted_iota(jnp.int32, (B, B), 0)
    col_pos = lax.broadcasted_iota(jnp.int32, (B, B), 1)
    system = block_ref[...] + exact_dot(filtered, filtered, 0, 0)
    system = system + jnp.where(row_pos == col_pos, regular_ref[...], 0.0)
    identity = jnp.where(row_pos == col_pos, 1.0, 0.0)
    half = B // 2
    sub = lax.broadcasted_iota(jnp.int32, (STRIP, half), 0)
    lane = lax.broadcasted_iota(jnp.int32, (STRIP, half), 1)
    zero = jnp.zeros((STRIP, half), jnp.float32)
    for start in range(0, B, STRIP):
        rows = slice(start, start + STRIP)
        strip = jnp.concatenate([system[rows, :], identity[rows, :]], axis=1)
        if start:
            done = upper[:start, :]
            strip = strip - exact_dot(done[:, rows], done, 0, 0)
        low = 0 if start < half else half
        held = [strip[:, at : at + half] for at in range(low, low + 3 * half, half)]
        for first in range(0, STRIP, PIVOTS):
            at = start + first - low
            columns = [
                jnp.broadcast_to(held[0][:, at + q : at + q + 1], (STRIP, half)) for q in range(PIVOTS)
            ]
            pivot_rows = [[part[first + q : first + q + 1, :] for part in held] for q in range(PIVOTS)]
            for q in range(PIVOTS):
                j = first + q
                coef = jnp.where(sub > j, columns[q] * (1.0 / columns[q][j : j + 1, :]), 0.0)
                for m in range(q + 1, PIVOTS):
                    columns[m] = columns[m] - coef * columns[m][j : j + 1, :]
                    scale = coef[first + m : first + m + 1, :]
                    pivot_rows[m] = [
                        row - scale * other for row, other in zip(pivot_rows[m], pivot_rows[q])
                    ]
                held = [part - coef * row for part, row in zip(held, pivot_rows[q])]
        diag = jnp.sum(jnp.where(lane == sub + (start - low), held[0], 0.0), axis=1, keepdims=True)
        held = [part / jnp.sqrt(diag) for part in held]
        upper[rows, :] = jnp.concatenate([*held, zero] if low == 0 else [zero, *held], axis=1)
    inverse_ref[...] = upper[:, B:].T


def corner_factor(block, design, filter_matrix, regular):
    return pl.pallas_call(
        corner_kernel,
        out_shape=jax.ShapeDtypeStruct((B, B), jnp.float32),
        scratch_shapes=[pltpu.VMEM((B, 2 * B), jnp.float32)],
        compiler_params=pltpu.CompilerParams(vmem_limit_bytes=8 * 2**20),
        cost_estimate=pl.CostEstimate(flops=10**9, bytes_accessed=2**20, transcendentals=0),
        name="corner_factor",
    )(block, design, filter_matrix, regular)


def right_kernel(place_ref, strip_ref, gram_ref, inverse_ref, side_ref, out_ref):
    strip = strip_ref[...] + gram_ref[...]
    panel_high, panel_low = split(-split_dot(inverse_ref[...].T, strip))
    out_ref[:B, :] = panel_high
    out_ref[B : 2 * B, :] = panel_low
    out_ref[2 * B : 3 * B, :] = panel_high
    out_ref[3 * B :, :] = side_ref[...]

    @pl.when(place_ref[1] == 0)
    def _():
        row_pos = lax.broadcasted_iota(jnp.int32, (B, B), 0)
        identity = jnp.where(row_pos == lax.broadcasted_iota(jnp.int32, (B, B), 1), 1.0, 0.0)
        identity = identity.astype(jnp.bfloat16)
        out_ref[:B, :B] = identity
        out_ref[B : 2 * B, :B] = jnp.zeros((B, B), jnp.bfloat16)
        out_ref[2 * B : 3 * B, :B] = identity


def right_side(place, strip, gram_rows, inverse, side):
    cols = gram_rows.shape[1]
    depth = 3 * B + side.shape[0]
    return pl.pallas_call(
        right_kernel,
        in_specs=[pl.BlockSpec(memory_space=pltpu.SMEM)] + [pl.BlockSpec(memory_space=pltpu.VMEM)] * 4,
        out_specs=pl.BlockSpec(memory_space=pltpu.VMEM),
        out_shape=jax.ShapeDtypeStruct((depth, cols), jnp.bfloat16),
        compiler_params=pltpu.CompilerParams(vmem_limit_bytes=24 * 2**20),
        cost_estimate=pl.CostEstimate(
            flops=6 * cols * B * B, bytes_accessed=12 * cols * B, transcendentals=0
        ),
        name="right_side",
    )(place, strip, gram_rows, inverse, side)


def filter_kernel(
    place_ref,
    joined_ref,
    lead_ref,
    other_ref,
    filter_ref,
    regular_ref,
    lead_reg_ref,
    left_ref,
    right_ref,
    gram_rows_ref,
    gram_cols_ref,
):
    row_index, col_index = place_ref[0], place_ref[1]
    cols = right_ref.shape[1]
    obs = filter_ref.shape[0]
    core = lax.rem(col_index, 2)
    filtered = split_dot(filter_ref[...], joined_ref[:, : 2 * cols])
    here, rows_own = filtered[:, :cols], filtered[:, cols : 2 * cols]
    lead = split_dot(filter_ref[...], lead_ref[...])
    row_pos = lax.broadcasted_iota(jnp.int32, (B, cols), 0)
    col_pos = lax.broadcasted_iota(jnp.int32, (1, cols), 1) + col_index * cols
    gram_rows_ref[...] = split_dot(lead.T, here) + jnp.where(row_pos == col_pos, regular_ref[...], 0.0)
    high, low = split(jnp.where(col_pos < B, 0.0, here))
    right_ref[:obs, :] = high
    right_ref[obs : 2 * obs, :] = low
    right_ref[2 * obs :, :] = high
    rows_other = split_dot(filter_ref[...], other_ref[...])
    for half, value in ((core, rows_own), (1 - core, rows_other)):
        value = value.T
        high, low = split(value)
        rows = pl.ds(pl.multiple_of(half * cols, cols), cols)
        left_ref[rows, :obs] = high
        left_ref[rows, obs : 2 * obs] = high
        left_ref[rows, 2 * obs :] = low
        row_pos = lax.broadcasted_iota(jnp.int32, (cols, B), 0) + (2 * row_index + half) * cols
        lead_pos = lax.broadcasted_iota(jnp.int32, (cols, B), 1)
        gram_cols_ref[rows, :] = split_dot(value, lead) + jnp.where(
            row_pos == lead_pos, lead_reg_ref[...], 0.0
        )


def filter_sides(place, joined, lead, other, filter_matrix, regular, lead_reg):
    cols = other.shape[1]
    obs = filter_matrix.shape[0]
    vmem = pl.BlockSpec(memory_space=pltpu.VMEM)
    return pl.pallas_call(
        filter_kernel,
        in_specs=[pl.BlockSpec(memory_space=pltpu.SMEM)] + [vmem] * 6,
        out_specs=[vmem] * 4,
        out_shape=[
            jax.ShapeDtypeStruct((2 * cols, 3 * obs), jnp.bfloat16),
            jax.ShapeDtypeStruct((3 * obs, cols), jnp.bfloat16),
            jax.ShapeDtypeStruct((B, cols), jnp.float32),
            jax.ShapeDtypeStruct((2 * cols, B), jnp.float32),
        ],
        compiler_params=pltpu.CompilerParams(vmem_limit_bytes=32 * 2**20),
        cost_estimate=pl.CostEstimate(
            flops=18 * cols * obs * B, bytes_accessed=24 * cols * B, transcendentals=0
        ),
        name="filter_sides",
    )(place, joined, lead, other, filter_matrix, regular, lead_reg)


def block_rows(half):
    return max(size for size in range(128, 513, 128) if half % size == 0)


def tile_kernel(place_ref, normals_ref, strip_ref, gram_ref, left_ref, right_ref, inverse_ref, regular_ref, out_ref):
    step = pl.program_id(0)
    block, cols = out_ref.shape
    high, low = split(split_dot(strip_ref[...] + gram_ref[...], inverse_ref[...]))
    left = jnp.concatenate([high, high, low, left_ref[...]], axis=1)
    first_row = (place_ref[0] * pl.num_programs(0) + step) * block
    first_col = place_ref[1] * cols
    col_pos = lax.broadcasted_iota(jnp.int32, (1, cols), 1) + first_col
    keep = jnp.where(col_pos < B, 0.0, 1.0)
    out_ref[...] = normals_ref[...] * keep + jnp.dot(
        left, right_ref[...], preferred_element_type=jnp.float32
    )

    @pl.when((first_row < first_col + cols) & (first_col < first_row + block))
    def _():
        row_pos = lax.broadcasted_iota(jnp.int32, (block, cols), 0) + first_row
        on_diag = (row_pos == col_pos) & (col_pos >= B)
        out_ref[...] = out_ref[...] + jnp.where(on_diag, regular_ref[...], 0.0)


def tile_rows(place, normals, strip, gram_cols, left, right, inverse, regular):
    rows, cols = normals.shape
    block = block_rows(rows // 2)

    def whole(array):
        return pl.BlockSpec(array.shape, lambda i, place: (0,) * array.ndim, pipeline_mode=pl.Buffered(1))

    def blocks(width):
        return pl.BlockSpec((block, width), lambda i, place: (i, 0))

    return pl.pallas_call(
        tile_kernel,
        grid_spec=pltpu.PrefetchScalarGridSpec(
            num_scalar_prefetch=1,
            grid=(rows // block,),
            in_specs=[blocks(cols), blocks(B), blocks(B), blocks(left.shape[1])]
            + [whole(array) for array in [right, inverse, regular]],
            out_specs=blocks(cols),
        ),
        out_shape=jax.ShapeDtypeStruct((rows, cols), jnp.float32),
        compiler_params=pltpu.CompilerParams(vmem_limit_bytes=32 * 2**20),
        cost_estimate=pl.CostEstimate(
            flops=2 * rows * cols * right.shape[0], bytes_accessed=8 * rows * cols, transcendentals=0
        ),
        name="tile_rows",
    )(place, normals, strip, gram_cols, left, right, inverse, regular)


def after(value, earlier):
    return lax.optimization_barrier((value, earlier))[0]


def filter_matrix_of(filter_blocks, count):
    positions = jnp.arange(count, dtype=jnp.int32)
    lag = (positions[:, None] - positions[None, :])[:, None, :, None]
    own = filter_blocks[0][None, :, None, :]
    prior = filter_blocks[1][None, :, None, :]
    blocks = jnp.where(lag == 0, own, jnp.where(lag == 1, prior, 0.0))
    return blocks.reshape(count * P_SIZE, count * P_SIZE)


def row_strip_piece(normals, later):
    peers = lax.axis_size("col")
    chips = peers // 2
    size = normals.shape[0] // chips
    col_index = lax.axis_index("col")
    arrived = [
        lax.ppermute(normals[z * size : (z + 1) * size, :B], "col", [(0, 2 * z)]) for z in range(1, chips)
    ]
    arrived = sum(after(arrived, later))
    piece = jnp.where(col_index == 0, normals[:size, :B], arrived)
    second = lax.ppermute(piece[size // 2 :], "col", [(c, c + 1) for c in range(0, peers, 2)])
    return jnp.where(col_index % 2 == 0, piece[: size // 2], second)


def doubled(value, bits, reached):
    row_peers, col_peers = lax.axis_size("row"), lax.axis_size("col")
    here = lax.axis_index("row") * col_peers + lax.axis_index("col")
    for bit in bits:
        pairs = [(i, i | bit) for i in reached if i | bit < row_peers * col_peers]
        got = lax.ppermute(value, ("row", "col"), pairs)
        value = jnp.where((here & bit) != 0, got, value)
        reached = reached + [to for _, to in pairs]
    return value, reached


def body(normals, design, filter_blocks, regular):
    rows_here, cols_here = normals.shape
    obs_here = design.shape[0]
    row_peers = lax.axis_size("row")
    row_index = lax.axis_index("row")
    col_index = lax.axis_index("col")
    obs = row_peers * obs_here
    core = col_index % 2

    col_peers = lax.axis_size("col")
    col_strip = lax.psum(jnp.where(row_index == 0, normals[:B], 0.0), "row")

    top_strip = jnp.where(row_index == 0, normals[:B], 0.0)
    col_strip = lax.psum(top_strip, "row")

    index_bits = [1 << i for i in range((row_peers * col_peers - 1).bit_length())]
    leading, reached = doubled(normals[:B, :B], [bit for bit in index_bits if bit >= col_peers], [0])

    chips = col_peers // 2
    design = after(design, top_strip)
    along = [design]
    for s in range(1, chips):
        along.append(lax.ppermute(design, "col", [(c, (c + 2 * s) % col_peers) for c in range(col_peers)]))
    along = jnp.stack(along)
    lead = lax.dynamic_index_in_dim(along, col_index // 2, 0, keepdims=False)[:, :B]
    sent = []
    for to in range(row_peers):
        far = lax.dynamic_index_in_dim(along, (col_index // 2 - to) % chips, 0, keepdims=False)
        sent.append(jnp.concatenate([design, far, lead], axis=1))
    sent = after(jnp.stack(sent), leading)
    joined = lax.all_to_all(sent, "row", 0, 0, tiled=True)
    joined = joined.reshape(obs, 2 * cols_here + B)

    strip = lax.all_gather(row_strip_piece(normals, joined), "col", axis=0, tiled=True)

    leading, reached = doubled(leading, [bit for bit in reversed(index_bits) if 1 < bit < col_peers], reached)
    leading = jnp.concatenate([joined[:, 2 * cols_here :], leading], axis=0)
    leading, _ = doubled(leading, [1], reached)
    lead, corner = leading[:obs], leading[obs:]
    other = lax.ppermute(
        joined[:, cols_here : 2 * cols_here], "col", [(c, c ^ 1) for c in range(col_peers)]
    )
    filters = filter_matrix_of(filter_blocks, obs // P_SIZE)
    lead_reg = regular[:B].reshape(1, B)
    own_reg = lax.dynamic_slice_in_dim(regular, col_index * cols_here, cols_here).reshape(1, cols_here)
    place = jnp.stack([row_index, col_index]).astype(jnp.int32)
    inverse = corner_factor(corner, lead, filters, lead_reg)
    gram_left, gram_right, gram_rows, gram_cols = filter_sides(place, joined, lead, other, filters, own_reg, lead_reg)
    right = right_side(place, col_strip, gram_rows, inverse, gram_right)
    return tile_rows(place, normals, strip, gram_cols, gram_left, right, inverse, own_reg)


def solution(mesh):
    in_specs = (P("row", "col"), P("row", "col"), P(), P())
    out_specs = P("row", "col")
    return jax.shard_map(body, mesh=mesh, in_specs=in_specs, out_specs=out_specs, check_vma=False)
```

```python
import functools

import jax
import jax.numpy as jnp
from jax import lax
from jax.experimental import pallas as pl
from jax.experimental.pallas import tpu as pltpu
from jax.sharding import PartitionSpec as P

B = 256
P_SIZE = 32
STRIP = 32
PIVOTS = 4
HIGHEST = lax.Precision.HIGHEST


def exact_dot(left, right, left_dim, right_dim):
    return lax.dot_general(
        left,
        right,
        (((left_dim,), (right_dim,)), ((), ())),
        precision=HIGHEST,
        preferred_element_type=jnp.float32,
    )


def split(value):
    high = value.astype(jnp.bfloat16)
    low = (value - high.astype(jnp.float32)).astype(jnp.bfloat16)
    return high, low


def split_dot(left, right):
    left_high, left_low = split(left)
    right_high, right_low = split(right)
    wide = functools.partial(jnp.dot, preferred_element_type=jnp.float32)
    return wide(left_high, right_high) + (wide(left_high, right_low) + wide(left_low, right_high))


def corner_kernel(block_ref, design_ref, filter_ref, regular_ref, inverse_ref, upper):
    filtered = exact_dot(filter_ref[...], design_ref[...], 1, 0)
    row_pos = lax.broadcasted_iota(jnp.int32, (B, B), 0)
    col_pos = lax.broadcasted_iota(jnp.int32, (B, B), 1)
    system = block_ref[...] + exact_dot(filtered, filtered, 0, 0)
    system = system + jnp.where(row_pos == col_pos, regular_ref[...], 0.0)
    identity = jnp.where(row_pos == col_pos, 1.0, 0.0)
    half = B // 2
    sub = lax.broadcasted_iota(jnp.int32, (STRIP, half), 0)
    lane = lax.broadcasted_iota(jnp.int32, (STRIP, half), 1)
    zero = jnp.zeros((STRIP, half), jnp.float32)
    for start in range(0, B, STRIP):
        rows = slice(start, start + STRIP)
        strip = jnp.concatenate([system[rows, :], identity[rows, :]], axis=1)
        if start:
            done = upper[:start, :]
            strip = strip - exact_dot(done[:, rows], done, 0, 0)
        low = 0 if start < half else half
        held = [strip[:, at : at + half] for at in range(low, low + 3 * half, half)]
        for first in range(0, STRIP, PIVOTS):
            at = start + first - low
            columns = [
                jnp.broadcast_to(held[0][:, at + q : at + q + 1], (STRIP, half)) for q in range(PIVOTS)
            ]
            pivot_rows = [[part[first + q : first + q + 1, :] for part in held] for q in range(PIVOTS)]
            for q in range(PIVOTS):
                j = first + q
                coef = jnp.where(sub > j, columns[q] * (1.0 / columns[q][j : j + 1, :]), 0.0)
                for m in range(q + 1, PIVOTS):
                    columns[m] = columns[m] - coef * columns[m][j : j + 1, :]
                    scale = coef[first + m : first + m + 1, :]
                    pivot_rows[m] = [
                        row - scale * other for row, other in zip(pivot_rows[m], pivot_rows[q])
                    ]
                held = [part - coef * row for part, row in zip(held, pivot_rows[q])]
        diag = jnp.sum(jnp.where(lane == sub + (start - low), held[0], 0.0), axis=1, keepdims=True)
        held = [part / jnp.sqrt(diag) for part in held]
        upper[rows, :] = jnp.concatenate([*held, zero] if low == 0 else [zero, *held], axis=1)
    inverse_ref[...] = upper[:, B:].T


def corner_factor(block, design, filter_matrix, regular):
    return pl.pallas_call(
        corner_kernel,
        out_shape=jax.ShapeDtypeStruct((B, B), jnp.float32),
        scratch_shapes=[pltpu.VMEM((B, 2 * B), jnp.float32)],
        compiler_params=pltpu.CompilerParams(vmem_limit_bytes=8 * 2**20),
        cost_estimate=pl.CostEstimate(flops=0, bytes_accessed=0, transcendentals=0),
        name="corner_factor",
    )(block, design, filter_matrix, regular)


def sides_kernel(
    place_ref,
    joined_ref,
    lead_ref,
    other_ref,
    strip_ref,
    inverse_ref,
    filter_ref,
    regular_ref,
    lead_reg_ref,
    left_ref,
    right_ref,
    gram_cols_ref,
):
    row_index, col_index = place_ref[0], place_ref[1]
    cols = right_ref.shape[1]
    obs = filter_ref.shape[0]
    core = lax.rem(col_index, 2)
    filtered = split_dot(filter_ref[...], joined_ref[:, : 2 * cols])
    here, rows_own = filtered[:, :cols], filtered[:, cols:]
    lead = split_dot(filter_ref[...], lead_ref[...])

    row_pos = lax.broadcasted_iota(jnp.int32, (B, cols), 0)
    col_pos = lax.broadcasted_iota(jnp.int32, (1, cols), 1) + col_index * cols
    strip = strip_ref[...] + split_dot(lead.T, here)
    strip = strip + jnp.where(row_pos == col_pos, regular_ref[...], 0.0)
    high, low = split(-split_dot(inverse_ref[...].T, strip))
    right_ref[:B, :] = high
    right_ref[B : 2 * B, :] = low
    right_ref[2 * B : 3 * B, :] = high
    high, low = split(jnp.where(col_pos < B, 0.0, here))
    right_ref[3 * B : 3 * B + obs, :] = high
    right_ref[3 * B + obs : 3 * B + 2 * obs, :] = low
    right_ref[3 * B + 2 * obs :, :] = high

    @pl.when(col_index == 0)
    def _():
        row_pos = lax.broadcasted_iota(jnp.int32, (B, B), 0)
        identity = jnp.where(row_pos == lax.broadcasted_iota(jnp.int32, (B, B), 1), 1.0, 0.0)
        identity = identity.astype(jnp.bfloat16)
        right_ref[:B, :B] = identity
        right_ref[B : 2 * B, :B] = jnp.zeros((B, B), jnp.bfloat16)
        right_ref[2 * B : 3 * B, :B] = identity

    rows_other = split_dot(filter_ref[...], other_ref[...])
    for half, value in ((core, rows_own), (1 - core, rows_other)):
        value = value.T
        high, low = split(value)
        rows = pl.ds(pl.multiple_of(half * cols, cols), cols)
        left_ref[rows, :obs] = high
        left_ref[rows, obs : 2 * obs] = high
        left_ref[rows, 2 * obs :] = low
        row_pos = lax.broadcasted_iota(jnp.int32, (cols, B), 0) + (2 * row_index + half) * cols
        lead_pos = lax.broadcasted_iota(jnp.int32, (cols, B), 1)
        gram_cols_ref[rows, :] = split_dot(value, lead) + jnp.where(
            row_pos == lead_pos, lead_reg_ref[...], 0.0
        )


def both_sides(place, joined, lead, other, strip, inverse, filter_matrix, regular, lead_reg):
    cols = other.shape[1]
    obs = filter_matrix.shape[0]
    vmem = pl.BlockSpec(memory_space=pltpu.VMEM)
    return pl.pallas_call(
        sides_kernel,
        in_specs=[pl.BlockSpec(memory_space=pltpu.SMEM)] + [vmem] * 8,
        out_specs=[vmem] * 3,
        out_shape=[
            pltpu.HBM((2 * cols, 3 * obs), jnp.bfloat16),
            pltpu.HBM((3 * (obs + B), cols), jnp.bfloat16),
            pltpu.HBM((2 * cols, B), jnp.float32),
        ],
        compiler_params=pltpu.CompilerParams(vmem_limit_bytes=36 * 2**20),
        cost_estimate=pl.CostEstimate(flops=0, bytes_accessed=0, transcendentals=0),
        name="both_sides",
    )(place, joined, lead, other, strip, inverse, filter_matrix, regular, lead_reg)


def block_rows(half):
    return max(size for size in range(128, 513, 128) if half % size == 0)


def tile_kernel(place_ref, normals_ref, strip_ref, gram_ref, left_ref, right_ref, inverse_ref, regular_ref, out_ref):
    step = pl.program_id(0)
    block, cols = out_ref.shape
    high, low = split(split_dot(strip_ref[...] + gram_ref[...], inverse_ref[...]))
    left = jnp.concatenate([high, high, low, left_ref[...]], axis=1)
    first_row = (place_ref[0] * pl.num_programs(0) + step) * block
    first_col = place_ref[1] * cols
    col_pos = lax.broadcasted_iota(jnp.int32, (1, cols), 1) + first_col
    keep = jnp.where(col_pos < B, 0.0, 1.0)
    out_ref[...] = normals_ref[...] * keep + jnp.dot(
        left, right_ref[...], preferred_element_type=jnp.float32
    )

    @pl.when((first_row < first_col + cols) & (first_col < first_row + block))
    def _():
        row_pos = lax.broadcasted_iota(jnp.int32, (block, cols), 0) + first_row
        on_diag = (row_pos == col_pos) & (col_pos >= B)
        out_ref[...] = out_ref[...] + jnp.where(on_diag, regular_ref[...], 0.0)


def tile_rows(place, normals, strip, gram_cols, left, right, inverse, regular):
    rows, cols = normals.shape
    block = block_rows(rows // 2)

    def whole(array):
        return pl.BlockSpec(array.shape, lambda i, place: (0,) * array.ndim, pipeline_mode=pl.Buffered(1))

    def blocks(width):
        return pl.BlockSpec((block, width), lambda i, place: (i, 0))

    return pl.pallas_call(
        tile_kernel,
        grid_spec=pltpu.PrefetchScalarGridSpec(
            num_scalar_prefetch=1,
            grid=(rows // block,),
            in_specs=[blocks(cols), blocks(B), blocks(B), blocks(left.shape[1])]
            + [whole(array) for array in [right, inverse, regular]],
            out_specs=blocks(cols),
        ),
        out_shape=jax.ShapeDtypeStruct((rows, cols), jnp.float32),
        compiler_params=pltpu.CompilerParams(vmem_limit_bytes=32 * 2**20),
        cost_estimate=pl.CostEstimate(flops=0, bytes_accessed=0, transcendentals=0),
        name="tile_rows",
    )(place, normals, strip, gram_cols, left, right, inverse, regular)


def after(value, earlier):
    return lax.optimization_barrier((value, earlier))[0]


def filter_matrix_of(filter_blocks, count):
    positions = jnp.arange(count, dtype=jnp.int32)
    lag = (positions[:, None] - positions[None, :])[:, None, :, None]
    own = filter_blocks[0][None, :, None, :]
    prior = filter_blocks[1][None, :, None, :]
    blocks = jnp.where(lag == 0, own, jnp.where(lag == 1, prior, 0.0))
    return blocks.reshape(count * P_SIZE, count * P_SIZE)


def row_strip_piece(normals):
    peers = lax.axis_size("col")
    chips = peers // 2
    size = normals.shape[0] // chips
    col_index = lax.axis_index("col")
    arrived = [
        lax.ppermute(normals[z * size : (z + 1) * size, :B], "col", [(0, 2 * z)]) for z in range(1, chips)
    ]
    arrived = sum(arrived)
    piece = jnp.where(col_index == 0, normals[:size, :B], arrived)
    second = lax.ppermute(piece[size // 2 :], "col", [(c, c + 1) for c in range(0, peers, 2)])
    return jnp.where(col_index % 2 == 0, piece[: size // 2], second)


def doubled(value, bits, reached):
    row_peers, col_peers = lax.axis_size("row"), lax.axis_size("col")
    here = lax.axis_index("row") * col_peers + lax.axis_index("col")
    for bit in bits:
        pairs = [(i, i | bit) for i in reached if i | bit < row_peers * col_peers]
        got = lax.ppermute(value, ("row", "col"), pairs)
        value = jnp.where((here & bit) != 0, got, value)
        reached = reached + [to for _, to in pairs]
    return value, reached


def body(normals, design, filter_blocks, regular):
    rows_here, cols_here = normals.shape
    obs_here = design.shape[0]
    row_peers = lax.axis_size("row")
    row_index = lax.axis_index("row")
    col_index = lax.axis_index("col")
    obs = row_peers * obs_here
    core = col_index % 2

    col_peers = lax.axis_size("col")
    col_strip = lax.psum(jnp.where(row_index == 0, normals[:B], 0.0), "row")

    top_strip = jnp.where(row_index == 0, normals[:B], 0.0)
    col_strip = lax.psum(top_strip, "row")

    piece = row_strip_piece(normals)
    strip = lax.all_gather(piece, "col", axis=0, tiled=True)

    index_bits = [1 << i for i in range((row_peers * col_peers - 1).bit_length())]
    leading, reached = doubled(normals[:B, :B], [bit for bit in index_bits if bit >= col_peers], [0])

    chips = col_peers // 2
    design = after(design, top_strip)
    along = [design]
    for s in range(1, chips):
        along.append(lax.ppermute(design, "col", [(c, (c + 2 * s) % col_peers) for c in range(col_peers)]))
    along = jnp.stack(along)
    lead = lax.dynamic_index_in_dim(along, col_index // 2, 0, keepdims=False)[:, :B]
    sent = []
    for to in range(row_peers):
        far = lax.dynamic_index_in_dim(along, (col_index // 2 - to) % chips, 0, keepdims=False)
        sent.append(jnp.concatenate([design, far, lead], axis=1))
    sent = after(jnp.stack(sent), (leading, piece))
    joined = lax.all_to_all(sent, "row", 0, 0, tiled=True)
    joined = joined.reshape(obs, 2 * cols_here + B)

    leading, reached = doubled(leading, [bit for bit in reversed(index_bits) if 1 < bit < col_peers], reached)
    leading = jnp.concatenate([joined[:, 2 * cols_here :], leading], axis=0)
    leading, _ = doubled(leading, [1], reached)
    lead, corner = leading[:obs], leading[obs:]
    other = lax.ppermute(
        joined[:, cols_here : 2 * cols_here], "col", [(c, c ^ 1) for c in range(col_peers)]
    )
    filters = filter_matrix_of(filter_blocks, obs // P_SIZE)
    lead_reg = regular[:B].reshape(1, B)
    own_reg = lax.dynamic_slice_in_dim(regular, col_index * cols_here, cols_here).reshape(1, cols_here)
    place = jnp.stack([row_index, col_index]).astype(jnp.int32)
    inverse = corner_factor(corner, lead, filters, lead_reg)
    left, right, gram_cols = both_sides(
        place, joined, lead, other, col_strip, inverse, filters, own_reg, lead_reg
    )
    large = [pltpu.with_memory_space_constraint(array, pltpu.HBM) for array in (normals, strip, gram_cols, left)]
    return tile_rows(place, *large, right, inverse, own_reg)


def solution(mesh):
    in_specs = (P("row", "col"), P("row", "col"), P(), P())
    out_specs = P("row", "col")
    return jax.shard_map(body, mesh=mesh, in_specs=in_specs, out_specs=out_specs, check_vma=False)
```

```python
import functools

import jax
import jax.numpy as jnp
from jax import lax
from jax.experimental import pallas as pl
from jax.experimental.pallas import tpu as pltpu
from jax.sharding import PartitionSpec as P

B = 256
P_SIZE = 32
STRIP = 32
PIVOTS = 4
HIGHEST = lax.Precision.HIGHEST


def exact_dot(left, right, left_dim, right_dim):
    return lax.dot_general(
        left,
        right,
        (((left_dim,), (right_dim,)), ((), ())),
        precision=HIGHEST,
        preferred_element_type=jnp.float32,
    )


def split(value):
    high = value.astype(jnp.bfloat16)
    low = (value - high.astype(jnp.float32)).astype(jnp.bfloat16)
    return high, low


def split_dot(left, right):
    left_high, left_low = split(left)
    right_high, right_low = split(right)
    wide = functools.partial(jnp.dot, preferred_element_type=jnp.float32)
    return wide(left_high, right_high) + (wide(left_high, right_low) + wide(left_low, right_high))


def corner_kernel(block_ref, design_ref, filter_ref, regular_ref, inverse_ref, upper):
    filtered = exact_dot(filter_ref[...], design_ref[...], 1, 0)
    row_pos = lax.broadcasted_iota(jnp.int32, (B, B), 0)
    col_pos = lax.broadcasted_iota(jnp.int32, (B, B), 1)
    system = block_ref[...] + exact_dot(filtered, filtered, 0, 0)
    system = system + jnp.where(row_pos == col_pos, regular_ref[...], 0.0)
    identity = jnp.where(row_pos == col_pos, 1.0, 0.0)
    half = B // 2
    sub = lax.broadcasted_iota(jnp.int32, (STRIP, half), 0)
    lane = lax.broadcasted_iota(jnp.int32, (STRIP, half), 1)
    zero = jnp.zeros((STRIP, half), jnp.float32)
    for start in range(0, B, STRIP):
        rows = slice(start, start + STRIP)
        strip = jnp.concatenate([system[rows, :], identity[rows, :]], axis=1)
        if start:
            done = upper[:start, :]
            strip = strip - exact_dot(done[:, rows], done, 0, 0)
        low = 0 if start < half else half
        held = [strip[:, at : at + half] for at in range(low, low + 3 * half, half)]
        for first in range(0, STRIP, PIVOTS):
            at = start + first - low
            columns = [
                jnp.broadcast_to(held[0][:, at + q : at + q + 1], (STRIP, half)) for q in range(PIVOTS)
            ]
            pivot_rows = [[part[first + q : first + q + 1, :] for part in held] for q in range(PIVOTS)]
            for q in range(PIVOTS):
                j = first + q
                coef = jnp.where(sub > j, columns[q] * (1.0 / columns[q][j : j + 1, :]), 0.0)
                for m in range(q + 1, PIVOTS):
                    columns[m] = columns[m] - coef * columns[m][j : j + 1, :]
                    scale = coef[first + m : first + m + 1, :]
                    pivot_rows[m] = [
                        row - scale * other for row, other in zip(pivot_rows[m], pivot_rows[q])
                    ]
                held = [part - coef * row for part, row in zip(held, pivot_rows[q])]
        diag = jnp.sum(jnp.where(lane == sub + (start - low), held[0], 0.0), axis=1, keepdims=True)
        held = [part / jnp.sqrt(diag) for part in held]
        upper[rows, :] = jnp.concatenate([*held, zero] if low == 0 else [zero, *held], axis=1)
    inverse_ref[...] = upper[:, B:].T


def corner_factor(block, design, filter_matrix, regular):
    return pl.pallas_call(
        corner_kernel,
        out_shape=jax.ShapeDtypeStruct((B, B), jnp.float32),
        scratch_shapes=[pltpu.VMEM((B, 2 * B), jnp.float32)],
        compiler_params=pltpu.CompilerParams(vmem_limit_bytes=8 * 2**20),
        cost_estimate=pl.CostEstimate(flops=0, bytes_accessed=0, transcendentals=0),
        name="corner_factor",
    )(block, design, filter_matrix, regular)


def sides_kernel(
    place_ref,
    joined_ref,
    lead_ref,
    other_ref,
    strip_ref,
    inverse_ref,
    filter_ref,
    regular_ref,
    lead_reg_ref,
    left_ref,
    right_ref,
    gram_cols_ref,
):
    row_index, col_index = place_ref[0], place_ref[1]
    cols = right_ref.shape[1]
    obs = filter_ref.shape[0]
    core = lax.rem(col_index, 2)
    filtered = split_dot(filter_ref[...], joined_ref[:, : 2 * cols])
    here, rows_own = filtered[:, :cols], filtered[:, cols:]
    lead = split_dot(filter_ref[...], lead_ref[...])

    row_pos = lax.broadcasted_iota(jnp.int32, (B, cols), 0)
    col_pos = lax.broadcasted_iota(jnp.int32, (1, cols), 1) + col_index * cols
    strip = strip_ref[...] + split_dot(lead.T, here)
    strip = strip + jnp.where(row_pos == col_pos, regular_ref[...], 0.0)
    high, low = split(-split_dot(inverse_ref[...].T, strip))
    right_ref[:B, :] = high
    right_ref[B : 2 * B, :] = low
    right_ref[2 * B : 3 * B, :] = high
    high, low = split(jnp.where(col_pos < B, 0.0, here))
    right_ref[3 * B : 3 * B + obs, :] = high
    right_ref[3 * B + obs : 3 * B + 2 * obs, :] = low
    right_ref[3 * B + 2 * obs :, :] = high

    @pl.when(col_index == 0)
    def _():
        row_pos = lax.broadcasted_iota(jnp.int32, (B, B), 0)
        identity = jnp.where(row_pos == lax.broadcasted_iota(jnp.int32, (B, B), 1), 1.0, 0.0)
        identity = identity.astype(jnp.bfloat16)
        right_ref[:B, :B] = identity
        right_ref[B : 2 * B, :B] = jnp.zeros((B, B), jnp.bfloat16)
        right_ref[2 * B : 3 * B, :B] = identity

    rows_other = split_dot(filter_ref[...], other_ref[...])
    for half, value in ((core, rows_own), (1 - core, rows_other)):
        value = value.T
        high, low = split(value)
        rows = pl.ds(pl.multiple_of(half * cols, cols), cols)
        left_ref[rows, :obs] = high
        left_ref[rows, obs : 2 * obs] = high
        left_ref[rows, 2 * obs :] = low
        row_pos = lax.broadcasted_iota(jnp.int32, (cols, B), 0) + (2 * row_index + half) * cols
        lead_pos = lax.broadcasted_iota(jnp.int32, (cols, B), 1)
        gram_cols_ref[rows, :] = split_dot(value, lead) + jnp.where(
            row_pos == lead_pos, lead_reg_ref[...], 0.0
        )


def both_sides(place, joined, lead, other, strip, inverse, filter_matrix, regular, lead_reg):
    cols = other.shape[1]
    obs = filter_matrix.shape[0]
    vmem = pl.BlockSpec(memory_space=pltpu.VMEM)
    return pl.pallas_call(
        sides_kernel,
        in_specs=[pl.BlockSpec(memory_space=pltpu.SMEM)] + [vmem] * 8,
        out_specs=[vmem] * 3,
        out_shape=[
            pltpu.HBM((2 * cols, 3 * obs), jnp.bfloat16),
            pltpu.HBM((3 * (obs + B), cols), jnp.bfloat16),
            pltpu.HBM((2 * cols, B), jnp.float32),
        ],
        compiler_params=pltpu.CompilerParams(vmem_limit_bytes=36 * 2**20),
        cost_estimate=pl.CostEstimate(flops=0, bytes_accessed=0, transcendentals=0),
        name="both_sides",
    )(place, joined, lead, other, strip, inverse, filter_matrix, regular, lead_reg)


def block_rows(half):
    return max(size for size in range(128, 513, 128) if half % size == 0)


def tile_kernel(place_ref, normals_ref, strip_ref, gram_ref, left_ref, right_ref, inverse_ref, regular_ref, out_ref):
    step = pl.program_id(0)
    block, cols = out_ref.shape
    high, low = split(split_dot(strip_ref[...] + gram_ref[...], inverse_ref[...]))
    left = jnp.concatenate([high, high, low, left_ref[...]], axis=1)
    first_row = (place_ref[0] * pl.num_programs(0) + step) * block
    first_col = place_ref[1] * cols
    col_pos = lax.broadcasted_iota(jnp.int32, (1, cols), 1) + first_col
    keep = jnp.where(col_pos < B, 0.0, 1.0)
    out_ref[...] = normals_ref[...] * keep + jnp.dot(
        left, right_ref[...], preferred_element_type=jnp.float32
    )

    @pl.when((first_row < first_col + cols) & (first_col < first_row + block))
    def _():
        row_pos = lax.broadcasted_iota(jnp.int32, (block, cols), 0) + first_row
        on_diag = (row_pos == col_pos) & (col_pos >= B)
        out_ref[...] = out_ref[...] + jnp.where(on_diag, regular_ref[...], 0.0)


def tile_rows(place, normals, strip, gram_cols, left, right, inverse, regular):
    rows, cols = normals.shape
    block = block_rows(rows // 2)

    def whole(array):
        return pl.BlockSpec(array.shape, lambda i, place: (0,) * array.ndim, pipeline_mode=pl.Buffered(1))

    def blocks(width):
        return pl.BlockSpec((block, width), lambda i, place: (i, 0))

    return pl.pallas_call(
        tile_kernel,
        grid_spec=pltpu.PrefetchScalarGridSpec(
            num_scalar_prefetch=1,
            grid=(rows // block,),
            in_specs=[blocks(cols), blocks(B), blocks(B), blocks(left.shape[1])]
            + [whole(array) for array in [right, inverse, regular]],
            out_specs=blocks(cols),
        ),
        out_shape=jax.ShapeDtypeStruct((rows, cols), jnp.float32),
        compiler_params=pltpu.CompilerParams(vmem_limit_bytes=32 * 2**20),
        cost_estimate=pl.CostEstimate(flops=0, bytes_accessed=0, transcendentals=0),
        name="tile_rows",
    )(place, normals, strip, gram_cols, left, right, inverse, regular)


def after(value, earlier):
    return lax.optimization_barrier((value, earlier))[0]


def filter_matrix_of(filter_blocks, count):
    positions = jnp.arange(count, dtype=jnp.int32)
    lag = (positions[:, None] - positions[None, :])[:, None, :, None]
    own = filter_blocks[0][None, :, None, :]
    prior = filter_blocks[1][None, :, None, :]
    blocks = jnp.where(lag == 0, own, jnp.where(lag == 1, prior, 0.0))
    return blocks.reshape(count * P_SIZE, count * P_SIZE)


def row_strip_piece(normals, earlier, meanwhile):
    peers = lax.axis_size("col")
    chips = peers // 2
    size = normals.shape[0] // chips
    col_index = lax.axis_index("col")
    shares = after([normals[z * size : (z + 1) * size, :B] for z in range(1, chips)], earlier)
    arrived = [lax.ppermute(share, "col", [(0, 2 * z)]) for z, share in enumerate(shares, 1)]
    arrived = sum(after(arrived, meanwhile))
    piece = jnp.where(col_index == 0, normals[:size, :B], arrived)
    second = lax.ppermute(piece[size // 2 :], "col", [(c, c + 1) for c in range(0, peers, 2)])
    return jnp.where(col_index % 2 == 0, piece[: size // 2], second)


def doubled(value, bits, reached):
    row_peers, col_peers = lax.axis_size("row"), lax.axis_size("col")
    here = lax.axis_index("row") * col_peers + lax.axis_index("col")
    for bit in bits:
        pairs = [(i, i | bit) for i in reached if i | bit < row_peers * col_peers]
        got = lax.ppermute(value, ("row", "col"), pairs)
        value = jnp.where((here & bit) != 0, got, value)
        reached = reached + [to for _, to in pairs]
    return value, reached


def body(normals, design, filter_blocks, regular):
    rows_here, cols_here = normals.shape
    obs_here = design.shape[0]
    row_peers = lax.axis_size("row")
    row_index = lax.axis_index("row")
    col_index = lax.axis_index("col")
    col_peers = lax.axis_size("col")
    obs = row_peers * obs_here
    core = col_index % 2


    col_strip = lax.psum(jnp.where(row_index == 0, normals[:B], 0.0), "row")

    index_bits = [1 << i for i in range((row_peers * col_peers - 1).bit_length())]
    z_bits = [bit for bit in reversed(index_bits) if 1 < bit < col_peers]
    row_bits = [bit for bit in index_bits if bit >= col_peers]
    leading, reached = doubled(normals[:B, :B], z_bits, [0])

    chips = col_peers // 2
    chip = col_index // 2
    along = [design]
    for s in range(1, chips):
        along.append(lax.ppermute(design, "col", [(c, (c + 2 * s) % col_peers) for c in range(col_peers)]))
    along = jnp.stack(along)

    leading, reached = doubled(leading, row_bits, reached)
    lead = lax.dynamic_index_in_dim(along, chip, 0, keepdims=False)[:, :B]
    lead = lax.all_gather(lead, "row", axis=0, tiled=True)
    leading = jnp.concatenate([lead, leading], axis=0)

    sent = []
    for to in range(row_peers):
        far = lax.dynamic_index_in_dim(along, (chip - to) % chips, 0, keepdims=False)
        sent.append(jnp.concatenate([design, far], axis=1))
    sent = jnp.stack(sent)
    joined = lax.all_to_all(sent, "row", 0, 0, tiled=True)
    joined = joined.reshape(obs, 2 * cols_here)

    piece = row_strip_piece(normals, along, (leading, sent))
    strip = lax.all_gather(piece, "col", axis=0, tiled=True)

    leading, _ = doubled(leading, [1], reached)
    lead, corner = leading[:obs], leading[obs:]
    filters = filter_matrix_of(filter_blocks, obs // P_SIZE)
    lead_reg = regular[:B].reshape(1, B)
    inverse = corner_factor(corner, lead, filters, lead_reg)

    other = lax.ppermute(
        after(joined[:, cols_here:], inverse), "col", [(c, c ^ 1) for c in range(col_peers)]
    )
    own_reg = lax.dynamic_slice_in_dim(regular, col_index * cols_here, cols_here).reshape(1, cols_here)
    place = jnp.stack([row_index, col_index]).astype(jnp.int32)
    left, right, gram_cols = both_sides(
        place, joined, lead, other, col_strip, inverse, filters, own_reg, lead_reg
    )
    large = [pltpu.with_memory_space_constraint(array, pltpu.HBM) for array in (normals, strip, gram_cols, left)]
    return tile_rows(place, *large, right, inverse, own_reg)


def solution(mesh):
    in_specs = (P("row", "col"), P("row", "col"), P(), P())
    out_specs = P("row", "col")
    return jax.shard_map(body, mesh=mesh, in_specs=in_specs, out_specs=out_specs, check_vma=False)
```

```python
import functools

import jax
import jax.numpy as jnp
from jax import lax
from jax.experimental import pallas as pl
from jax.experimental.pallas import tpu as pltpu
from jax.sharding import PartitionSpec as P

B = 256
P_SIZE = 32
STRIP = 32
PIVOTS = 4
HIGHEST = lax.Precision.HIGHEST


def exact_dot(left, right, left_dim, right_dim):
    return lax.dot_general(
        left,
        right,
        (((left_dim,), (right_dim,)), ((), ())),
        precision=HIGHEST,
        preferred_element_type=jnp.float32,
    )


def split(value):
    high = value.astype(jnp.bfloat16)
    low = (value - high.astype(jnp.float32)).astype(jnp.bfloat16)
    return high, low


def split_dot(left, right):
    left_high, left_low = split(left)
    right_high, right_low = split(right)
    wide = functools.partial(jnp.dot, preferred_element_type=jnp.float32)
    return wide(left_high, right_high) + (wide(left_high, right_low) + wide(left_low, right_high))


def corner_kernel(block_ref, design_ref, filter_ref, regular_ref, inverse_ref, upper):
    filtered = exact_dot(filter_ref[...], design_ref[...], 1, 0)
    row_pos = lax.broadcasted_iota(jnp.int32, (B, B), 0)
    col_pos = lax.broadcasted_iota(jnp.int32, (B, B), 1)
    system = block_ref[...] + exact_dot(filtered, filtered, 0, 0)
    system = system + jnp.where(row_pos == col_pos, regular_ref[...], 0.0)
    identity = jnp.where(row_pos == col_pos, 1.0, 0.0)
    half = B // 2
    sub = lax.broadcasted_iota(jnp.int32, (STRIP, half), 0)
    lane = lax.broadcasted_iota(jnp.int32, (STRIP, half), 1)
    zero = jnp.zeros((STRIP, half), jnp.float32)
    for start in range(0, B, STRIP):
        rows = slice(start, start + STRIP)
        strip = jnp.concatenate([system[rows, :], identity[rows, :]], axis=1)
        if start:
            done = upper[:start, :]
            strip = strip - exact_dot(done[:, rows], done, 0, 0)
        low = 0 if start < half else half
        held = [strip[:, at : at + half] for at in range(low, low + 3 * half, half)]
        for first in range(0, STRIP, PIVOTS):
            at = start + first - low
            columns = [
                jnp.broadcast_to(held[0][:, at + q : at + q + 1], (STRIP, half)) for q in range(PIVOTS)
            ]
            pivot_rows = [[part[first + q : first + q + 1, :] for part in held] for q in range(PIVOTS)]
            for q in range(PIVOTS):
                j = first + q
                coef = jnp.where(sub > j, columns[q] * (1.0 / columns[q][j : j + 1, :]), 0.0)
                for m in range(q + 1, PIVOTS):
                    columns[m] = columns[m] - coef * columns[m][j : j + 1, :]
                    scale = coef[first + m : first + m + 1, :]
                    pivot_rows[m] = [
                        row - scale * other for row, other in zip(pivot_rows[m], pivot_rows[q])
                    ]
                held = [part - coef * row for part, row in zip(held, pivot_rows[q])]
        diag = jnp.sum(jnp.where(lane == sub + (start - low), held[0], 0.0), axis=1, keepdims=True)
        held = [part / jnp.sqrt(diag) for part in held]
        upper[rows, :] = jnp.concatenate([*held, zero] if low == 0 else [zero, *held], axis=1)
    inverse_ref[...] = upper[:, B:].T


def corner_factor(block, design, filter_matrix, regular):
    return pl.pallas_call(
        corner_kernel,
        out_shape=jax.ShapeDtypeStruct((B, B), jnp.float32),
        scratch_shapes=[pltpu.VMEM((B, 2 * B), jnp.float32)],
        compiler_params=pltpu.CompilerParams(vmem_limit_bytes=8 * 2**20),
        cost_estimate=pl.CostEstimate(flops=16 * 10**9, bytes_accessed=0, transcendentals=0),
        name="corner_factor",
    )(block, design, filter_matrix, regular)


def sides_kernel(
    place_ref,
    joined_ref,
    lead_ref,
    other_ref,
    strip_ref,
    inverse_ref,
    filter_ref,
    regular_ref,
    lead_reg_ref,
    left_ref,
    right_ref,
    gram_cols_ref,
):
    row_index, col_index = place_ref[0], place_ref[1]
    cols = right_ref.shape[1]
    obs = filter_ref.shape[0]
    core = lax.rem(col_index, 2)
    filtered = split_dot(filter_ref[...], joined_ref[:, : 2 * cols])
    here, rows_own = filtered[:, :cols], filtered[:, cols:]
    lead = split_dot(filter_ref[...], lead_ref[...])

    row_pos = lax.broadcasted_iota(jnp.int32, (B, cols), 0)
    col_pos = lax.broadcasted_iota(jnp.int32, (1, cols), 1) + col_index * cols
    strip = strip_ref[...] + split_dot(lead.T, here)
    strip = strip + jnp.where(row_pos == col_pos, regular_ref[...], 0.0)
    high, low = split(-split_dot(inverse_ref[...].T, strip))
    right_ref[:B, :] = high
    right_ref[B : 2 * B, :] = low
    right_ref[2 * B : 3 * B, :] = high
    high, low = split(jnp.where(col_pos < B, 0.0, here))
    right_ref[3 * B : 3 * B + obs, :] = high
    right_ref[3 * B + obs : 3 * B + 2 * obs, :] = low
    right_ref[3 * B + 2 * obs :, :] = high

    @pl.when(col_index == 0)
    def _():
        row_pos = lax.broadcasted_iota(jnp.int32, (B, B), 0)
        identity = jnp.where(row_pos == lax.broadcasted_iota(jnp.int32, (B, B), 1), 1.0, 0.0)
        identity = identity.astype(jnp.bfloat16)
        right_ref[:B, :B] = identity
        right_ref[B : 2 * B, :B] = jnp.zeros((B, B), jnp.bfloat16)
        right_ref[2 * B : 3 * B, :B] = identity

    rows_other = split_dot(filter_ref[...], other_ref[...])
    for half, value in ((core, rows_own), (1 - core, rows_other)):
        value = value.T
        high, low = split(value)
        rows = pl.ds(pl.multiple_of(half * cols, cols), cols)
        left_ref[rows, :obs] = high
        left_ref[rows, obs : 2 * obs] = high
        left_ref[rows, 2 * obs :] = low
        row_pos = lax.broadcasted_iota(jnp.int32, (cols, B), 0) + (2 * row_index + half) * cols
        lead_pos = lax.broadcasted_iota(jnp.int32, (cols, B), 1)
        gram_cols_ref[rows, :] = split_dot(value, lead) + jnp.where(
            row_pos == lead_pos, lead_reg_ref[...], 0.0
        )


def both_sides(place, joined, lead, other, strip, inverse, filter_matrix, regular, lead_reg):
    cols = other.shape[1]
    obs = filter_matrix.shape[0]
    vmem = pl.BlockSpec(memory_space=pltpu.VMEM)
    return pl.pallas_call(
        sides_kernel,
        in_specs=[pl.BlockSpec(memory_space=pltpu.SMEM)] + [vmem] * 8,
        out_specs=[vmem] * 3,
        out_shape=[
            pltpu.HBM((2 * cols, 3 * obs), jnp.bfloat16),
            jax.ShapeDtypeStruct((3 * (obs + B), cols), jnp.bfloat16),
            pltpu.HBM((2 * cols, B), jnp.float32),
        ],
        compiler_params=pltpu.CompilerParams(vmem_limit_bytes=26 * 2**20),
        cost_estimate=pl.CostEstimate(flops=0, bytes_accessed=0, transcendentals=0),
        name="both_sides",
    )(place, joined, lead, other, strip, inverse, filter_matrix, regular, lead_reg)


def block_rows(half):
    return max(size for size in range(128, 513, 128) if half % size == 0)


def tile_kernel(place_ref, normals_ref, strip_ref, gram_ref, left_ref, right_ref, inverse_ref, regular_ref, out_ref):
    step = pl.program_id(0)
    block, cols = out_ref.shape
    high, low = split(split_dot(strip_ref[...] + gram_ref[...], inverse_ref[...]))
    left = jnp.concatenate([high, high, low, left_ref[...]], axis=1)
    first_row = (place_ref[0] * pl.num_programs(0) + step) * block
    first_col = place_ref[1] * cols
    col_pos = lax.broadcasted_iota(jnp.int32, (1, cols), 1) + first_col
    keep = jnp.where(col_pos < B, 0.0, 1.0)
    out_ref[...] = normals_ref[...] * keep + jnp.dot(
        left, right_ref[...], preferred_element_type=jnp.float32
    )

    @pl.when((first_row < first_col + cols) & (first_col < first_row + block))
    def _():
        row_pos = lax.broadcasted_iota(jnp.int32, (block, cols), 0) + first_row
        on_diag = (row_pos == col_pos) & (col_pos >= B)
        out_ref[...] = out_ref[...] + jnp.where(on_diag, regular_ref[...], 0.0)


def tile_rows(place, normals, strip, gram_cols, left, right, inverse, regular):
    rows, cols = normals.shape
    block = block_rows(rows // 2)

    def whole(array):
        return pl.BlockSpec(array.shape, lambda i, place: (0,) * array.ndim, pipeline_mode=pl.Buffered(1))

    def blocks(width):
        return pl.BlockSpec((block, width), lambda i, place: (i, 0))

    return pl.pallas_call(
        tile_kernel,
        grid_spec=pltpu.PrefetchScalarGridSpec(
            num_scalar_prefetch=1,
            grid=(rows // block,),
            in_specs=[blocks(cols), blocks(B), blocks(B), blocks(left.shape[1])]
            + [whole(array) for array in [right, inverse, regular]],
            out_specs=blocks(cols),
        ),
        out_shape=jax.ShapeDtypeStruct((rows, cols), jnp.float32),
        compiler_params=pltpu.CompilerParams(vmem_limit_bytes=26 * 2**20),
        cost_estimate=pl.CostEstimate(flops=0, bytes_accessed=0, transcendentals=0),
        name="tile_rows",
    )(place, normals, strip, gram_cols, left, right, inverse, regular)


def after(value, earlier):
    return lax.optimization_barrier((value, earlier))[0]


def filter_matrix_of(filter_blocks, count):
    positions = jnp.arange(count, dtype=jnp.int32)
    lag = (positions[:, None] - positions[None, :])[:, None, :, None]
    own = filter_blocks[0][None, :, None, :]
    prior = filter_blocks[1][None, :, None, :]
    blocks = jnp.where(lag == 0, own, jnp.where(lag == 1, prior, 0.0))
    return blocks.reshape(count * P_SIZE, count * P_SIZE)


def row_strip_piece(normals, earlier, meanwhile):
    peers = lax.axis_size("col")
    chips = peers // 2
    size = normals.shape[0] // chips
    col_index = lax.axis_index("col")
    shares = after([normals[z * size : (z + 1) * size, :B] for z in range(1, chips)], earlier)
    arrived = [lax.ppermute(share, "col", [(0, 2 * z)]) for z, share in enumerate(shares, 1)]
    arrived = sum(after(arrived, meanwhile))
    piece = jnp.where(col_index == 0, normals[:size, :B], arrived)
    second = lax.ppermute(piece[size // 2 :], "col", [(c, c + 1) for c in range(0, peers, 2)])
    return jnp.where(col_index % 2 == 0, piece[: size // 2], second)


def doubled(value, bits, reached):
    row_peers, col_peers = lax.axis_size("row"), lax.axis_size("col")
    here = lax.axis_index("row") * col_peers + lax.axis_index("col")
    for bit in bits:
        pairs = [(i, i | bit) for i in reached if i | bit < row_peers * col_peers]
        got = lax.ppermute(value, ("row", "col"), pairs)
        value = jnp.where((here & bit) != 0, got, value)
        reached = reached + [to for _, to in pairs]
    return value, reached


def body(normals, design, filter_blocks, regular):
    rows_here, cols_here = normals.shape
    obs_here = design.shape[0]
    row_peers = lax.axis_size("row")
    row_index = lax.axis_index("row")
    col_index = lax.axis_index("col")
    col_peers = lax.axis_size("col")
    obs = row_peers * obs_here
    core = col_index % 2


    col_strip = lax.psum(jnp.where(row_index == 0, normals[:B], 0.0), "row")

    index_bits = [1 << i for i in range((row_peers * col_peers - 1).bit_length())]
    z_bits = [bit for bit in reversed(index_bits) if 1 < bit < col_peers]
    row_bits = [bit for bit in index_bits if bit >= col_peers]
    leading, reached = doubled(normals[:B, :B], z_bits, [0])

    chips = col_peers // 2
    chip = col_index // 2
    along = [design]
    for s in range(1, chips):
        along.append(lax.ppermute(design, "col", [(c, (c + 2 * s) % col_peers) for c in range(col_peers)]))
    along = jnp.stack(along)

    leading, reached = doubled(leading, row_bits, reached)
    lead = lax.dynamic_index_in_dim(along, chip, 0, keepdims=False)[:, :B]
    lead = lax.all_gather(lead, "row", axis=0, tiled=True)
    leading = jnp.concatenate([lead, leading], axis=0)

    sent = []
    for to in range(row_peers):
        far = lax.dynamic_index_in_dim(along, (chip - to) % chips, 0, keepdims=False)
        sent.append(jnp.concatenate([design, far], axis=1))
    sent = jnp.stack(sent)
    joined = lax.all_to_all(sent, "row", 0, 0, tiled=True)
    joined = joined.reshape(obs, 2 * cols_here)

    piece = row_strip_piece(normals, along, (leading, sent))
    strip = lax.all_gather(piece, "col", axis=0, tiled=True)

    leading, _ = doubled(leading, [1], reached)
    lead, corner = leading[:obs], leading[obs:]
    filters = filter_matrix_of(filter_blocks, obs // P_SIZE)
    lead_reg = regular[:B].reshape(1, B)
    inverse = corner_factor(corner, lead, filters, lead_reg)

    other = lax.ppermute(
        after(joined[:, cols_here:], inverse), "col", [(c, c ^ 1) for c in range(col_peers)]
    )
    own_reg = lax.dynamic_slice_in_dim(regular, col_index * cols_here, cols_here).reshape(1, cols_here)
    place = jnp.stack([row_index, col_index]).astype(jnp.int32)
    left, right, gram_cols = both_sides(
        place, joined, lead, other, col_strip, inverse, filters, own_reg, lead_reg
    )
    large = [pltpu.with_memory_space_constraint(array, pltpu.HBM) for array in (strip, gram_cols, left)]
    fetched = pltpu.with_memory_space_constraint(normals, pltpu.VMEM)
    return tile_rows(place, fetched, *large, right, inverse, own_reg)


def solution(mesh):
    in_specs = (P("row", "col"), P("row", "col"), P(), P())
    out_specs = P("row", "col")
    return jax.shard_map(body, mesh=mesh, in_specs=in_specs, out_specs=out_specs, check_vma=False)
```

```python
import functools

import jax
import jax.numpy as jnp
from jax import lax
from jax.experimental import pallas as pl
from jax.experimental.pallas import tpu as pltpu
from jax.sharding import PartitionSpec as P

B = 256
P_SIZE = 32
STRIP = 32
PIVOTS = 4
HIGHEST = lax.Precision.HIGHEST


def exact_dot(left, right, left_dim, right_dim):
    return lax.dot_general(
        left,
        right,
        (((left_dim,), (right_dim,)), ((), ())),
        precision=HIGHEST,
        preferred_element_type=jnp.float32,
    )


def split(value):
    high = value.astype(jnp.bfloat16)
    low = (value - high.astype(jnp.float32)).astype(jnp.bfloat16)
    return high, low


def split_dot(left, right):
    left_high, left_low = split(left)
    right_high, right_low = split(right)
    wide = functools.partial(jnp.dot, preferred_element_type=jnp.float32)
    return wide(left_high, right_high) + (wide(left_high, right_low) + wide(left_low, right_high))


def corner_kernel(block_ref, design_ref, filter_ref, regular_ref, inverse_ref, upper):
    filtered = exact_dot(filter_ref[...], design_ref[...], 1, 0)
    row_pos = lax.broadcasted_iota(jnp.int32, (B, B), 0)
    col_pos = lax.broadcasted_iota(jnp.int32, (B, B), 1)
    system = block_ref[...] + exact_dot(filtered, filtered, 0, 0)
    system = system + jnp.where(row_pos == col_pos, regular_ref[...], 0.0)
    identity = jnp.where(row_pos == col_pos, 1.0, 0.0)
    half = B // 2
    sub = lax.broadcasted_iota(jnp.int32, (STRIP, half), 0)
    lane = lax.broadcasted_iota(jnp.int32, (STRIP, half), 1)
    zero = jnp.zeros((STRIP, half), jnp.float32)
    for start in range(0, B, STRIP):
        rows = slice(start, start + STRIP)
        strip = jnp.concatenate([system[rows, :], identity[rows, :]], axis=1)
        if start:
            done = upper[:start, :]
            strip = strip - exact_dot(done[:, rows], done, 0, 0)
        low = 0 if start < half else half
        held = [strip[:, at : at + half] for at in range(low, low + 3 * half, half)]
        for first in range(0, STRIP, PIVOTS):
            at = start + first - low
            columns = [
                jnp.broadcast_to(held[0][:, at + q : at + q + 1], (STRIP, half)) for q in range(PIVOTS)
            ]
            pivot_rows = [[part[first + q : first + q + 1, :] for part in held] for q in range(PIVOTS)]
            for q in range(PIVOTS):
                j = first + q
                coef = jnp.where(sub > j, columns[q] * (1.0 / columns[q][j : j + 1, :]), 0.0)
                for m in range(q + 1, PIVOTS):
                    columns[m] = columns[m] - coef * columns[m][j : j + 1, :]
                    scale = coef[first + m : first + m + 1, :]
                    pivot_rows[m] = [
                        row - scale * other for row, other in zip(pivot_rows[m], pivot_rows[q])
                    ]
                held = [part - coef * row for part, row in zip(held, pivot_rows[q])]
        diag = jnp.sum(jnp.where(lane == sub + (start - low), held[0], 0.0), axis=1, keepdims=True)
        held = [part / jnp.sqrt(diag) for part in held]
        upper[rows, :] = jnp.concatenate([*held, zero] if low == 0 else [zero, *held], axis=1)
    inverse_ref[...] = upper[:, B:].T


def corner_factor(block, design, filter_matrix, regular):
    return pl.pallas_call(
        corner_kernel,
        out_shape=jax.ShapeDtypeStruct((B, B), jnp.float32),
        scratch_shapes=[pltpu.VMEM((B, 2 * B), jnp.float32)],
        compiler_params=pltpu.CompilerParams(vmem_limit_bytes=8 * 2**20),
        cost_estimate=pl.CostEstimate(flops=0, bytes_accessed=0, transcendentals=0),
        name="corner_factor",
    )(block, design, filter_matrix, regular)


def sides_kernel(
    place_ref,
    joined_ref,
    lead_ref,
    other_ref,
    strip_ref,
    inverse_ref,
    filter_ref,
    regular_ref,
    lead_reg_ref,
    left_ref,
    right_ref,
    gram_cols_ref,
):
    row_index, col_index = place_ref[0], place_ref[1]
    cols = right_ref.shape[1]
    obs = filter_ref.shape[0]
    core = lax.rem(col_index, 2)
    filtered = split_dot(filter_ref[...], joined_ref[:, : 2 * cols])
    here, rows_own = filtered[:, :cols], filtered[:, cols:]
    lead = split_dot(filter_ref[...], lead_ref[...])

    row_pos = lax.broadcasted_iota(jnp.int32, (B, cols), 0)
    col_pos = lax.broadcasted_iota(jnp.int32, (1, cols), 1) + col_index * cols
    strip = strip_ref[...] + split_dot(lead.T, here)
    strip = strip + jnp.where(row_pos == col_pos, regular_ref[...], 0.0)
    high, low = split(-split_dot(inverse_ref[...].T, strip))
    right_ref[:B, :] = high
    right_ref[B : 2 * B, :] = low
    right_ref[2 * B : 3 * B, :] = high
    high, low = split(jnp.where(col_pos < B, 0.0, here))
    right_ref[3 * B : 3 * B + obs, :] = high
    right_ref[3 * B + obs : 3 * B + 2 * obs, :] = low
    right_ref[3 * B + 2 * obs :, :] = high

    @pl.when(col_index == 0)
    def _():
        row_pos = lax.broadcasted_iota(jnp.int32, (B, B), 0)
        identity = jnp.where(row_pos == lax.broadcasted_iota(jnp.int32, (B, B), 1), 1.0, 0.0)
        identity = identity.astype(jnp.bfloat16)
        right_ref[:B, :B] = identity
        right_ref[B : 2 * B, :B] = jnp.zeros((B, B), jnp.bfloat16)
        right_ref[2 * B : 3 * B, :B] = identity

    rows_other = split_dot(filter_ref[...], other_ref[...])
    for half, value in ((core, rows_own), (1 - core, rows_other)):
        value = value.T
        high, low = split(value)
        rows = pl.ds(pl.multiple_of(half * cols, cols), cols)
        left_ref[rows, :obs] = high
        left_ref[rows, obs : 2 * obs] = high
        left_ref[rows, 2 * obs :] = low
        row_pos = lax.broadcasted_iota(jnp.int32, (cols, B), 0) + (2 * row_index + half) * cols
        lead_pos = lax.broadcasted_iota(jnp.int32, (cols, B), 1)
        gram_cols_ref[rows, :] = split_dot(value, lead) + jnp.where(
            row_pos == lead_pos, lead_reg_ref[...], 0.0
        )


def both_sides(place, joined, lead, other, strip, inverse, filter_matrix, regular, lead_reg):
    cols = other.shape[1]
    obs = filter_matrix.shape[0]
    vmem = pl.BlockSpec(memory_space=pltpu.VMEM)
    return pl.pallas_call(
        sides_kernel,
        in_specs=[pl.BlockSpec(memory_space=pltpu.SMEM)] + [vmem] * 8,
        out_specs=[vmem] * 3,
        out_shape=[
            pltpu.HBM((2 * cols, 3 * obs), jnp.bfloat16),
            jax.ShapeDtypeStruct((3 * (obs + B), cols), jnp.bfloat16),
            pltpu.HBM((2 * cols, B), jnp.float32),
        ],
        compiler_params=pltpu.CompilerParams(vmem_limit_bytes=26 * 2**20),
        cost_estimate=pl.CostEstimate(flops=0, bytes_accessed=0, transcendentals=0),
        name="both_sides",
    )(place, joined, lead, other, strip, inverse, filter_matrix, regular, lead_reg)


def block_rows(half):
    return max(size for size in range(128, 513, 128) if half % size == 0)


def tile_kernel(place_ref, normals_ref, strip_ref, gram_ref, left_ref, right_ref, inverse_ref, regular_ref, out_ref):
    step = pl.program_id(0)
    block, cols = out_ref.shape
    high, low = split(split_dot(strip_ref[...] + gram_ref[...], inverse_ref[...]))
    left = jnp.concatenate([high, high, low, left_ref[...]], axis=1)
    first_row = (place_ref[0] * pl.num_programs(0) + step) * block
    first_col = place_ref[1] * cols
    col_pos = lax.broadcasted_iota(jnp.int32, (1, cols), 1) + first_col
    keep = jnp.where(col_pos < B, 0.0, 1.0)
    width = max(size for size in range(128, 513, 128) if cols % size == 0)
    for at in range(0, cols, width):
        here = slice(at, at + width)
        out_ref[:, here] = normals_ref[:, here] * keep[:, here] + jnp.dot(
            left, right_ref[:, here], preferred_element_type=jnp.float32
        )

    @pl.when((first_row < first_col + cols) & (first_col < first_row + block))
    def _():
        row_pos = lax.broadcasted_iota(jnp.int32, (block, cols), 0) + first_row
        on_diag = (row_pos == col_pos) & (col_pos >= B)
        out_ref[...] = out_ref[...] + jnp.where(on_diag, regular_ref[...], 0.0)


def tile_rows(place, normals, strip, gram_cols, left, right, inverse, regular):
    rows, cols = normals.shape
    block = block_rows(rows // 2)

    def whole(array):
        return pl.BlockSpec(array.shape, lambda i, place: (0,) * array.ndim, pipeline_mode=pl.Buffered(1))

    def blocks(width):
        return pl.BlockSpec((block, width), lambda i, place: (i, 0))

    return pl.pallas_call(
        tile_kernel,
        grid_spec=pltpu.PrefetchScalarGridSpec(
            num_scalar_prefetch=1,
            grid=(rows // block,),
            in_specs=[blocks(cols), blocks(B), blocks(B), blocks(left.shape[1])]
            + [whole(array) for array in [right, inverse, regular]],
            out_specs=blocks(cols),
        ),
        out_shape=jax.ShapeDtypeStruct((rows, cols), jnp.float32),
        compiler_params=pltpu.CompilerParams(vmem_limit_bytes=26 * 2**20),
        cost_estimate=pl.CostEstimate(flops=0, bytes_accessed=0, transcendentals=0),
        name="tile_rows",
    )(place, normals, strip, gram_cols, left, right, inverse, regular)


def after(value, earlier):
    return lax.optimization_barrier((value, earlier))[0]


def filter_matrix_of(filter_blocks, count):
    positions = jnp.arange(count, dtype=jnp.int32)
    lag = (positions[:, None] - positions[None, :])[:, None, :, None]
    own = filter_blocks[0][None, :, None, :]
    prior = filter_blocks[1][None, :, None, :]
    blocks = jnp.where(lag == 0, own, jnp.where(lag == 1, prior, 0.0))
    return blocks.reshape(count * P_SIZE, count * P_SIZE)


def row_strip_piece(normals, earlier, meanwhile):
    peers = lax.axis_size("col")
    chips = peers // 2
    size = normals.shape[0] // chips
    col_index = lax.axis_index("col")
    shares = after([normals[z * size : (z + 1) * size, :B] for z in range(1, chips)], earlier)
    arrived = [lax.ppermute(share, "col", [(0, 2 * z)]) for z, share in enumerate(shares, 1)]
    arrived = sum(after(arrived, meanwhile))
    piece = jnp.where(col_index == 0, normals[:size, :B], arrived)
    second = lax.ppermute(piece[size // 2 :], "col", [(c, c + 1) for c in range(0, peers, 2)])
    return jnp.where(col_index % 2 == 0, piece[: size // 2], second)


def doubled(value, bits, reached):
    row_peers, col_peers = lax.axis_size("row"), lax.axis_size("col")
    here = lax.axis_index("row") * col_peers + lax.axis_index("col")
    for bit in bits:
        pairs = [(i, i | bit) for i in reached if i | bit < row_peers * col_peers]
        got = lax.ppermute(value, ("row", "col"), pairs)
        value = jnp.where((here & bit) != 0, got, value)
        reached = reached + [to for _, to in pairs]
    return value, reached


def body(normals, design, filter_blocks, regular):
    rows_here, cols_here = normals.shape
    obs_here = design.shape[0]
    row_peers = lax.axis_size("row")
    row_index = lax.axis_index("row")
    col_index = lax.axis_index("col")
    col_peers = lax.axis_size("col")
    obs = row_peers * obs_here
    core = col_index % 2


    col_strip = lax.psum(jnp.where(row_index == 0, normals[:B], 0.0), "row")

    index_bits = [1 << i for i in range((row_peers * col_peers - 1).bit_length())]
    z_bits = [bit for bit in reversed(index_bits) if 1 < bit < col_peers]
    row_bits = [bit for bit in index_bits if bit >= col_peers]
    leading, reached = doubled(normals[:B, :B], z_bits, [0])
    along_z = leading

    chips = col_peers // 2
    chip = col_index // 2
    along = [design]
    for s in range(1, chips):
        along.append(lax.ppermute(design, "col", [(c, (c + 2 * s) % col_peers) for c in range(col_peers)]))
    along = jnp.stack(along)

    sent = []
    for to in range(row_peers):
        far = lax.dynamic_index_in_dim(along, (chip - to) % chips, 0, keepdims=False)
        sent.append(jnp.concatenate([design, far], axis=1))
    sent = jnp.stack(sent)
    leading, reached = doubled(leading, row_bits, reached)
    lead = lax.dynamic_index_in_dim(along, chip, 0, keepdims=False)[:, :B]
    lead = lax.all_gather(after(lead, sent), "row", axis=0, tiled=True)
    leading = jnp.concatenate([lead, leading], axis=0)

    joined = lax.all_to_all(sent, "row", 0, 0, tiled=True)
    joined = joined.reshape(obs, 2 * cols_here)

    piece = row_strip_piece(normals, along, (along_z, joined))
    strip = lax.all_gather(piece, "col", axis=0, tiled=True)

    leading, _ = doubled(leading, [1], reached)
    lead, corner = leading[:obs], leading[obs:]
    filters = filter_matrix_of(filter_blocks, obs // P_SIZE)
    lead_reg = regular[:B].reshape(1, B)
    inverse = corner_factor(corner, lead, filters, lead_reg)

    other = lax.ppermute(joined[:, cols_here:], "col", [(c, c ^ 1) for c in range(col_peers)])
    own_reg = lax.dynamic_slice_in_dim(regular, col_index * cols_here, cols_here).reshape(1, cols_here)
    place = jnp.stack([row_index, col_index]).astype(jnp.int32)
    left, right, gram_cols = both_sides(
        place, joined, lead, other, col_strip, inverse, filters, own_reg, lead_reg
    )
    large = [pltpu.with_memory_space_constraint(array, pltpu.HBM) for array in (normals, strip, gram_cols, left)]
    return tile_rows(place, *large, right, inverse, own_reg)


def solution(mesh):
    in_specs = (P("row", "col"), P("row", "col"), P(), P())
    out_specs = P("row", "col")
    return jax.shard_map(body, mesh=mesh, in_specs=in_specs, out_specs=out_specs, check_vma=False)
```

```python
import functools

import jax
import jax.numpy as jnp
from jax import lax
from jax.experimental import pallas as pl
from jax.experimental.pallas import tpu as pltpu
from jax.sharding import PartitionSpec as P

B = 256
P_SIZE = 32
STRIP = 32
PIVOTS = 4
HIGHEST = lax.Precision.HIGHEST


def exact_dot(left, right, left_dim, right_dim):
    return lax.dot_general(
        left,
        right,
        (((left_dim,), (right_dim,)), ((), ())),
        precision=HIGHEST,
        preferred_element_type=jnp.float32,
    )


def split(value):
    high = value.astype(jnp.bfloat16)
    low = (value - high.astype(jnp.float32)).astype(jnp.bfloat16)
    return high, low


def split_dot(left, right):
    left_high, left_low = split(left)
    right_high, right_low = split(right)
    wide = functools.partial(jnp.dot, preferred_element_type=jnp.float32)
    return wide(left_high, right_high) + (wide(left_high, right_low) + wide(left_low, right_high))


def corner_kernel(block_ref, design_ref, filter_ref, regular_ref, inverse_ref, upper):
    filtered = exact_dot(filter_ref[...], design_ref[...], 1, 0)
    row_pos = lax.broadcasted_iota(jnp.int32, (B, B), 0)
    col_pos = lax.broadcasted_iota(jnp.int32, (B, B), 1)
    system = block_ref[...] + exact_dot(filtered, filtered, 0, 0)
    system = system + jnp.where(row_pos == col_pos, regular_ref[...], 0.0)
    identity = jnp.where(row_pos == col_pos, 1.0, 0.0)
    half = B // 2
    sub = lax.broadcasted_iota(jnp.int32, (STRIP, half), 0)
    lane = lax.broadcasted_iota(jnp.int32, (STRIP, half), 1)
    zero = jnp.zeros((STRIP, half), jnp.float32)
    for start in range(0, B, STRIP):
        rows = slice(start, start + STRIP)
        strip = jnp.concatenate([system[rows, :], identity[rows, :]], axis=1)
        if start:
            done = upper[:start, :]
            strip = strip - exact_dot(done[:, rows], done, 0, 0)
        low = 0 if start < half else half
        held = [strip[:, at : at + half] for at in range(low, low + 3 * half, half)]
        for first in range(0, STRIP, PIVOTS):
            at = start + first - low
            columns = [
                jnp.broadcast_to(held[0][:, at + q : at + q + 1], (STRIP, half)) for q in range(PIVOTS)
            ]
            pivot_rows = [[part[first + q : first + q + 1, :] for part in held] for q in range(PIVOTS)]
            for q in range(PIVOTS):
                j = first + q
                coef = jnp.where(sub > j, columns[q] * (1.0 / columns[q][j : j + 1, :]), 0.0)
                for m in range(q + 1, PIVOTS):
                    columns[m] = columns[m] - coef * columns[m][j : j + 1, :]
                    scale = coef[first + m : first + m + 1, :]
                    pivot_rows[m] = [
                        row - scale * other for row, other in zip(pivot_rows[m], pivot_rows[q])
                    ]
                held = [part - coef * row for part, row in zip(held, pivot_rows[q])]
        diag = jnp.sum(jnp.where(lane == sub + (start - low), held[0], 0.0), axis=1, keepdims=True)
        held = [part / jnp.sqrt(diag) for part in held]
        upper[rows, :] = jnp.concatenate([*held, zero] if low == 0 else [zero, *held], axis=1)
    inverse_ref[...] = upper[:, B:].T


def corner_factor(block, design, filter_matrix, regular):
    return pl.pallas_call(
        corner_kernel,
        out_shape=jax.ShapeDtypeStruct((B, B), jnp.float32),
        scratch_shapes=[pltpu.VMEM((B, 2 * B), jnp.float32)],
        compiler_params=pltpu.CompilerParams(vmem_limit_bytes=8 * 2**20),
        cost_estimate=pl.CostEstimate(flops=0, bytes_accessed=0, transcendentals=0),
        name="corner_factor",
    )(block, design, filter_matrix, regular)


def sides_kernel(
    place_ref,
    joined_ref,
    lead_ref,
    other_ref,
    strip_ref,
    inverse_ref,
    filter_ref,
    regular_ref,
    lead_reg_ref,
    left_ref,
    right_ref,
    gram_cols_ref,
):
    row_index, col_index = place_ref[0], place_ref[1]
    cols = right_ref.shape[1]
    obs = filter_ref.shape[0]
    core = lax.rem(col_index, 2)
    filtered = split_dot(filter_ref[...], joined_ref[:, : 2 * cols])
    here, rows_own = filtered[:, :cols], filtered[:, cols:]
    lead = split_dot(filter_ref[...], lead_ref[...])

    row_pos = lax.broadcasted_iota(jnp.int32, (B, cols), 0)
    col_pos = lax.broadcasted_iota(jnp.int32, (1, cols), 1) + col_index * cols
    strip = strip_ref[...] + split_dot(lead.T, here)
    strip = strip + jnp.where(row_pos == col_pos, regular_ref[...], 0.0)
    high, low = split(-split_dot(inverse_ref[...].T, strip))
    right_ref[:B, :] = high
    right_ref[B : 2 * B, :] = low
    right_ref[2 * B : 3 * B, :] = high
    high, low = split(jnp.where(col_pos < B, 0.0, here))
    right_ref[3 * B : 3 * B + obs, :] = high
    right_ref[3 * B + obs : 3 * B + 2 * obs, :] = low
    right_ref[3 * B + 2 * obs :, :] = high

    @pl.when(col_index == 0)
    def _():
        row_pos = lax.broadcasted_iota(jnp.int32, (B, B), 0)
        identity = jnp.where(row_pos == lax.broadcasted_iota(jnp.int32, (B, B), 1), 1.0, 0.0)
        identity = identity.astype(jnp.bfloat16)
        right_ref[:B, :B] = identity
        right_ref[B : 2 * B, :B] = jnp.zeros((B, B), jnp.bfloat16)
        right_ref[2 * B : 3 * B, :B] = identity

    rows_other = split_dot(filter_ref[...], other_ref[...])
    for half, value in ((core, rows_own), (1 - core, rows_other)):
        value = value.T
        high, low = split(value)
        rows = pl.ds(pl.multiple_of(half * cols, cols), cols)
        left_ref[rows, :obs] = high
        left_ref[rows, obs : 2 * obs] = high
        left_ref[rows, 2 * obs :] = low
        row_pos = lax.broadcasted_iota(jnp.int32, (cols, B), 0) + (2 * row_index + half) * cols
        lead_pos = lax.broadcasted_iota(jnp.int32, (cols, B), 1)
        gram_cols_ref[rows, :] = split_dot(value, lead) + jnp.where(
            row_pos == lead_pos, lead_reg_ref[...], 0.0
        )


def both_sides(place, joined, lead, other, strip, inverse, filter_matrix, regular, lead_reg):
    cols = other.shape[1]
    obs = filter_matrix.shape[0]
    vmem = pl.BlockSpec(memory_space=pltpu.VMEM)
    return pl.pallas_call(
        sides_kernel,
        in_specs=[pl.BlockSpec(memory_space=pltpu.SMEM)] + [vmem] * 8,
        out_specs=[vmem] * 3,
        out_shape=[
            pltpu.HBM((2 * cols, 3 * obs), jnp.bfloat16),
            pltpu.HBM((3 * (obs + B), cols), jnp.bfloat16),
            pltpu.HBM((2 * cols, B), jnp.float32),
        ],
        compiler_params=pltpu.CompilerParams(vmem_limit_bytes=26 * 2**20),
        cost_estimate=pl.CostEstimate(flops=0, bytes_accessed=0, transcendentals=0),
        name="both_sides",
    )(place, joined, lead, other, strip, inverse, filter_matrix, regular, lead_reg)


def block_rows(half):
    return max(size for size in range(128, 513, 128) if half % size == 0)


def tile_kernel(place_ref, normals_ref, strip_ref, gram_ref, left_ref, right_ref, inverse_ref, regular_ref, out_ref):
    step = pl.program_id(0)
    block, cols = out_ref.shape
    high, low = split(split_dot(strip_ref[...] + gram_ref[...], inverse_ref[...]))
    left = jnp.concatenate([high, high, low, left_ref[...]], axis=1)
    first_row = (place_ref[0] * pl.num_programs(0) + step) * block
    first_col = place_ref[1] * cols
    col_pos = lax.broadcasted_iota(jnp.int32, (1, cols), 1) + first_col
    keep = jnp.where(col_pos < B, 0.0, 1.0)
    width = max(size for size in range(128, 513, 128) if cols % size == 0)
    for at in range(0, cols, width):
        here = slice(at, at + width)
        out_ref[:, here] = normals_ref[:, here] * keep[:, here] + jnp.dot(
            left, right_ref[:, here], preferred_element_type=jnp.float32
        )

    @pl.when((first_row < first_col + cols) & (first_col < first_row + block))
    def _():
        row_pos = lax.broadcasted_iota(jnp.int32, (block, cols), 0) + first_row
        on_diag = (row_pos == col_pos) & (col_pos >= B)
        out_ref[...] = out_ref[...] + jnp.where(on_diag, regular_ref[...], 0.0)


def tile_rows(place, normals, strip, gram_cols, left, right, inverse, regular):
    rows, cols = normals.shape
    block = block_rows(rows // 2)

    def whole(array):
        return pl.BlockSpec(array.shape, lambda i, place: (0,) * array.ndim, pipeline_mode=pl.Buffered(1))

    def blocks(width):
        return pl.BlockSpec((block, width), lambda i, place: (i, 0))

    return pl.pallas_call(
        tile_kernel,
        grid_spec=pltpu.PrefetchScalarGridSpec(
            num_scalar_prefetch=1,
            grid=(rows // block,),
            in_specs=[blocks(cols), blocks(B), blocks(B), blocks(left.shape[1])]
            + [whole(array) for array in [right, inverse, regular]],
            out_specs=blocks(cols),
        ),
        out_shape=jax.ShapeDtypeStruct((rows, cols), jnp.float32),
        compiler_params=pltpu.CompilerParams(vmem_limit_bytes=26 * 2**20),
        cost_estimate=pl.CostEstimate(flops=0, bytes_accessed=0, transcendentals=0),
        name="tile_rows",
    )(place, normals, strip, gram_cols, left, right, inverse, regular)


def after(value, earlier):
    return lax.optimization_barrier((value, earlier))[0]


def filter_matrix_of(filter_blocks, count):
    positions = jnp.arange(count, dtype=jnp.int32)
    lag = (positions[:, None] - positions[None, :])[:, None, :, None]
    own = filter_blocks[0][None, :, None, :]
    prior = filter_blocks[1][None, :, None, :]
    blocks = jnp.where(lag == 0, own, jnp.where(lag == 1, prior, 0.0))
    return blocks.reshape(count * P_SIZE, count * P_SIZE)


def row_strip_piece(normals, earlier, meanwhile):
    peers = lax.axis_size("col")
    chips = peers // 2
    size = normals.shape[0] // chips
    col_index = lax.axis_index("col")
    shares = after([normals[z * size : (z + 1) * size, :B] for z in range(1, chips)], earlier)
    arrived = [lax.ppermute(share, "col", [(0, 2 * z)]) for z, share in enumerate(shares, 1)]
    arrived = sum(after(arrived, meanwhile))
    piece = jnp.where(col_index == 0, normals[:size, :B], arrived)
    second = lax.ppermute(piece[size // 2 :], "col", [(c, c + 1) for c in range(0, peers, 2)])
    return jnp.where(col_index % 2 == 0, piece[: size // 2], second)


def doubled(value, bits, reached):
    row_peers, col_peers = lax.axis_size("row"), lax.axis_size("col")
    here = lax.axis_index("row") * col_peers + lax.axis_index("col")
    for bit in bits:
        pairs = [(i, i | bit) for i in reached if i | bit < row_peers * col_peers]
        got = lax.ppermute(value, ("row", "col"), pairs)
        value = jnp.where((here & bit) != 0, got, value)
        reached = reached + [to for _, to in pairs]
    return value, reached


def body(normals, design, filter_blocks, regular):
    rows_here, cols_here = normals.shape
    obs_here = design.shape[0]
    row_peers = lax.axis_size("row")
    row_index = lax.axis_index("row")
    col_index = lax.axis_index("col")
    col_peers = lax.axis_size("col")
    obs = row_peers * obs_here
    core = col_index % 2


    col_strip = lax.psum(jnp.where(row_index == 0, normals[:B], 0.0), "row")

    index_bits = [1 << i for i in range((row_peers * col_peers - 1).bit_length())]
    z_bits = [bit for bit in reversed(index_bits) if 1 < bit < col_peers]
    row_bits = [bit for bit in index_bits if bit >= col_peers]
    leading, reached = doubled(normals[:B, :B], z_bits, [0])
    along_z = leading

    chips = col_peers // 2
    chip = col_index // 2
    along = [design]
    for s in range(1, chips):
        along.append(lax.ppermute(design, "col", [(c, (c + 2 * s) % col_peers) for c in range(col_peers)]))
    along = jnp.stack(along)

    sent = []
    for to in range(row_peers):
        far = lax.dynamic_index_in_dim(along, (chip - to) % chips, 0, keepdims=False)
        sent.append(jnp.concatenate([design, far], axis=1))
    sent = jnp.stack(sent)
    leading, reached = doubled(leading, row_bits, reached)
    lead = lax.dynamic_index_in_dim(along, chip, 0, keepdims=False)[:, :B]
    lead = lax.all_gather(after(lead, sent), "row", axis=0, tiled=True)
    leading = jnp.concatenate([lead, leading], axis=0)

    joined = lax.all_to_all(sent, "row", 0, 0, tiled=True)
    joined = joined.reshape(obs, 2 * cols_here)

    piece = row_strip_piece(normals, along, (along_z, joined, lead))
    strip = lax.all_gather(piece, "col", axis=0, tiled=True)

    leading, _ = doubled(leading, [1], reached)
    lead, corner = leading[:obs], leading[obs:]
    filters = filter_matrix_of(filter_blocks, obs // P_SIZE)
    lead_reg = regular[:B].reshape(1, B)
    inverse = corner_factor(corner, lead, filters, lead_reg)

    other = lax.ppermute(joined[:, cols_here:], "col", [(c, c ^ 1) for c in range(col_peers)])
    own_reg = lax.dynamic_slice_in_dim(regular, col_index * cols_here, cols_here).reshape(1, cols_here)
    place = jnp.stack([row_index, col_index]).astype(jnp.int32)
    left, right, gram_cols = both_sides(
        place, joined, lead, other, col_strip, inverse, filters, own_reg, lead_reg
    )
    large = [normals, strip, gram_cols, left, right]
    large = [pltpu.with_memory_space_constraint(array, pltpu.HBM) for array in large]
    return tile_rows(place, *large, inverse, own_reg)


def solution(mesh):
    in_specs = (P("row", "col"), P("row", "col"), P(), P())
    out_specs = P("row", "col")
    return jax.shard_map(body, mesh=mesh, in_specs=in_specs, out_specs=out_specs, check_vma=False)
```

```python
import functools

import jax
import jax.numpy as jnp
from jax import lax
from jax.experimental import pallas as pl
from jax.experimental.pallas import tpu as pltpu
from jax.sharding import PartitionSpec as P

B = 256
P_SIZE = 32
STRIP = 32
PIVOTS = 4
HIGHEST = lax.Precision.HIGHEST


def exact_dot(left, right, left_dim, right_dim):
    return lax.dot_general(
        left,
        right,
        (((left_dim,), (right_dim,)), ((), ())),
        precision=HIGHEST,
        preferred_element_type=jnp.float32,
    )


def split(value):
    high = value.astype(jnp.bfloat16)
    low = (value - high.astype(jnp.float32)).astype(jnp.bfloat16)
    return high, low


def split_dot(left, right):
    left_high, left_low = split(left)
    right_high, right_low = split(right)
    wide = functools.partial(jnp.dot, preferred_element_type=jnp.float32)
    return wide(left_high, right_high) + (wide(left_high, right_low) + wide(left_low, right_high))


def corner_kernel(block_ref, design_ref, filter_ref, regular_ref, inverse_ref, upper):
    filtered = exact_dot(filter_ref[...], design_ref[...], 1, 0)
    row_pos = lax.broadcasted_iota(jnp.int32, (B, B), 0)
    col_pos = lax.broadcasted_iota(jnp.int32, (B, B), 1)
    system = block_ref[...] + exact_dot(filtered, filtered, 0, 0)
    system = system + jnp.where(row_pos == col_pos, regular_ref[...], 0.0)
    identity = jnp.where(row_pos == col_pos, 1.0, 0.0)
    half = B // 2
    sub = lax.broadcasted_iota(jnp.int32, (STRIP, half), 0)
    lane = lax.broadcasted_iota(jnp.int32, (STRIP, half), 1)
    zero = jnp.zeros((STRIP, half), jnp.float32)
    for start in range(0, B, STRIP):
        rows = slice(start, start + STRIP)
        strip = jnp.concatenate([system[rows, :], identity[rows, :]], axis=1)
        if start:
            done = upper[:start, :]
            strip = strip - exact_dot(done[:, rows], done, 0, 0)
        low = 0 if start < half else half
        held = [strip[:, at : at + half] for at in range(low, low + 3 * half, half)]
        for first in range(0, STRIP, PIVOTS):
            at = start + first - low
            columns = [
                jnp.broadcast_to(held[0][:, at + q : at + q + 1], (STRIP, half)) for q in range(PIVOTS)
            ]
            pivot_rows = [[part[first + q : first + q + 1, :] for part in held] for q in range(PIVOTS)]
            for q in range(PIVOTS):
                j = first + q
                coef = jnp.where(sub > j, columns[q] * (1.0 / columns[q][j : j + 1, :]), 0.0)
                for m in range(q + 1, PIVOTS):
                    columns[m] = columns[m] - coef * columns[m][j : j + 1, :]
                    scale = coef[first + m : first + m + 1, :]
                    pivot_rows[m] = [
                        row - scale * other for row, other in zip(pivot_rows[m], pivot_rows[q])
                    ]
                held = [part - coef * row for part, row in zip(held, pivot_rows[q])]
        diag = jnp.sum(jnp.where(lane == sub + (start - low), held[0], 0.0), axis=1, keepdims=True)
        held = [part / jnp.sqrt(diag) for part in held]
        upper[rows, :] = jnp.concatenate([*held, zero] if low == 0 else [zero, *held], axis=1)
    inverse_ref[...] = upper[:, B:].T


def corner_factor(block, design, filter_matrix, regular):
    return pl.pallas_call(
        corner_kernel,
        out_shape=jax.ShapeDtypeStruct((B, B), jnp.float32),
        scratch_shapes=[pltpu.VMEM((B, 2 * B), jnp.float32)],
        compiler_params=pltpu.CompilerParams(vmem_limit_bytes=8 * 2**20),
        cost_estimate=pl.CostEstimate(flops=0, bytes_accessed=0, transcendentals=0),
        name="corner_factor",
    )(block, design, filter_matrix, regular)


def sides_kernel(
    place_ref,
    joined_ref,
    lead_ref,
    other_ref,
    strip_ref,
    inverse_ref,
    filter_ref,
    regular_ref,
    lead_reg_ref,
    left_ref,
    right_ref,
    gram_cols_ref,
):
    row_index, col_index = place_ref[0], place_ref[1]
    cols = right_ref.shape[1]
    obs = filter_ref.shape[0]
    core = lax.rem(col_index, 2)
    filtered = split_dot(filter_ref[...], joined_ref[:, : 2 * cols])
    here, rows_own = filtered[:, :cols], filtered[:, cols:]
    lead = split_dot(filter_ref[...], lead_ref[...])

    row_pos = lax.broadcasted_iota(jnp.int32, (B, cols), 0)
    col_pos = lax.broadcasted_iota(jnp.int32, (1, cols), 1) + col_index * cols
    strip = strip_ref[...] + split_dot(lead.T, here)
    strip = strip + jnp.where(row_pos == col_pos, regular_ref[...], 0.0)
    high, low = split(-split_dot(inverse_ref[...].T, strip))
    right_ref[:B, :] = high
    right_ref[B : 2 * B, :] = low
    right_ref[2 * B : 3 * B, :] = high
    high, low = split(jnp.where(col_pos < B, 0.0, here))
    right_ref[3 * B : 3 * B + obs, :] = high
    right_ref[3 * B + obs : 3 * B + 2 * obs, :] = low
    right_ref[3 * B + 2 * obs :, :] = high

    @pl.when(col_index == 0)
    def _():
        row_pos = lax.broadcasted_iota(jnp.int32, (B, B), 0)
        identity = jnp.where(row_pos == lax.broadcasted_iota(jnp.int32, (B, B), 1), 1.0, 0.0)
        identity = identity.astype(jnp.bfloat16)
        right_ref[:B, :B] = identity
        right_ref[B : 2 * B, :B] = jnp.zeros((B, B), jnp.bfloat16)
        right_ref[2 * B : 3 * B, :B] = identity

    rows_other = split_dot(filter_ref[...], other_ref[...])
    for half, value in ((core, rows_own), (1 - core, rows_other)):
        value = value.T
        high, low = split(value)
        rows = pl.ds(pl.multiple_of(half * cols, cols), cols)
        left_ref[rows, :obs] = high
        left_ref[rows, obs : 2 * obs] = high
        left_ref[rows, 2 * obs :] = low
        row_pos = lax.broadcasted_iota(jnp.int32, (cols, B), 0) + (2 * row_index + half) * cols
        lead_pos = lax.broadcasted_iota(jnp.int32, (cols, B), 1)
        gram_cols_ref[rows, :] = split_dot(value, lead) + jnp.where(
            row_pos == lead_pos, lead_reg_ref[...], 0.0
        )


def both_sides(place, joined, lead, other, strip, inverse, filter_matrix, regular, lead_reg):
    cols = other.shape[1]
    obs = filter_matrix.shape[0]
    vmem = pl.BlockSpec(memory_space=pltpu.VMEM)
    return pl.pallas_call(
        sides_kernel,
        in_specs=[pl.BlockSpec(memory_space=pltpu.SMEM)] + [vmem] * 8,
        out_specs=[vmem] * 3,
        out_shape=[
            pltpu.HBM((2 * cols, 3 * obs), jnp.bfloat16),
            pltpu.HBM((3 * (obs + B), cols), jnp.bfloat16),
            pltpu.HBM((2 * cols, B), jnp.float32),
        ],
        compiler_params=pltpu.CompilerParams(vmem_limit_bytes=26 * 2**20),
        cost_estimate=pl.CostEstimate(flops=0, bytes_accessed=0, transcendentals=0),
        name="both_sides",
    )(place, joined, lead, other, strip, inverse, filter_matrix, regular, lead_reg)


def block_rows(half):
    return max(size for size in range(128, 513, 128) if half % size == 0)


def tile_kernel(place_ref, normals_ref, strip_ref, gram_ref, left_ref, right_ref, inverse_ref, regular_ref, out_ref):
    step = pl.program_id(0)
    block, cols = out_ref.shape
    high, low = split(split_dot(strip_ref[...] + gram_ref[...], inverse_ref[...]))
    left = jnp.concatenate([high, high, low, left_ref[...]], axis=1)
    first_row = (place_ref[0] * pl.num_programs(0) + step) * block
    first_col = place_ref[1] * cols
    col_pos = lax.broadcasted_iota(jnp.int32, (1, cols), 1) + first_col
    keep = jnp.where(col_pos < B, 0.0, 1.0)
    width = max(size for size in range(128, 513, 128) if cols % size == 0)
    for at in range(0, cols, width):
        here = slice(at, at + width)
        out_ref[:, here] = normals_ref[:, here] * keep[:, here] + jnp.dot(
            left, right_ref[:, here], preferred_element_type=jnp.float32
        )

    @pl.when((first_row < first_col + cols) & (first_col < first_row + block))
    def _():
        row_pos = lax.broadcasted_iota(jnp.int32, (block, cols), 0) + first_row
        on_diag = (row_pos == col_pos) & (col_pos >= B)
        out_ref[...] = out_ref[...] + jnp.where(on_diag, regular_ref[...], 0.0)


def tile_rows(place, normals, strip, gram_cols, left, right, inverse, regular):
    rows, cols = normals.shape
    block = block_rows(rows // 2)

    def whole(array):
        return pl.BlockSpec(array.shape, lambda i, place: (0,) * array.ndim, pipeline_mode=pl.Buffered(1))

    def blocks(width):
        return pl.BlockSpec((block, width), lambda i, place: (i, 0))

    return pl.pallas_call(
        tile_kernel,
        grid_spec=pltpu.PrefetchScalarGridSpec(
            num_scalar_prefetch=1,
            grid=(rows // block,),
            in_specs=[blocks(cols), blocks(B), blocks(B), blocks(left.shape[1])]
            + [whole(array) for array in [right, inverse, regular]],
            out_specs=blocks(cols),
        ),
        out_shape=jax.ShapeDtypeStruct((rows, cols), jnp.float32),
        compiler_params=pltpu.CompilerParams(vmem_limit_bytes=26 * 2**20),
        cost_estimate=pl.CostEstimate(flops=0, bytes_accessed=0, transcendentals=0),
        name="tile_rows",
    )(place, normals, strip, gram_cols, left, right, inverse, regular)


def after(value, earlier):
    return lax.optimization_barrier((value, earlier))[0]


def filter_matrix_of(filter_blocks, count):
    positions = jnp.arange(count, dtype=jnp.int32)
    lag = (positions[:, None] - positions[None, :])[:, None, :, None]
    own = filter_blocks[0][None, :, None, :]
    prior = filter_blocks[1][None, :, None, :]
    blocks = jnp.where(lag == 0, own, jnp.where(lag == 1, prior, 0.0))
    return blocks.reshape(count * P_SIZE, count * P_SIZE)


def row_strip_piece(normals, earlier, meanwhile):
    peers = lax.axis_size("col")
    chips = peers // 2
    size = normals.shape[0] // chips
    col_index = lax.axis_index("col")
    shares = after([normals[z * size : (z + 1) * size, :B] for z in range(1, chips)], earlier)
    arrived = [lax.ppermute(share, "col", [(0, 2 * z)]) for z, share in enumerate(shares, 1)]
    arrived = sum(after(arrived, meanwhile))
    piece = jnp.where(col_index == 0, normals[:size, :B], arrived)
    second = lax.ppermute(piece[size // 2 :], "col", [(c, c + 1) for c in range(0, peers, 2)])
    return jnp.where(col_index % 2 == 0, piece[: size // 2], second)


def doubled(value, bits, reached):
    row_peers, col_peers = lax.axis_size("row"), lax.axis_size("col")
    here = lax.axis_index("row") * col_peers + lax.axis_index("col")
    for bit in bits:
        pairs = [(i, i | bit) for i in reached if i | bit < row_peers * col_peers]
        got = lax.ppermute(value, ("row", "col"), pairs)
        value = jnp.where((here & bit) != 0, got, value)
        reached = reached + [to for _, to in pairs]
    return value, reached


def body(normals, design, filter_blocks, regular):
    rows_here, cols_here = normals.shape
    obs_here = design.shape[0]
    row_peers = lax.axis_size("row")
    row_index = lax.axis_index("row")
    col_index = lax.axis_index("col")
    col_peers = lax.axis_size("col")
    obs = row_peers * obs_here
    core = col_index % 2


    col_strip = lax.psum(jnp.where(row_index == 0, normals[:B], 0.0), "row")

    index_bits = [1 << i for i in range((row_peers * col_peers - 1).bit_length())]
    z_bits = [bit for bit in reversed(index_bits) if 1 < bit < col_peers]
    row_bits = [bit for bit in index_bits if bit >= col_peers]
    leading, reached = doubled(normals[:B, :B], z_bits, [0])
    along_z = leading

    chips = col_peers // 2
    chip = col_index // 2
    along = [design]
    for s in range(1, chips):
        along.append(lax.ppermute(design, "col", [(c, (c + 2 * s) % col_peers) for c in range(col_peers)]))
    along = jnp.stack(along)

    sent = []
    for to in range(row_peers):
        far = lax.dynamic_index_in_dim(along, (chip - to) % chips, 0, keepdims=False)
        sent.append(jnp.concatenate([design, far], axis=1))
    sent = jnp.stack(sent)
    leading, reached = doubled(leading, row_bits, reached)
    lead = lax.dynamic_index_in_dim(along, chip, 0, keepdims=False)[:, :B]
    lead = lax.all_gather(after(lead, sent), "row", axis=0, tiled=True)
    leading = jnp.concatenate([lead, leading], axis=0)

    joined = lax.all_to_all(sent, "row", 0, 0, tiled=True)
    joined = joined.reshape(obs, 2 * cols_here)

    piece = row_strip_piece(normals, along, (along_z, joined, lead))
    strip = lax.all_gather(piece, "col", axis=0, tiled=True)

    leading, _ = doubled(after(leading, col_strip), [1], reached)
    lead, corner = leading[:obs], leading[obs:]
    filters = filter_matrix_of(filter_blocks, obs // P_SIZE)
    lead_reg = regular[:B].reshape(1, B)
    inverse = corner_factor(corner, lead, filters, lead_reg)

    other = lax.ppermute(joined[:, cols_here:], "col", [(c, c ^ 1) for c in range(col_peers)])
    own_reg = lax.dynamic_slice_in_dim(regular, col_index * cols_here, cols_here).reshape(1, cols_here)
    place = jnp.stack([row_index, col_index]).astype(jnp.int32)
    left, right, gram_cols = both_sides(
        place, joined, lead, other, col_strip, inverse, filters, own_reg, lead_reg
    )
    large = [normals, strip, gram_cols, left, right]
    large = [pltpu.with_memory_space_constraint(array, pltpu.HBM) for array in large]
    return tile_rows(place, *large, inverse, own_reg)


def solution(mesh):
    in_specs = (P("row", "col"), P("row", "col"), P(), P())
    out_specs = P("row", "col")
    return jax.shard_map(body, mesh=mesh, in_specs=in_specs, out_specs=out_specs, check_vma=False)
```

```python
import functools

import jax
import jax.numpy as jnp
from jax import lax
from jax.experimental import pallas as pl
from jax.experimental.pallas import tpu as pltpu
from jax.sharding import PartitionSpec as P

B = 256
P_SIZE = 32
STRIP = 32
PIVOTS = 4
HIGHEST = lax.Precision.HIGHEST


def exact_dot(left, right, left_dim, right_dim):
    return lax.dot_general(
        left,
        right,
        (((left_dim,), (right_dim,)), ((), ())),
        precision=HIGHEST,
        preferred_element_type=jnp.float32,
    )


def split(value):
    high = value.astype(jnp.bfloat16)
    low = (value - high.astype(jnp.float32)).astype(jnp.bfloat16)
    return high, low


def split_dot(left, right):
    left_high, left_low = split(left)
    right_high, right_low = split(right)
    wide = functools.partial(jnp.dot, preferred_element_type=jnp.float32)
    return wide(left_high, right_high) + (wide(left_high, right_low) + wide(left_low, right_high))


def corner_kernel(block_ref, design_ref, filter_ref, regular_ref, inverse_ref, upper):
    filtered = exact_dot(filter_ref[...], design_ref[...], 1, 0)
    row_pos = lax.broadcasted_iota(jnp.int32, (B, B), 0)
    col_pos = lax.broadcasted_iota(jnp.int32, (B, B), 1)
    system = block_ref[...] + exact_dot(filtered, filtered, 0, 0)
    system = system + jnp.where(row_pos == col_pos, regular_ref[...], 0.0)
    identity = jnp.where(row_pos == col_pos, 1.0, 0.0)
    half = B // 2
    sub = lax.broadcasted_iota(jnp.int32, (STRIP, half), 0)
    lane = lax.broadcasted_iota(jnp.int32, (STRIP, half), 1)
    zero = jnp.zeros((STRIP, half), jnp.float32)
    for start in range(0, B, STRIP):
        rows = slice(start, start + STRIP)
        strip = jnp.concatenate([system[rows, :], identity[rows, :]], axis=1)
        if start:
            done = upper[:start, :]
            strip = strip - exact_dot(done[:, rows], done, 0, 0)
        low = 0 if start < half else half
        held = [strip[:, at : at + half] for at in range(low, low + 3 * half, half)]
        for first in range(0, STRIP, PIVOTS):
            at = start + first - low
            columns = [
                jnp.broadcast_to(held[0][:, at + q : at + q + 1], (STRIP, half)) for q in range(PIVOTS)
            ]
            pivot_rows = [[part[first + q : first + q + 1, :] for part in held] for q in range(PIVOTS)]
            for q in range(PIVOTS):
                j = first + q
                coef = jnp.where(sub > j, columns[q] * (1.0 / columns[q][j : j + 1, :]), 0.0)
                for m in range(q + 1, PIVOTS):
                    columns[m] = columns[m] - coef * columns[m][j : j + 1, :]
                    scale = coef[first + m : first + m + 1, :]
                    pivot_rows[m] = [
                        row - scale * other for row, other in zip(pivot_rows[m], pivot_rows[q])
                    ]
                held = [part - coef * row for part, row in zip(held, pivot_rows[q])]
        diag = jnp.sum(jnp.where(lane == sub + (start - low), held[0], 0.0), axis=1, keepdims=True)
        held = [part / jnp.sqrt(diag) for part in held]
        upper[rows, :] = jnp.concatenate([*held, zero] if low == 0 else [zero, *held], axis=1)
    inverse_ref[...] = upper[:, B:].T


def corner_factor(block, design, filter_matrix, regular):
    return pl.pallas_call(
        corner_kernel,
        out_shape=jax.ShapeDtypeStruct((B, B), jnp.float32),
        scratch_shapes=[pltpu.VMEM((B, 2 * B), jnp.float32)],
        compiler_params=pltpu.CompilerParams(vmem_limit_bytes=8 * 2**20),
        cost_estimate=pl.CostEstimate(flops=0, bytes_accessed=0, transcendentals=0),
        name="corner_factor",
    )(block, design, filter_matrix, regular)


def columns_kernel(
    place_ref, joined_ref, lead_ref, strip_ref, inverse_ref, filter_ref, regular_ref, right_ref
):
    col_index = place_ref[1]
    cols = right_ref.shape[1]
    obs = filter_ref.shape[0]
    here = split_dot(filter_ref[...], joined_ref[:, :cols])
    lead = split_dot(filter_ref[...], lead_ref[...])
    row_pos = lax.broadcasted_iota(jnp.int32, (B, cols), 0)
    col_pos = lax.broadcasted_iota(jnp.int32, (1, cols), 1) + col_index * cols
    strip = strip_ref[...] + split_dot(lead.T, here)
    strip = strip + jnp.where(row_pos == col_pos, regular_ref[...], 0.0)
    high, low = split(-split_dot(inverse_ref[...].T, strip))
    right_ref[:B, :] = high
    right_ref[B : 2 * B, :] = low
    right_ref[2 * B : 3 * B, :] = high
    high, low = split(jnp.where(col_pos < B, 0.0, here))
    right_ref[3 * B : 3 * B + obs, :] = high
    right_ref[3 * B + obs : 3 * B + 2 * obs, :] = low
    right_ref[3 * B + 2 * obs :, :] = high

    @pl.when(col_index == 0)
    def _():
        row_pos = lax.broadcasted_iota(jnp.int32, (B, B), 0)
        identity = jnp.where(row_pos == lax.broadcasted_iota(jnp.int32, (B, B), 1), 1.0, 0.0)
        identity = identity.astype(jnp.bfloat16)
        right_ref[:B, :B] = identity
        right_ref[B : 2 * B, :B] = jnp.zeros((B, B), jnp.bfloat16)
        right_ref[2 * B : 3 * B, :B] = identity


def column_side(place, joined, lead, strip, inverse, filter_matrix, regular):
    cols = strip.shape[1]
    obs = filter_matrix.shape[0]
    vmem = pl.BlockSpec(memory_space=pltpu.VMEM)
    return pl.pallas_call(
        columns_kernel,
        in_specs=[pl.BlockSpec(memory_space=pltpu.SMEM)] + [vmem] * 6,
        out_specs=vmem,
        out_shape=pltpu.HBM((3 * (obs + B), cols), jnp.bfloat16),
        compiler_params=pltpu.CompilerParams(vmem_limit_bytes=26 * 2**20),
        cost_estimate=pl.CostEstimate(flops=0, bytes_accessed=0, transcendentals=0),
        name="column_side",
    )(place, joined, lead, strip, inverse, filter_matrix, regular)


def rows_kernel(place_ref, joined_ref, lead_ref, other_ref, filter_ref, lead_reg_ref, left_ref, gram_cols_ref):
    row_index, col_index = place_ref[0], place_ref[1]
    cols = other_ref.shape[1]
    obs = filter_ref.shape[0]
    core = lax.rem(col_index, 2)
    lead = split_dot(filter_ref[...], lead_ref[...])
    for half, value in ((core, joined_ref[:, cols:]), (1 - core, other_ref[...])):
        value = split_dot(filter_ref[...], value).T
        high, low = split(value)
        rows = pl.ds(pl.multiple_of(half * cols, cols), cols)
        left_ref[rows, :obs] = high
        left_ref[rows, obs : 2 * obs] = high
        left_ref[rows, 2 * obs :] = low
        row_pos = lax.broadcasted_iota(jnp.int32, (cols, B), 0) + (2 * row_index + half) * cols
        lead_pos = lax.broadcasted_iota(jnp.int32, (cols, B), 1)
        gram_cols_ref[rows, :] = split_dot(value, lead) + jnp.where(
            row_pos == lead_pos, lead_reg_ref[...], 0.0
        )


def row_side(place, joined, lead, other, filter_matrix, lead_reg):
    cols = other.shape[1]
    obs = filter_matrix.shape[0]
    vmem = pl.BlockSpec(memory_space=pltpu.VMEM)
    return pl.pallas_call(
        rows_kernel,
        in_specs=[pl.BlockSpec(memory_space=pltpu.SMEM)] + [vmem] * 5,
        out_specs=[vmem] * 2,
        out_shape=[
            pltpu.HBM((2 * cols, 3 * obs), jnp.bfloat16),
            pltpu.HBM((2 * cols, B), jnp.float32),
        ],
        compiler_params=pltpu.CompilerParams(vmem_limit_bytes=26 * 2**20),
        cost_estimate=pl.CostEstimate(flops=0, bytes_accessed=0, transcendentals=0),
        name="row_side",
    )(place, joined, lead, other, filter_matrix, lead_reg)


def block_rows(half):
    return max(size for size in range(128, 513, 128) if half % size == 0)


def tile_kernel(place_ref, normals_ref, strip_ref, gram_ref, left_ref, right_ref, inverse_ref, regular_ref, out_ref):
    step = pl.program_id(0)
    block, cols = out_ref.shape
    high, low = split(split_dot(strip_ref[...] + gram_ref[...], inverse_ref[...]))
    left = jnp.concatenate([high, high, low, left_ref[...]], axis=1)
    first_row = (place_ref[0] * pl.num_programs(0) + step) * block
    first_col = place_ref[1] * cols
    col_pos = lax.broadcasted_iota(jnp.int32, (1, cols), 1) + first_col
    keep = jnp.where(col_pos < B, 0.0, 1.0)
    width = max(size for size in range(128, 513, 128) if cols % size == 0)
    for at in range(0, cols, width):
        here = slice(at, at + width)
        out_ref[:, here] = normals_ref[:, here] * keep[:, here] + jnp.dot(
            left, right_ref[:, here], preferred_element_type=jnp.float32
        )

    @pl.when((first_row < first_col + cols) & (first_col < first_row + block))
    def _():
        row_pos = lax.broadcasted_iota(jnp.int32, (block, cols), 0) + first_row
        on_diag = (row_pos == col_pos) & (col_pos >= B)
        out_ref[...] = out_ref[...] + jnp.where(on_diag, regular_ref[...], 0.0)


def tile_rows(place, normals, strip, gram_cols, left, right, inverse, regular):
    rows, cols = normals.shape
    block = block_rows(rows // 2)

    def whole(array):
        return pl.BlockSpec(array.shape, lambda i, place: (0,) * array.ndim, pipeline_mode=pl.Buffered(1))

    def blocks(width):
        return pl.BlockSpec((block, width), lambda i, place: (i, 0))

    return pl.pallas_call(
        tile_kernel,
        grid_spec=pltpu.PrefetchScalarGridSpec(
            num_scalar_prefetch=1,
            grid=(rows // block,),
            in_specs=[blocks(cols), blocks(B), blocks(B), blocks(left.shape[1])]
            + [whole(array) for array in [right, inverse, regular]],
            out_specs=blocks(cols),
        ),
        out_shape=jax.ShapeDtypeStruct((rows, cols), jnp.float32),
        compiler_params=pltpu.CompilerParams(vmem_limit_bytes=26 * 2**20),
        cost_estimate=pl.CostEstimate(flops=0, bytes_accessed=0, transcendentals=0),
        name="tile_rows",
    )(place, normals, strip, gram_cols, left, right, inverse, regular)


def after(value, earlier):
    return lax.optimization_barrier((value, earlier))[0]


def filter_matrix_of(filter_blocks, count):
    positions = jnp.arange(count, dtype=jnp.int32)
    lag = (positions[:, None] - positions[None, :])[:, None, :, None]
    own = filter_blocks[0][None, :, None, :]
    prior = filter_blocks[1][None, :, None, :]
    blocks = jnp.where(lag == 0, own, jnp.where(lag == 1, prior, 0.0))
    return blocks.reshape(count * P_SIZE, count * P_SIZE)


def row_strip_piece(normals, earlier, meanwhile):
    peers = lax.axis_size("col")
    chips = peers // 2
    size = normals.shape[0] // chips
    col_index = lax.axis_index("col")
    shares = after([normals[z * size : (z + 1) * size, :B] for z in range(1, chips)], earlier)
    arrived = [lax.ppermute(share, "col", [(0, 2 * z)]) for z, share in enumerate(shares, 1)]
    arrived = sum(after(arrived, meanwhile))
    piece = jnp.where(col_index == 0, normals[:size, :B], arrived)
    second = lax.ppermute(piece[size // 2 :], "col", [(c, c + 1) for c in range(0, peers, 2)])
    return jnp.where(col_index % 2 == 0, piece[: size // 2], second)


def doubled(value, bits, reached):
    row_peers, col_peers = lax.axis_size("row"), lax.axis_size("col")
    here = lax.axis_index("row") * col_peers + lax.axis_index("col")
    for bit in bits:
        pairs = [(i, i | bit) for i in reached if i | bit < row_peers * col_peers]
        got = lax.ppermute(value, ("row", "col"), pairs)
        value = jnp.where((here & bit) != 0, got, value)
        reached = reached + [to for _, to in pairs]
    return value, reached


def body(normals, design, filter_blocks, regular):
    rows_here, cols_here = normals.shape
    obs_here = design.shape[0]
    row_peers = lax.axis_size("row")
    row_index = lax.axis_index("row")
    col_index = lax.axis_index("col")
    col_peers = lax.axis_size("col")
    obs = row_peers * obs_here
    core = col_index % 2


    col_strip = lax.psum(jnp.where(row_index == 0, normals[:B], 0.0), "row")

    index_bits = [1 << i for i in range((row_peers * col_peers - 1).bit_length())]
    z_bits = [bit for bit in reversed(index_bits) if 1 < bit < col_peers]
    row_bits = [bit for bit in index_bits if bit >= col_peers]
    leading, reached = doubled(normals[:B, :B], z_bits, [0])
    along_z = leading

    chips = col_peers // 2
    chip = col_index // 2
    along = [design]
    for s in range(1, chips):
        along.append(lax.ppermute(design, "col", [(c, (c + 2 * s) % col_peers) for c in range(col_peers)]))
    along = jnp.stack(along)

    sent = []
    for to in range(row_peers):
        far = lax.dynamic_index_in_dim(along, (chip - to) % chips, 0, keepdims=False)
        sent.append(jnp.concatenate([design, far], axis=1))
    sent = jnp.stack(sent)
    leading, reached = doubled(leading, row_bits, reached)
    lead = lax.dynamic_index_in_dim(along, chip, 0, keepdims=False)[:, :B]
    lead = lax.all_gather(after(lead, sent), "row", axis=0, tiled=True)
    leading = jnp.concatenate([lead, leading], axis=0)

    joined = lax.all_to_all(sent, "row", 0, 0, tiled=True)
    joined = joined.reshape(obs, 2 * cols_here)

    piece = row_strip_piece(normals, along, (along_z, joined, lead))
    strip = lax.all_gather(piece, "col", axis=0, tiled=True)

    leading, _ = doubled(leading, [1], reached)
    lead, corner = leading[:obs], leading[obs:]
    filters = filter_matrix_of(filter_blocks, obs // P_SIZE)
    lead_reg = regular[:B].reshape(1, B)
    own_reg = lax.dynamic_slice_in_dim(regular, col_index * cols_here, cols_here).reshape(1, cols_here)
    place = jnp.stack([row_index, col_index]).astype(jnp.int32)
    other = lax.ppermute(joined[:, cols_here:], "col", [(c, c ^ 1) for c in range(col_peers)])
    left, gram_cols = row_side(place, joined, lead, other, filters, lead_reg)
    inverse = corner_factor(after(corner, gram_cols), lead, filters, lead_reg)
    right = column_side(place, joined, lead, col_strip, inverse, filters, own_reg)
    large = [normals, strip, gram_cols, left, right]
    large = [pltpu.with_memory_space_constraint(array, pltpu.HBM) for array in large]
    return tile_rows(place, *large, inverse, own_reg)


def solution(mesh):
    in_specs = (P("row", "col"), P("row", "col"), P(), P())
    out_specs = P("row", "col")
    return jax.shard_map(body, mesh=mesh, in_specs=in_specs, out_specs=out_specs, check_vma=False)
```

```python
import functools

import jax
import jax.numpy as jnp
from jax import lax
from jax.experimental import pallas as pl
from jax.experimental.pallas import tpu as pltpu
from jax.sharding import PartitionSpec as P

B = 256
P_SIZE = 32
STRIP = 32
PIVOTS = 8
HIGHEST = lax.Precision.HIGHEST


def exact_dot(left, right, left_dim, right_dim):
    return lax.dot_general(
        left,
        right,
        (((left_dim,), (right_dim,)), ((), ())),
        precision=HIGHEST,
        preferred_element_type=jnp.float32,
    )


def split(value):
    high = value.astype(jnp.bfloat16)
    low = (value - high.astype(jnp.float32)).astype(jnp.bfloat16)
    return high, low


def split_dot(left, right):
    left_high, left_low = split(left)
    right_high, right_low = split(right)
    wide = functools.partial(jnp.dot, preferred_element_type=jnp.float32)
    return wide(left_high, right_high) + (wide(left_high, right_low) + wide(left_low, right_high))


def corner_kernel(block_ref, design_ref, filter_ref, regular_ref, inverse_ref, upper):
    filtered = exact_dot(filter_ref[...], design_ref[...], 1, 0)
    row_pos = lax.broadcasted_iota(jnp.int32, (B, B), 0)
    col_pos = lax.broadcasted_iota(jnp.int32, (B, B), 1)
    system = block_ref[...] + exact_dot(filtered, filtered, 0, 0)
    system = system + jnp.where(row_pos == col_pos, regular_ref[...], 0.0)
    identity = jnp.where(row_pos == col_pos, 1.0, 0.0)
    half = B // 2
    sub = lax.broadcasted_iota(jnp.int32, (STRIP, half), 0)
    lane = lax.broadcasted_iota(jnp.int32, (STRIP, half), 1)
    zero = jnp.zeros((STRIP, half), jnp.float32)
    for start in range(0, B, STRIP):
        rows = slice(start, start + STRIP)
        strip = jnp.concatenate([system[rows, :], identity[rows, :]], axis=1)
        if start:
            done = upper[:start, :]
            strip = strip - exact_dot(done[:, rows], done, 0, 0)
        low = 0 if start < half else half
        held = [strip[:, at : at + half] for at in range(low, low + 3 * half, half)]
        for first in range(0, STRIP, PIVOTS):
            at = start + first - low
            columns = [
                jnp.broadcast_to(held[0][:, at + q : at + q + 1], (STRIP, half)) for q in range(PIVOTS)
            ]
            pivot_rows = [[part[first + q : first + q + 1, :] for part in held] for q in range(PIVOTS)]
            for q in range(PIVOTS):
                j = first + q
                coef = jnp.where(sub > j, columns[q] * (1.0 / columns[q][j : j + 1, :]), 0.0)
                for m in range(q + 1, PIVOTS):
                    columns[m] = columns[m] - coef * columns[m][j : j + 1, :]
                    scale = coef[first + m : first + m + 1, :]
                    pivot_rows[m] = [
                        row - scale * other for row, other in zip(pivot_rows[m], pivot_rows[q])
                    ]
                held = [part - coef * row for part, row in zip(held, pivot_rows[q])]
        diag = jnp.sum(jnp.where(lane == sub + (start - low), held[0], 0.0), axis=1, keepdims=True)
        held = [part / jnp.sqrt(diag) for part in held]
        upper[rows, :] = jnp.concatenate([*held, zero] if low == 0 else [zero, *held], axis=1)
    inverse_ref[...] = upper[:, B:].T


def corner_factor(block, design, filter_matrix, regular):
    return pl.pallas_call(
        corner_kernel,
        out_shape=jax.ShapeDtypeStruct((B, B), jnp.float32),
        scratch_shapes=[pltpu.VMEM((B, 2 * B), jnp.float32)],
        compiler_params=pltpu.CompilerParams(vmem_limit_bytes=8 * 2**20),
        cost_estimate=pl.CostEstimate(flops=0, bytes_accessed=0, transcendentals=0),
        name="corner_factor",
    )(block, design, filter_matrix, regular)


def columns_kernel(
    place_ref, joined_ref, lead_ref, strip_ref, inverse_ref, filter_ref, regular_ref, right_ref
):
    col_index = place_ref[1]
    cols = right_ref.shape[1]
    obs = filter_ref.shape[0]
    here = split_dot(filter_ref[...], joined_ref[:, :cols])
    lead = split_dot(filter_ref[...], lead_ref[...])
    row_pos = lax.broadcasted_iota(jnp.int32, (B, cols), 0)
    col_pos = lax.broadcasted_iota(jnp.int32, (1, cols), 1) + col_index * cols
    strip = strip_ref[...] + split_dot(lead.T, here)
    strip = strip + jnp.where(row_pos == col_pos, regular_ref[...], 0.0)
    high, low = split(-split_dot(inverse_ref[...].T, strip))
    right_ref[:B, :] = high
    right_ref[B : 2 * B, :] = low
    right_ref[2 * B : 3 * B, :] = high
    high, low = split(jnp.where(col_pos < B, 0.0, here))
    right_ref[3 * B : 3 * B + obs, :] = high
    right_ref[3 * B + obs : 3 * B + 2 * obs, :] = low
    right_ref[3 * B + 2 * obs :, :] = high

    @pl.when(col_index == 0)
    def _():
        row_pos = lax.broadcasted_iota(jnp.int32, (B, B), 0)
        identity = jnp.where(row_pos == lax.broadcasted_iota(jnp.int32, (B, B), 1), 1.0, 0.0)
        identity = identity.astype(jnp.bfloat16)
        right_ref[:B, :B] = identity
        right_ref[B : 2 * B, :B] = jnp.zeros((B, B), jnp.bfloat16)
        right_ref[2 * B : 3 * B, :B] = identity


def column_side(place, joined, lead, strip, inverse, filter_matrix, regular):
    cols = strip.shape[1]
    obs = filter_matrix.shape[0]
    vmem = pl.BlockSpec(memory_space=pltpu.VMEM)
    return pl.pallas_call(
        columns_kernel,
        in_specs=[pl.BlockSpec(memory_space=pltpu.SMEM)] + [vmem] * 6,
        out_specs=vmem,
        out_shape=pltpu.HBM((3 * (obs + B), cols), jnp.bfloat16),
        compiler_params=pltpu.CompilerParams(vmem_limit_bytes=26 * 2**20),
        cost_estimate=pl.CostEstimate(flops=0, bytes_accessed=0, transcendentals=0),
        name="column_side",
    )(place, joined, lead, strip, inverse, filter_matrix, regular)


def rows_kernel(place_ref, joined_ref, lead_ref, other_ref, filter_ref, lead_reg_ref, left_ref, gram_cols_ref):
    row_index, col_index = place_ref[0], place_ref[1]
    cols = other_ref.shape[1]
    obs = filter_ref.shape[0]
    core = lax.rem(col_index, 2)
    lead = split_dot(filter_ref[...], lead_ref[...])
    for half, value in ((core, joined_ref[:, cols:]), (1 - core, other_ref[...])):
        value = split_dot(filter_ref[...], value).T
        high, low = split(value)
        rows = pl.ds(pl.multiple_of(half * cols, cols), cols)
        left_ref[rows, :obs] = high
        left_ref[rows, obs : 2 * obs] = high
        left_ref[rows, 2 * obs :] = low
        row_pos = lax.broadcasted_iota(jnp.int32, (cols, B), 0) + (2 * row_index + half) * cols
        lead_pos = lax.broadcasted_iota(jnp.int32, (cols, B), 1)
        gram_cols_ref[rows, :] = split_dot(value, lead) + jnp.where(
            row_pos == lead_pos, lead_reg_ref[...], 0.0
        )


def row_side(place, joined, lead, other, filter_matrix, lead_reg):
    cols = other.shape[1]
    obs = filter_matrix.shape[0]
    vmem = pl.BlockSpec(memory_space=pltpu.VMEM)
    return pl.pallas_call(
        rows_kernel,
        in_specs=[pl.BlockSpec(memory_space=pltpu.SMEM)] + [vmem] * 5,
        out_specs=[vmem] * 2,
        out_shape=[
            pltpu.HBM((2 * cols, 3 * obs), jnp.bfloat16),
            pltpu.HBM((2 * cols, B), jnp.float32),
        ],
        compiler_params=pltpu.CompilerParams(vmem_limit_bytes=26 * 2**20),
        cost_estimate=pl.CostEstimate(flops=0, bytes_accessed=0, transcendentals=0),
        name="row_side",
    )(place, joined, lead, other, filter_matrix, lead_reg)


def block_rows(half):
    return max(size for size in range(128, 513, 128) if half % size == 0)


def tile_kernel(place_ref, normals_ref, strip_ref, gram_ref, left_ref, right_ref, inverse_ref, regular_ref, out_ref):
    step = pl.program_id(0)
    block, cols = out_ref.shape
    high, low = split(split_dot(strip_ref[...] + gram_ref[...], inverse_ref[...]))
    left = jnp.concatenate([high, high, low, left_ref[...]], axis=1)
    first_row = (place_ref[0] * pl.num_programs(0) + step) * block
    first_col = place_ref[1] * cols
    col_pos = lax.broadcasted_iota(jnp.int32, (1, cols), 1) + first_col
    keep = jnp.where(col_pos < B, 0.0, 1.0)
    width = max(size for size in range(128, 513, 128) if cols % size == 0)
    for at in range(0, cols, width):
        here = slice(at, at + width)
        out_ref[:, here] = normals_ref[:, here] * keep[:, here] + jnp.dot(
            left, right_ref[:, here], preferred_element_type=jnp.float32
        )

    @pl.when((first_row < first_col + cols) & (first_col < first_row + block))
    def _():
        row_pos = lax.broadcasted_iota(jnp.int32, (block, cols), 0) + first_row
        on_diag = (row_pos == col_pos) & (col_pos >= B)
        out_ref[...] = out_ref[...] + jnp.where(on_diag, regular_ref[...], 0.0)


def tile_rows(place, normals, strip, gram_cols, left, right, inverse, regular):
    rows, cols = normals.shape
    block = block_rows(rows // 2)

    def whole(array):
        return pl.BlockSpec(array.shape, lambda i, place: (0,) * array.ndim, pipeline_mode=pl.Buffered(1))

    def blocks(width):
        return pl.BlockSpec((block, width), lambda i, place: (i, 0))

    return pl.pallas_call(
        tile_kernel,
        grid_spec=pltpu.PrefetchScalarGridSpec(
            num_scalar_prefetch=1,
            grid=(rows // block,),
            in_specs=[blocks(cols), blocks(B), blocks(B), blocks(left.shape[1])]
            + [whole(array) for array in [right, inverse, regular]],
            out_specs=blocks(cols),
        ),
        out_shape=jax.ShapeDtypeStruct((rows, cols), jnp.float32),
        compiler_params=pltpu.CompilerParams(vmem_limit_bytes=26 * 2**20),
        cost_estimate=pl.CostEstimate(flops=0, bytes_accessed=0, transcendentals=0),
        name="tile_rows",
    )(place, normals, strip, gram_cols, left, right, inverse, regular)


def after(value, earlier):
    return lax.optimization_barrier((value, earlier))[0]


def filter_matrix_of(filter_blocks, count):
    positions = jnp.arange(count, dtype=jnp.int32)
    lag = (positions[:, None] - positions[None, :])[:, None, :, None]
    own = filter_blocks[0][None, :, None, :]
    prior = filter_blocks[1][None, :, None, :]
    blocks = jnp.where(lag == 0, own, jnp.where(lag == 1, prior, 0.0))
    return blocks.reshape(count * P_SIZE, count * P_SIZE)


def row_strip_piece(normals, earlier, meanwhile):
    peers = lax.axis_size("col")
    chips = peers // 2
    size = normals.shape[0] // chips
    col_index = lax.axis_index("col")
    shares = after([normals[z * size : (z + 1) * size, :B] for z in range(1, chips)], earlier)
    arrived = [lax.ppermute(share, "col", [(0, 2 * z)]) for z, share in enumerate(shares, 1)]
    arrived = sum(after(arrived, meanwhile))
    piece = jnp.where(col_index == 0, normals[:size, :B], arrived)
    second = lax.ppermute(piece[size // 2 :], "col", [(c, c + 1) for c in range(0, peers, 2)])
    return jnp.where(col_index % 2 == 0, piece[: size // 2], second)


def doubled(value, bits, reached):
    row_peers, col_peers = lax.axis_size("row"), lax.axis_size("col")
    here = lax.axis_index("row") * col_peers + lax.axis_index("col")
    for bit in bits:
        pairs = [(i, i | bit) for i in reached if i | bit < row_peers * col_peers]
        got = lax.ppermute(value, ("row", "col"), pairs)
        value = jnp.where((here & bit) != 0, got, value)
        reached = reached + [to for _, to in pairs]
    return value, reached


def body(normals, design, filter_blocks, regular):
    rows_here, cols_here = normals.shape
    obs_here = design.shape[0]
    row_peers = lax.axis_size("row")
    row_index = lax.axis_index("row")
    col_index = lax.axis_index("col")
    col_peers = lax.axis_size("col")
    obs = row_peers * obs_here
    core = col_index % 2


    col_strip = lax.psum(jnp.where(row_index == 0, normals[:B], 0.0), "row")

    index_bits = [1 << i for i in range((row_peers * col_peers - 1).bit_length())]
    z_bits = [bit for bit in reversed(index_bits) if 1 < bit < col_peers]
    row_bits = [bit for bit in index_bits if bit >= col_peers]
    leading, reached = doubled(normals[:B, :B], z_bits, [0])
    along_z = leading

    chips = col_peers // 2
    chip = col_index // 2
    along = [design]
    for s in range(1, chips):
        along.append(lax.ppermute(design, "col", [(c, (c + 2 * s) % col_peers) for c in range(col_peers)]))
    along = jnp.stack(along)

    sent = []
    for to in range(row_peers):
        far = lax.dynamic_index_in_dim(along, (chip - to) % chips, 0, keepdims=False)
        sent.append(jnp.concatenate([design, far], axis=1))
    sent = after(jnp.stack(sent), along_z)
    leading, reached = doubled(leading, row_bits, reached)
    lead = lax.dynamic_index_in_dim(along, chip, 0, keepdims=False)[:, :B]
    lead = lax.all_gather(after(lead, sent), "row", axis=0, tiled=True)
    leading = jnp.concatenate([lead, leading], axis=0)

    joined = lax.all_to_all(sent, "row", 0, 0, tiled=True)
    joined = joined.reshape(obs, 2 * cols_here)

    piece = row_strip_piece(normals, along, (along_z, joined, lead))
    strip = lax.all_gather(piece, "col", axis=0, tiled=True)

    leading, _ = doubled(leading, [1], reached)
    lead, corner = leading[:obs], leading[obs:]
    filters = filter_matrix_of(filter_blocks, obs // P_SIZE)
    lead_reg = regular[:B].reshape(1, B)
    own_reg = lax.dynamic_slice_in_dim(regular, col_index * cols_here, cols_here).reshape(1, cols_here)
    place = jnp.stack([row_index, col_index]).astype(jnp.int32)
    other = lax.ppermute(joined[:, cols_here:], "col", [(c, c ^ 1) for c in range(col_peers)])
    left, gram_cols = row_side(place, joined, lead, other, filters, lead_reg)
    inverse = corner_factor(after(corner, gram_cols), lead, filters, lead_reg)
    right = column_side(place, joined, lead, col_strip, inverse, filters, own_reg)
    large = [normals, strip, gram_cols, left, right]
    large = [pltpu.with_memory_space_constraint(array, pltpu.HBM) for array in large]
    return tile_rows(place, *large, inverse, own_reg)


def solution(mesh):
    in_specs = (P("row", "col"), P("row", "col"), P(), P())
    out_specs = P("row", "col")
    return jax.shard_map(body, mesh=mesh, in_specs=in_specs, out_specs=out_specs, check_vma=False)
```
